256 devices in a mesh: section: 8 (over x, y_lo), dp: 32 (over z, y_hi, core).
Axes of the slice: x: 4, y: 4 (y_hi: 2, y_lo: 2; y = y_hi * 2 + y_lo), z: 8, core: 2. Of those that a mesh axis runs over, the one named last changes fastest.
Arguments:
- params: bfloat16 [8, 2560, 2048], P('section', 'dp'), may hold values from -2 to 2
- moment_one: float32 [8, 2560, 2048], P('section', 'dp'), may hold values from -3 to 3
- moment_two: float32 [8, 2560, 2048], P('section', 'dp'), may hold values from 0.05 to 1
- sent_rows: bfloat16 [8, 32, 4, 192, 2048], P('section', 'dp'), may hold values from -6 to 6
- back_rows: bfloat16 [8, 32, 4, 192, 2048], P('section', 'dp'), may hold values from -6 to 6
- slot_ids: int32 [8, 32, 2], P('section', 'dp'), may hold values from 0 to 3, all different within a row
Outputs:
- new_params: bfloat16 [8, 2560, 2048], P('section', 'dp')
- new_moment_one: float32 [8, 2560, 2048], P('section', 'dp')
- new_moment_two: float32 [8, 2560, 2048], P('section', 'dp')
The draws below stay inside these ranges and needn't reach their ends.
Inputs may be any that keep to these rules, and one draw needn't show every extreme that they name: Each row of slot_ids names 2 different slots.
All inputs are finite; a program needn't handle non-finite values.
Results may differ from the reference program's by a relative error of at most 0.017.
Values may be sent and summed in bfloat16 or wider, within the bound.
A program may use at most 128 MiB of HBM per device.

```python
import math
import jax
import jax.numpy as jnp
from jax import lax

MODEL_WIDTH = 2048
HEAD_SIZE = 64
QUERY_HEADS = 16
KEY_VALUE_HEADS = 4
SEQ = 192
LOG = 4
MB = 2
STEP = 100
PROWS = 2560
N_SECTION = 8
N_DP = 32


def draw_params(key, part):
    key = jax.random.fold_in(key, 11)
    rotary_base = jax.random.normal(key, (N_SECTION, PROWS, MODEL_WIDTH), jnp.float32) * MODEL_WIDTH ** (-0.5)
    rotary_base = jnp.clip(rotary_base, -2.0, 2.0)
    return rotary_base.astype(jnp.bfloat16)


def block_scale(rng, dims, cuts, smallest, high):
    gain, own = 1.0, jax.random.fold_in(rng, 6)
    for dim, blocks in cuts:
        steps = jnp.exp(jax.random.uniform(jax.random.fold_in(own, dim), (blocks,), jnp.float32, smallest / len(cuts), high / len(cuts)))
        gain = gain * jnp.repeat(steps, dims[dim] // blocks).reshape([-1 if axis == dim else 1 for axis in range(len(dims))])
    return gain


def picks_of(stream_key, rows, amount, top, lift):
    order = jax.random.permutation(jax.random.fold_in(stream_key, 1), amount)
    pull = order
    for power in range(3):
        pull = pull * pull // amount
    pull = pull * lift // amount
    lots = jax.random.randint(jax.random.fold_in(stream_key, 2), (rows, amount), 0, 4096) + pull
    fixed_rows = jax.random.permutation(jax.random.fold_in(stream_key, 3), rows)[jnp.arange(amount) % rows]
    lots = jnp.where(jnp.arange(rows)[:, None] == fixed_rows[None, :], 1 << 14, lots)
    merit = lots * amount + jnp.arange(amount)
    return lax.top_k(merit.astype(jnp.int32), top)[1].astype(jnp.int32)


def centred(stream_key, shape, spread, bound, shards=(), held_as=jnp.bfloat16):
    level = block_scale(stream_key, shape, shards, -0.22, 0.18) if shards else 1.0
    values = jax.random.normal(stream_key, shape, jnp.float32) * spread * level
    return jnp.minimum(jnp.maximum(values, -bound), bound).astype(held_as)


def setup_inputs(seed: int = 0) -> dict:
    keys = jax.random.split(jax.random.key(seed), 7)
    params = draw_params(jax.random.fold_in(keys[6], 71), 0)
    moment_one = centred(keys[1], (N_SECTION, PROWS, MODEL_WIDTH), 0.5, 3.0, ((0, 8), (1, 32)), jnp.float32)
    moment_two = jnp.clip(jnp.exp(math.log(1.0) - 2.9957323 * jax.random.uniform(keys[2], (N_SECTION, PROWS, MODEL_WIDTH), jnp.float32) ** block_scale(keys[2], (N_SECTION, PROWS, MODEL_WIDTH), ((0, 8), (1, 32)), -0.2, 0.2)), 0.05, 1.0)
    sent_rows = centred(keys[3], (N_SECTION, N_DP, LOG, SEQ, MODEL_WIDTH), 1.0, 6.0, ((0, 8), (1, 32)))
    back_rows = centred(keys[4], (N_SECTION, N_DP, LOG, SEQ, MODEL_WIDTH), 1.0, 6.0, ((0, 8), (1, 32)))
    slot_ids = picks_of(keys[5], N_SECTION * N_DP, LOG, MB, 0).reshape((N_SECTION, N_DP, MB))
    return dict(params=params, moment_one=moment_one, moment_two=moment_two, sent_rows=sent_rows, back_rows=back_rows, slot_ids=slot_ids)


rope_base = 500000.0
learn_rate = 0.0003
decay_rate = 0.1

def rotary(values, cosine, sine):
    midway = values.shape[-1] // 2
    leading = values[..., :midway]
    trailing = values[..., midway:]
    return jnp.concatenate([leading * cosine - trailing * sine, trailing * cosine + leading * sine], axis=-1)

def attention_branch(weights, logged):
    batch_list, sequence_length, width = logged.shape
    tokens = batch_list * sequence_length
    query_total_width = QUERY_HEADS * HEAD_SIZE
    key_value_width = KEY_VALUE_HEADS * HEAD_SIZE
    head_groups = QUERY_HEADS // KEY_VALUE_HEADS
    flat = logged.reshape(tokens, width).astype(jnp.float32)
    scaling = lax.rsqrt(lax.optimization_barrier(jnp.mean(flat * flat, axis=-1, keepdims=True)) + 1e-05)
    normed = (flat * scaling).astype(jnp.bfloat16)
    projected_rows = lax.dot_general(normed, weights[:query_total_width + 2 * key_value_width], (((1,), (1,)), ((), ())), preferred_element_type=jnp.float32)
    query_rows = projected_rows[:, :query_total_width].reshape(batch_list, sequence_length, KEY_VALUE_HEADS, head_groups, HEAD_SIZE)
    key_portion = projected_rows[:, query_total_width:query_total_width + key_value_width].reshape(batch_list, sequence_length, KEY_VALUE_HEADS, HEAD_SIZE)
    value_portion = projected_rows[:, query_total_width + key_value_width:].reshape(batch_list, sequence_length, KEY_VALUE_HEADS, HEAD_SIZE)
    frequency = rope_base ** (-jnp.arange(HEAD_SIZE // 2, dtype=jnp.float32) * 2.0 / HEAD_SIZE)
    angles = jnp.arange(sequence_length, dtype=jnp.float32)[:, None] * frequency[None, :]
    cosine = jnp.cos(angles)
    sine = jnp.sin(angles)
    query_rows = rotary(query_rows, cosine[None, :, None, None, :], sine[None, :, None, None, :])
    key_portion = rotary(key_portion, cosine[None, :, None, :], sine[None, :, None, :])
    scores = jnp.einsum('bqhgd,bkhd->bhgqk', query_rows, key_portion) * HEAD_SIZE ** (-0.5)
    causal = jnp.arange(sequence_length)[:, None] >= jnp.arange(sequence_length)[None, :]
    scores = jnp.where(causal, scores, -1e+30)
    highest = lax.stop_gradient(lax.optimization_barrier(jnp.max(scores, axis=-1, keepdims=True)))
    raised = jnp.exp(scores - highest)
    probs = raised / lax.optimization_barrier(jnp.sum(raised, axis=-1, keepdims=True))
    context = jnp.einsum('bhgqk,bkhd->bqhgd', probs, value_portion).reshape(tokens, query_total_width).astype(jnp.bfloat16)
    return jnp.dot(context, weights[query_total_width + 2 * key_value_width:], preferred_element_type=jnp.float32)

def replay_gradient(weights, logged, upstream):
    batch_list, sequence_length, width = logged.shape
    outcome, pullback = jax.vjp(lambda current: attention_branch(current, logged), weights)
    return pullback(upstream.reshape(batch_list * sequence_length, width).astype(jnp.float32))[0]

def apply_adam(weights, first_moment, second_moment, gradient):
    first_new = 0.9 * first_moment + 0.1 * gradient
    second_new = 0.999 * second_moment + 0.001 * gradient * gradient
    fix_first = 1.0 - 0.9 ** STEP
    fix_second = 1.0 - 0.999 ** STEP
    update = first_new / fix_first / (jnp.sqrt(second_new / fix_second) + 1e-08)
    current = weights.astype(jnp.float32)
    renewed = (current - learn_rate * (update + decay_rate * current)).astype(jnp.bfloat16)
    return (renewed, first_new, second_new)

def reference(params, moment_one, moment_two, sent_rows, back_rows, slot_ids):

    def one_section(position):
        weights = params[position]
        before = (position + N_SECTION - 1) % N_SECTION
        after = (position + 1) % N_SECTION

        def one_replica(running, replica):
            wanted = slot_ids[position, replica]
            logged = jnp.take(sent_rows[before, replica], wanted, axis=0)
            upstream = jnp.take(back_rows[after, replica], wanted, axis=0)
            local_grad = replay_gradient(weights, logged, upstream)
            return (running + local_grad.astype(jnp.float32), None)
        summed, unused = lax.scan(one_replica, jnp.zeros((PROWS, MODEL_WIDTH), jnp.float32), jnp.arange(N_DP, dtype=jnp.int32))
        return apply_adam(weights, moment_one[position], moment_two[position], summed / N_DP)
    new_params, new_one, new_two = lax.map(one_section, jnp.arange(N_SECTION, dtype=jnp.int32))
    return (new_params, new_one, new_two)
```

```python
import functools

import jax
import jax.numpy as jnp
import numpy as np
from jax import lax
from jax.experimental import pallas as pl
from jax.experimental.pallas import tpu as pltpu
from jax.sharding import PartitionSpec as P

HEAD_SIZE = 64
QUERY_HEADS = 16
KEY_VALUE_HEADS = 4
STEP = 100
SEQ = 192
LOG = 4
MB = 2
PROWS = 2560

N_SECTION = 8
N_DP = 32
N_Z = 8
CHUNK = 64
PER_Z = 5
LOCAL = 20
SHARD = 80
PIECE = 16
PIECES = SHARD // PIECE
Q_ROWS = 512
K_AT = 512
V_AT = 640
O_AT = 768
QKV_BLOCKS = 12

rope_base = 500000.0
learn_rate = 0.0003
decay_rate = 0.1

MESH = pl.DeviceIdType.MESH
BF16 = jnp.bfloat16
F32 = jnp.float32


def nn(a, b):
    return lax.dot_general(a, b, (((1,), (0,)), ((), ())), preferred_element_type=F32)


def nt(a, b):
    return lax.dot_general(a, b, (((1,), (1,)), ((), ())), preferred_element_type=F32)


def core_of(block):
    return jnp.where(
        block < 16,
        lax.div(block, 8),
        jnp.where(block < 24, lax.rem(lax.div(block - 16, 2), 2), lax.div(block - 24, 8)),
    )


def place_of(block):
    return jnp.where(
        block < 16,
        lax.rem(block, 8),
        jnp.where(
            block < 24,
            8 + 2 * lax.div(block - 16, 4) + lax.rem(block - 16, 2),
            12 + lax.rem(block - 24, 8),
        ),
    )


def kernel(
    params_hbm,
    sent_hbm,
    back_hbm,
    ids_ref,
    cos_ref,
    sin_ref,
    grad_ref,
    shard,
    sent,
    back,
    ids_next,
    ids_prev,
    ids_one,
    ids_two,
    weights,
    acts,
    picked,
    proj,
    dctx,
    lhs,
    total,
    stage,
    from_low,
    from_high,
    final,
    sem_local,
    sem_ids,
    sem_ids_send,
    sem_ids_recv,
    first_send,
    gather_up,
    gather_down,
    gather_recv,
    norm_send,
    norm_recv,
    pick_send,
    pick_recv,
    pass_send,
    pass_recv,
    sum_send,
    low_recv,
    high_recv,
    final_send,
    final_recv,
):
    section = lax.axis_index("section")
    dp = lax.axis_index("dp")
    z = lax.div(dp, 4)
    core = lax.rem(dp, 2)
    other = 1 - core
    owner_y = lax.rem(lax.div(dp, 2), 2)
    sibling = dp + 1 - 2 * core
    up = lax.rem(dp + 4, N_DP)
    down = lax.rem(dp + N_DP - 4, N_DP)
    before = lax.rem(section + N_SECTION - 1, N_SECTION)
    after = lax.rem(section + 1, N_SECTION)
    before_two = lax.rem(section + N_SECTION - 2, N_SECTION)
    after_two = lax.rem(section + 2, N_SECTION)
    width = weights.shape[2]

    loads = [
        pltpu.make_async_copy(params_hbm, shard, sem_local.at[0]),
        pltpu.make_async_copy(sent_hbm, sent, sem_local.at[1]),
        pltpu.make_async_copy(back_hbm, back, sem_local.at[2]),
    ]
    for load in loads:
        load.start()

    barrier = pltpu.get_barrier_semaphore()
    peers = [(section, sibling), (section, up), (section, down), (before_two, dp), (after_two, dp)]
    for quarter in range(4):
        peers.append((before, 4 * z + quarter))
        peers.append((after, 4 * z + quarter))
    for peer in peers:
        pl.semaphore_signal(barrier, inc=1, device_id=peer, device_id_type=MESH)
    pl.semaphore_wait(barrier, len(peers))

    id_copies = [
        pltpu.make_async_remote_copy(
            src_ref=ids_ref,
            dst_ref=ids_next,
            send_sem=sem_ids_send.at[0],
            recv_sem=sem_ids_recv.at[0],
            device_id=(before, dp),
            device_id_type=MESH,
        ),
        pltpu.make_async_remote_copy(
            src_ref=ids_ref,
            dst_ref=ids_prev,
            send_sem=sem_ids_send.at[1],
            recv_sem=sem_ids_recv.at[1],
            device_id=(after, dp),
            device_id_type=MESH,
        ),
    ]
    for copy in id_copies:
        copy.start()

    loads[0].wait()

    def first_copy(piece, half):
        row = SHARD * dp + PIECE * piece
        block = lax.div(row, CHUNK)
        return pltpu.make_async_remote_copy(
            src_ref=shard.at[pl.ds(PIECE * piece, PIECE)],
            dst_ref=weights.at[place_of(block), pl.ds(pl.multiple_of(lax.rem(row, CHUNK), PIECE), PIECE)],
            send_sem=first_send.at[2 * piece + half],
            recv_sem=gather_recv.at[place_of(block)],
            device_id=(before, 4 * z + 2 * half + core_of(block)),
            device_id_type=MESH,
        )

    for piece in range(PIECES):
        for half in range(2):
            first_copy(piece, half).start()

    pick_copies = []
    norm_copies = []
    id_copies[0].wait_recv()
    to_one = pltpu.make_async_copy(ids_next, ids_one, sem_ids.at[0])
    to_one.start()
    to_one.wait()
    id_copies[1].wait_recv()
    to_two = pltpu.make_async_copy(ids_prev, ids_two, sem_ids.at[1])
    to_two.start()
    to_two.wait()

    loads[2].wait()
    for m in range(MB):
        wanted = ids_two[m, 0]

        def pick_rows(n, carry, m=m, wanted=wanted):
            rows = pl.ds(pl.multiple_of(n * 16, 16), 16)
            picked[m, rows, :] = back[wanted, rows, :]
            return carry

        lax.fori_loop(0, SEQ // 16, pick_rows, 0)
        pick_copies.append(
            pltpu.make_async_remote_copy(
                src_ref=picked.at[m],
                dst_ref=acts.at[1, 2 * core + m],
                send_sem=pick_send.at[m],
                recv_sem=pick_recv.at[m],
                device_id=(before_two, dp),
                device_id_type=MESH,
            )
        )
        pick_copies[m].start()

    loads[1].wait()
    for m in range(MB):
        wanted = ids_one[m, 0]

        def norm_rows(n, carry, m=m, wanted=wanted):
            rows = pl.ds(pl.multiple_of(n * 16, 16), 16)
            value = sent[wanted, rows, :].astype(F32)
            scaling = lax.rsqrt(jnp.mean(value * value, axis=-1, keepdims=True) + 1e-05)
            acts[0, 2 * core + m, rows, :] = (value * scaling).astype(BF16)
            return carry

        lax.fori_loop(0, SEQ // 16, norm_rows, 0)
        norm_copies.append(
            pltpu.make_async_remote_copy(
                src_ref=acts.at[0, 2 * core + m],
                dst_ref=acts.at[0, 2 * core + m],
                send_sem=norm_send.at[m],
                recv_sem=norm_recv.at[m],
                device_id=(section, sibling),
                device_id_type=MESH,
            )
        )
        norm_copies[m].start()

    def gather_copy(place, going_up):
        return pltpu.make_async_remote_copy(
            src_ref=weights.at[place],
            dst_ref=weights.at[place],
            send_sem=(gather_up if going_up else gather_down).at[place],
            recv_sem=gather_recv.at[place],
            device_id=(section, up if going_up else down),
            device_id_type=MESH,
        )

    def gather_step(n):
        m = n - PER_Z
        middle = jnp.logical_and(n >= PER_Z, n < 35)
        away = jnp.where(n < PER_Z, 0, jnp.where(middle, 1 + lax.div(m, 10), 4))
        which = jnp.where(n < PER_Z, n, jnp.where(middle, lax.div(lax.rem(m, 10), 2), n - 35))
        rising = jnp.logical_and(middle, lax.rem(m, 2) == 0)
        home = lax.rem(jnp.where(rising, z - away, z + away) + N_Z, N_Z)
        block = PER_Z * home + which
        odd = lax.rem(block, 2)
        mine = core_of(block) == core
        start = n < PER_Z
        falling = jnp.logical_and(middle, jnp.logical_not(rising))
        send_up = jnp.logical_or(start, jnp.logical_and(rising, away < 4 - odd))
        send_down = jnp.logical_or(start, jnp.logical_and(falling, away < 3 + odd))
        return place_of(block), mine, jnp.logical_and(mine, send_up), jnp.logical_and(mine, send_down)

    def gather(n, carry):
        place, mine, send_up, send_down = gather_step(n)

        @pl.when(mine)
        def _():
            gather_copy(place, True).wait_recv()

        @pl.when(send_up)
        def _():
            gather_copy(place, True).start()

        @pl.when(send_down)
        def _():
            gather_copy(place, False).start()

        return carry

    lax.fori_loop(0, 40, gather, 0)

    pass_copies = []
    for m in range(MB):
        pick_copies[m].wait_recv()
        pass_copies.append(
            pltpu.make_async_remote_copy(
                src_ref=acts.at[1, 2 * core + m],
                dst_ref=acts.at[1, 2 * core + m],
                send_sem=pass_send.at[m],
                recv_sem=pass_recv.at[m],
                device_id=(section, sibling),
                device_id_type=MESH,
            )
        )
        pass_copies[m].start()
    for m in range(MB):
        norm_copies[m].wait_recv()

    def project(n, carry):
        batch, part = lax.div(n, 3), lax.rem(n, 3)
        rows = weights[pl.ds(4 * part, 4)].reshape(4 * CHUNK, width)
        proj[batch, pl.ds(pl.multiple_of(part * 256, 256), 256), :] = nt(rows, acts[0, batch])
        return carry

    lax.fori_loop(0, 12, project, 0)

    for m in range(MB):
        pass_copies[m].wait_recv()

    def cotangent(n, carry):
        batch, part = lax.div(n, 2), lax.rem(n, 2)
        rows = weights[pl.ds(QKV_BLOCKS + 4 * part, 4)].reshape(4 * CHUNK, width)
        dctx[batch, pl.ds(pl.multiple_of(part * 256, 256), 256), :] = nt(rows, acts[1, batch]).astype(BF16)
        return carry

    lax.fori_loop(0, 8, cotangent, 0)

    cosine, sine = cos_ref[...], sin_ref[...]
    half = HEAD_SIZE // 2

    def rotate(value):
        a, b = value[:half], value[half:]
        return jnp.concatenate([a * cosine - b * sine, b * cosine + a * sine], axis=0)

    def rotate_back(value):
        a, b = value[:half], value[half:]
        return jnp.concatenate([a * cosine + b * sine, b * cosine - a * sine], axis=0)

    def attention(n, carry):
        batch, group = lax.div(n, 2), lax.rem(n, 2)
        key_rows = pl.ds(pl.multiple_of(K_AT + HEAD_SIZE * group, HEAD_SIZE), HEAD_SIZE)
        value_rows = pl.ds(pl.multiple_of(V_AT + HEAD_SIZE * group, HEAD_SIZE), HEAD_SIZE)
        key_t = rotate(proj[batch, key_rows, :])
        value_t = proj[batch, value_rows, :]
        key = key_t.T.astype(BF16)
        value = value_t.T.astype(BF16)
        key_t = key_t.astype(BF16)
        value_t = value_t.astype(BF16)
        kept = lax.broadcasted_iota(jnp.int32, (SEQ, SEQ), 0) <= lax.broadcasted_iota(jnp.int32, (SEQ, SEQ), 1)
        dkey = jnp.zeros((HEAD_SIZE, SEQ), F32)
        dvalue = jnp.zeros((HEAD_SIZE, SEQ), F32)
        for head in range(4):
            first = 256 * group + HEAD_SIZE * head
            rows = pl.ds(pl.multiple_of(first, HEAD_SIZE), HEAD_SIZE)
            query_t = (rotate(proj[batch, rows, :]) * HEAD_SIZE**-0.5).astype(BF16)
            scores = jnp.where(kept, nn(key, query_t), -1e30)
            raised = jnp.exp(scores - jnp.max(scores, axis=0, keepdims=True))
            probs = raised * (1.0 / jnp.sum(raised, axis=0, keepdims=True))
            probs_b = probs.astype(BF16)
            context_rows = pl.ds(pl.multiple_of(O_AT + first, HEAD_SIZE), HEAD_SIZE)
            lhs[batch, context_rows, :] = nn(value_t, probs_b).astype(BF16)
            cot = dctx[batch, rows, :]
            dprobs = nn(value, cot)
            dvalue = dvalue + nt(cot, probs_b)
            delta = jnp.sum(dprobs * probs, axis=0, keepdims=True)
            dscores = (probs * (dprobs - delta)).astype(BF16)
            dquery = nn(key_t, dscores) * HEAD_SIZE**-0.5
            lhs[batch, rows, :] = rotate_back(dquery).astype(BF16)
            dkey = dkey + nt(query_t, dscores)
        lhs[batch, key_rows, :] = rotate_back(dkey).astype(BF16)
        lhs[batch, value_rows, :] = dvalue.astype(BF16)
        return carry

    lax.fori_loop(0, 8, attention, 0)

    def sum_copy(place, going_up):
        landing, arrived = (from_low, low_recv) if going_up else (from_high, high_recv)
        return pltpu.make_async_remote_copy(
            src_ref=stage.at[place],
            dst_ref=landing.at[place],
            send_sem=sum_send.at[place],
            recv_sem=arrived.at[place],
            device_id=(section, up if going_up else down),
            device_id_type=MESH,
        )

    def final_copy(which, quarter):
        row = CHUNK * (PER_Z * z + which) + PIECE * quarter
        inside = row - PER_Z * CHUNK * z
        keeper = lax.div(inside, SHARD)
        offset = pl.multiple_of(inside - SHARD * keeper, PIECE)
        return pltpu.make_async_remote_copy(
            src_ref=stage.at[place_of(PER_Z * z + which), pl.ds(PIECE * quarter, PIECE)],
            dst_ref=final.at[owner_y, pl.ds(offset, PIECE)],
            send_sem=final_send.at[4 * which + quarter],
            recv_sem=final_recv.at[owner_y],
            device_id=(after, 4 * z + keeper),
            device_id_type=MESH,
        )

    def sum_step(n):
        m = n - PER_Z
        middle = jnp.logical_and(n >= PER_Z, n < 35)
        last = n >= 35
        away = jnp.where(n < PER_Z, 4, jnp.where(middle, 3 - lax.div(m, 10), 0))
        which = jnp.where(n < PER_Z, n, jnp.where(middle, lax.div(lax.rem(m, 10), 2), n - 35))
        falling = jnp.logical_and(middle, lax.rem(m, 2) == 1)
        home = lax.rem(jnp.where(falling, z - away, z + away) + N_Z, N_Z)
        block = PER_Z * home + which
        odd = lax.rem(block, 2)
        mine = core_of(block) == core
        rises = jnp.where(middle, jnp.logical_not(falling), odd == 0)
        has_low = jnp.logical_or(last, jnp.logical_and(rises, away < 4 - odd))
        has_high = jnp.logical_or(last, jnp.logical_and(jnp.logical_not(rises), away < 3 + odd))
        go_up = jnp.logical_and(mine, jnp.logical_and(rises, jnp.logical_not(last)))
        go_down = jnp.logical_and(mine, jnp.logical_and(jnp.logical_not(rises), jnp.logical_not(last)))
        return place_of(block), which, mine, has_low, has_high, go_up, go_down, jnp.logical_and(mine, last)

    def reduce(n, carry):
        place, which, mine, has_low, has_high, go_up, go_down, last = sum_step(n)

        @pl.when(mine)
        def _():
            rows = pl.ds(pl.multiple_of(place * CHUNK, CHUNK), CHUNK)
            side = jnp.where(place >= QKV_BLOCKS, 1, 0)
            for tile in range(4):
                columns = slice(tile * width // 4, (tile + 1) * width // 4)
                value = nn(lhs[0, rows, :], acts[side, 0, :, columns])
                for batch in range(1, 2 * MB):
                    value = value + nn(lhs[batch, rows, :], acts[side, batch, :, columns])
                total[:, columns] = value

        @pl.when(jnp.logical_and(mine, has_low))
        def _():
            sum_copy(place, True).wait_recv()
            total[...] += from_low[place].astype(F32)

        @pl.when(jnp.logical_and(mine, has_high))
        def _():
            sum_copy(place, False).wait_recv()
            total[...] += from_high[place].astype(F32)

        @pl.when(mine)
        def _():
            stage[place] = total[...].astype(BF16)

        @pl.when(go_up)
        def _():
            sum_copy(place, True).start()

        @pl.when(go_down)
        def _():
            sum_copy(place, False).start()

        @pl.when(last)
        def _():
            for quarter in range(CHUNK // PIECE):
                final_copy(which, quarter).start()

        return carry

    lax.fori_loop(0, 40, reduce, 0)

    for copy in id_copies + pick_copies + norm_copies + pass_copies:
        copy.wait_send()
    for piece in range(PIECES):
        for half_y in range(2):
            first_copy(piece, half_y).wait_send()

    def drain(n, carry):
        place, _, send_up, send_down = gather_step(n)

        @pl.when(send_up)
        def _():
            gather_copy(place, True).wait_send()

        @pl.when(send_down)
        def _():
            gather_copy(place, False).wait_send()

        place, which, _, _, _, go_up, go_down, last = sum_step(n)

        @pl.when(jnp.logical_or(go_up, go_down))
        def _():
            sum_copy(place, True).wait_send()

        @pl.when(last)
        def _():
            for quarter in range(CHUNK // PIECE):
                final_copy(which, quarter).wait_send()

        return carry

    lax.fori_loop(0, 40, drain, 0)

    for source in range(2):
        pltpu.make_async_remote_copy(
            src_ref=final.at[source],
            dst_ref=final.at[source],
            send_sem=final_send.at[0],
            recv_sem=final_recv.at[source],
            device_id=(after, dp),
            device_id_type=MESH,
        ).wait_recv()
    grad_ref[...] = final[0].astype(F32) + final[1].astype(F32)


def summed_gradient(params, sent, back, ids):
    width = params.shape[-1]
    frequency = rope_base ** (-np.arange(HEAD_SIZE // 2, dtype=np.float64) * 2.0 / HEAD_SIZE)
    angles = frequency[:, None] * np.arange(SEQ, dtype=np.float64)[None, :]
    cosine = jnp.asarray(np.cos(angles), F32)
    sine = jnp.asarray(np.sin(angles), F32)
    wide_ids = jnp.broadcast_to(ids.reshape(MB, 1), (MB, 128))
    wide_ids = jnp.concatenate([wide_ids, jnp.zeros((8 - MB, 128), jnp.int32)], axis=0)
    dma = pltpu.SemaphoreType.DMA
    in_vmem = pl.BlockSpec(memory_space=pltpu.VMEM)
    anywhere = pl.BlockSpec(memory_space=pl.ANY)
    return pl.pallas_call(
        kernel,
        out_shape=jax.ShapeDtypeStruct((SHARD, width), F32),
        in_specs=[anywhere, anywhere, anywhere, in_vmem, in_vmem, in_vmem],
        out_specs=in_vmem,
        scratch_shapes=[
            pltpu.VMEM((SHARD, width), BF16),
            pltpu.VMEM((LOG, SEQ, width), BF16),
            pltpu.VMEM((LOG, SEQ, width), BF16),
            pltpu.VMEM((8, 128), jnp.int32),
            pltpu.VMEM((8, 128), jnp.int32),
            pltpu.SMEM((8, 128), jnp.int32),
            pltpu.SMEM((8, 128), jnp.int32),
            pltpu.VMEM((LOCAL, CHUNK, width), BF16),
            pltpu.VMEM((2, 2 * MB, SEQ, width), BF16),
            pltpu.VMEM((MB, SEQ, width), BF16),
            pltpu.VMEM((2 * MB, O_AT, SEQ), F32),
            pltpu.VMEM((2 * MB, Q_ROWS, SEQ), BF16),
            pltpu.VMEM((2 * MB, LOCAL * CHUNK, SEQ), BF16),
            pltpu.VMEM((CHUNK, width), F32),
            pltpu.VMEM((LOCAL, CHUNK, width), BF16),
            pltpu.VMEM((LOCAL, CHUNK, width), BF16),
            pltpu.VMEM((LOCAL, CHUNK, width), BF16),
            pltpu.VMEM((2, SHARD, width), BF16),
            dma((3,)),
            dma((2,)),
            dma((2,)),
            dma((2,)),
            dma((2 * PIECES,)),
            dma((LOCAL,)),
            dma((LOCAL,)),
            dma((LOCAL,)),
            dma((MB,)),
            dma((MB,)),
            dma((MB,)),
            dma((MB,)),
            dma((MB,)),
            dma((MB,)),
            dma((LOCAL,)),
            dma((LOCAL,)),
            dma((LOCAL,)),
            dma((4 * PER_Z,)),
            dma((2,)),
        ],
        compiler_params=pltpu.CompilerParams(
            collective_id=0, has_side_effects=True, vmem_limit_bytes=60 * 1024 * 1024
        ),
    )(params, sent, back, wide_ids, cosine, sine)


def apply_adam(weights, first_moment, second_moment, gradient):
    first_new = 0.9 * first_moment + 0.1 * gradient
    second_new = 0.999 * second_moment + 0.001 * gradient * gradient
    fix_first = 1.0 - 0.9**STEP
    fix_second = 1.0 - 0.999**STEP
    update = first_new / fix_first / (jnp.sqrt(second_new / fix_second) + 1e-08)
    current = weights.astype(F32)
    renewed = (current - learn_rate * (update + decay_rate * current)).astype(BF16)
    return (renewed, first_new, second_new)


def shards(params, moment_one, moment_two, sent_rows, back_rows, slot_ids):
    summed = summed_gradient(params[0], sent_rows[0, 0], back_rows[0, 0], slot_ids[0, 0])
    renewed, first_new, second_new = apply_adam(params[0], moment_one[0], moment_two[0], summed / N_DP)
    return (renewed[None], first_new[None], second_new[None])


def solution(mesh):
    in_specs = (
        P("section", "dp", None),
        P("section", "dp", None),
        P("section", "dp", None),
        P("section", "dp", None, None, None),
        P("section", "dp", None, None, None),
        P("section", "dp", None),
    )
    out_specs = (P("section", "dp", None), P("section", "dp", None), P("section", "dp", None))
    return jax.shard_map(shards, mesh=mesh, in_specs=in_specs, out_specs=out_specs, check_vma=False)
```

```python
import jax
import jax.numpy as jnp
import numpy as np
from jax import lax
from jax.experimental import pallas as pl
from jax.experimental.pallas import tpu as pltpu
from jax.sharding import PartitionSpec as P

HEAD_SIZE = 64
QUERY_HEADS = 16
KEY_VALUE_HEADS = 4
STEP = 100
SEQ = 192
LOG = 4
MB = 2
PROWS = 2560

N_SECTION = 8
N_DP = 32
N_Z = 8
CHUNK = 64
PER_Z = 5
LOCAL = 20
SHARD = 80
LEAD = 8
PIECE = 16
PIECES = SHARD // PIECE
Q_ROWS = 512
K_AT = 512
V_AT = 640
O_AT = 768
QKV_BLOCKS = 12

rope_base = 500000.0
learn_rate = 0.0003
decay_rate = 0.1

MESH = pl.DeviceIdType.MESH
BF16 = jnp.bfloat16
F32 = jnp.float32


def nn(a, b):
    return lax.dot_general(a, b, (((1,), (0,)), ((), ())), preferred_element_type=F32)


def nt(a, b):
    return lax.dot_general(a, b, (((1,), (1,)), ((), ())), preferred_element_type=F32)


def core_of(block):
    return jnp.where(
        block < 16,
        lax.div(block, 8),
        jnp.where(block < 24, lax.rem(lax.div(block - 16, 2), 2), lax.div(block - 24, 8)),
    )


def place_of(block):
    return jnp.where(
        block < 16,
        lax.rem(block, 8),
        jnp.where(
            block < 24,
            8 + 2 * lax.div(block - 16, 4) + lax.rem(block - 16, 2),
            12 + lax.rem(block - 24, 8),
        ),
    )


def by_y(home, which):
    even = lax.rem(home, 2) == 0
    stays = jnp.logical_or(which == 2, which == jnp.where(even, 0, 4))
    return jnp.logical_not(stays)


def more_down(home, which):
    even = lax.rem(home, 2) == 0
    lone = which == jnp.where(even, 1, 3)
    second = jnp.logical_or(which == 4, which == jnp.where(even, 2, 1))
    return jnp.where(lone, lax.rem(lax.div(home, 2), 2), jnp.where(second, 1, 0))


def kernel(
    params_hbm,
    sent_hbm,
    back_hbm,
    ids_ref,
    cos_ref,
    sin_ref,
    grad_ref,
    shard,
    sent,
    back,
    ids_next,
    ids_prev,
    ids_one,
    ids_two,
    weights,
    relay,
    acts,
    picked,
    proj,
    dctx,
    lhs,
    total,
    stage,
    given,
    from_low,
    from_high,
    final,
    sem_local,
    sem_ids,
    sem_ids_send,
    sem_ids_recv,
    first_send,
    gather_up,
    gather_down,
    gather_recv,
    relay_up,
    relay_down,
    relay_out,
    relay_recv,
    own_local,
    own_send,
    own_recv,
    pick_send,
    pick_recv,
    pass_send,
    pass_recv,
    sum_send,
    low_recv,
    high_recv,
    give_send,
    give_recv,
    final_send,
    final_recv,
):
    section = lax.axis_index("section")
    dp = lax.axis_index("dp")
    z = lax.div(dp, 4)
    core = lax.rem(dp, 2)
    my_y = lax.rem(lax.div(dp, 2), 2)
    odd_section = lax.rem(section, 2)
    partner = section + 1 - 2 * odd_section
    sibling = dp + 1 - 2 * core
    up = lax.rem(dp + 4, N_DP)
    down = lax.rem(dp + N_DP - 4, N_DP)
    before = lax.rem(section + N_SECTION - 1, N_SECTION)
    after = lax.rem(section + 1, N_SECTION)
    before_two = lax.rem(section + N_SECTION - 2, N_SECTION)
    after_two = lax.rem(section + 2, N_SECTION)
    width = weights.shape[2]

    loads = [
        pltpu.make_async_copy(params_hbm, shard, sem_local.at[0]),
        pltpu.make_async_copy(sent_hbm, sent, sem_local.at[1]),
        pltpu.make_async_copy(back_hbm, back, sem_local.at[2]),
    ]
    for load in loads:
        load.start()

    barrier = pltpu.get_barrier_semaphore()
    beyond = jnp.where(odd_section == 0, before, after)
    peers = [(section, sibling), (section, up), (section, down), (before_two, dp), (after_two, dp), (beyond, dp)]
    for quarter in range(4):
        peers.append((partner, 4 * z + quarter))
    for peer in peers:
        pl.semaphore_signal(barrier, inc=1, device_id=peer, device_id_type=MESH)
    pl.semaphore_wait(barrier, len(peers))

    id_copies = [
        pltpu.make_async_remote_copy(
            src_ref=ids_ref,
            dst_ref=ids_next,
            send_sem=sem_ids_send.at[0],
            recv_sem=sem_ids_recv.at[0],
            device_id=(before, dp),
            device_id_type=MESH,
        ),
        pltpu.make_async_remote_copy(
            src_ref=ids_ref,
            dst_ref=ids_prev,
            send_sem=sem_ids_send.at[1],
            recv_sem=sem_ids_recv.at[1],
            device_id=(after, dp),
            device_id_type=MESH,
        ),
    ]
    for copy in id_copies:
        copy.start()

    loads[0].wait()

    def first_copy(piece, half):
        row = SHARD * dp + PIECE * piece
        block = lax.div(row, CHUNK)
        return pltpu.make_async_remote_copy(
            src_ref=shard.at[pl.ds(PIECE * piece, PIECE)],
            dst_ref=weights.at[place_of(block), pl.ds(pl.multiple_of(lax.rem(row, CHUNK), PIECE), PIECE)],
            send_sem=first_send.at[2 * piece + half],
            recv_sem=gather_recv.at[place_of(block)],
            device_id=(partner, 4 * z + 2 * half + core_of(block)),
            device_id_type=MESH,
        )

    def relay_piece(piece, local):
        row = SHARD * dp + PIECE * piece
        block = lax.div(row, CHUNK)
        source = shard.at[pl.ds(PIECE * piece, PIECE)]
        target = relay.at[place_of(block), pl.ds(pl.multiple_of(lax.rem(row, CHUNK), PIECE), PIECE)]
        arrived = relay_recv.at[place_of(block)]
        if local:
            return pltpu.make_async_copy(source, target, arrived)
        return pltpu.make_async_remote_copy(
            src_ref=source,
            dst_ref=target,
            send_sem=first_send.at[2 * piece],
            recv_sem=arrived,
            device_id=(section, sibling),
            device_id_type=MESH,
        )

    def piece_way(piece):
        block = lax.div(SHARD * dp + PIECE * piece, CHUNK)
        across = by_y(z, block - PER_Z * z)
        here = core_of(block) == core
        return across, jnp.logical_and(across, here), jnp.logical_and(across, jnp.logical_not(here))

    for piece in range(PIECES):
        across, here, there = piece_way(piece)

        @pl.when(jnp.logical_not(across))
        def _(piece=piece):
            for half in range(2):
                first_copy(piece, half).start()

        @pl.when(here)
        def _(piece=piece):
            relay_piece(piece, True).start()

        @pl.when(there)
        def _(piece=piece):
            relay_piece(piece, False).start()

    stays, leaves = odd_section, 1 - odd_section
    target_section = jnp.where(odd_section == 0, before_two, after_two)
    id_copies[0].wait_recv()
    to_one = pltpu.make_async_copy(ids_next, ids_one, sem_ids.at[0])
    to_one.start()
    to_one.wait()
    id_copies[1].wait_recv()
    to_two = pltpu.make_async_copy(ids_prev, ids_two, sem_ids.at[1])
    to_two.start()
    to_two.wait()
    loads[1].wait()
    loads[2].wait()
    own_copies = []
    own_locals = []
    pick_copies = []
    for m in range(MB):
        wanted_one, wanted_two = ids_one[m, 0], ids_two[m, 0]

        def pick_rows(n, carry, m=m, wanted_one=wanted_one, wanted_two=wanted_two):
            rows = pl.ds(pl.multiple_of(n * 16, 16), 16)
            value = sent[wanted_one, rows, :].astype(F32)
            scaling = lax.rsqrt(jnp.mean(value * value, axis=-1, keepdims=True) + 1e-05)
            picked[0, m, rows, :] = (value * scaling).astype(BF16)
            picked[1, m, rows, :] = back[wanted_two, rows, :]
            return carry

        lax.fori_loop(0, SEQ // 16, pick_rows, 0)
        pick_copies.append(
            pltpu.make_async_remote_copy(
                src_ref=picked.at[leaves, m],
                dst_ref=acts.at[leaves, 2 * core + m],
                send_sem=pick_send.at[m],
                recv_sem=pick_recv.at[m],
                device_id=(target_section, dp),
                device_id_type=MESH,
            )
        )
        own_copies.append(
            pltpu.make_async_remote_copy(
                src_ref=picked.at[stays, m],
                dst_ref=acts.at[stays, 2 * core + m],
                send_sem=own_send.at[m],
                recv_sem=own_recv.at[m],
                device_id=(section, sibling),
                device_id_type=MESH,
            )
        )
        own_locals.append(
            pltpu.make_async_copy(picked.at[stays, m], acts.at[stays, 2 * core + m], own_local.at[m])
        )
        pick_copies[m].start()
        own_copies[m].start()
        own_locals[m].start()

    def gather_copy(place, going_up):
        return pltpu.make_async_remote_copy(
            src_ref=weights.at[place],
            dst_ref=weights.at[place],
            send_sem=(gather_up if going_up else gather_down).at[place],
            recv_sem=gather_recv.at[place],
            device_id=(section, up if going_up else down),
            device_id_type=MESH,
        )

    def relay_copy(place, going_up):
        return pltpu.make_async_remote_copy(
            src_ref=relay.at[place],
            dst_ref=relay.at[place],
            send_sem=(relay_up if going_up else relay_down).at[place],
            recv_sem=relay_recv.at[place],
            device_id=(section, up if going_up else down),
            device_id_type=MESH,
        )

    def relay_over(place, half):
        return pltpu.make_async_remote_copy(
            src_ref=relay.at[place],
            dst_ref=weights.at[place],
            send_sem=relay_out.at[LOCAL * half + place],
            recv_sem=gather_recv.at[place],
            device_id=(partner, 4 * z + 2 * half + core),
            device_id_type=MESH,
        )

    def gather_step(n):
        m = n - PER_Z
        middle = jnp.logical_and(n >= PER_Z, n < 35)
        away = jnp.where(n < PER_Z, 0, jnp.where(middle, 1 + lax.div(m, 10), 4))
        which = jnp.where(n < PER_Z, n, jnp.where(middle, lax.div(lax.rem(m, 10), 2), n - 35))
        rising = jnp.logical_and(middle, lax.rem(m, 2) == 0)
        home = lax.rem(jnp.where(rising, z - away, z + away) + N_Z, N_Z)
        block = PER_Z * home + which
        odd = more_down(home, which)
        mine = core_of(block) == core
        across = by_y(home, which)
        mine_relay = jnp.logical_and(jnp.logical_and(mine, across), lax.div(which, 3) == my_y)
        mine_ring = jnp.logical_and(mine, jnp.logical_not(across))
        start = n < PER_Z
        falling = jnp.logical_and(middle, jnp.logical_not(rising))
        send_up = jnp.logical_or(start, jnp.logical_and(rising, away < 4 - odd))
        send_down = jnp.logical_or(start, jnp.logical_and(falling, away < 3 + odd))
        return place_of(block), mine_ring, mine_relay, send_up, send_down

    def gather(n, carry):
        place, mine_ring, mine_relay, send_up, send_down = gather_step(n)

        @pl.when(mine_ring)
        def _():
            gather_copy(place, True).wait_recv()

        @pl.when(jnp.logical_and(mine_ring, send_up))
        def _():
            gather_copy(place, True).start()

        @pl.when(jnp.logical_and(mine_ring, send_down))
        def _():
            gather_copy(place, False).start()

        @pl.when(mine_relay)
        def _():
            relay_copy(place, True).wait_recv()

        @pl.when(jnp.logical_and(mine_relay, send_up))
        def _():
            relay_copy(place, True).start()

        @pl.when(jnp.logical_and(mine_relay, send_down))
        def _():
            relay_copy(place, False).start()

        @pl.when(mine_relay)
        def _():
            for half_y in range(2):
                relay_over(place, half_y).start()

        return carry

    lax.fori_loop(0, 40, gather, 0)

    pass_copies = []
    for m in range(MB):
        pick_copies[m].wait_recv()
        pass_copies.append(
            pltpu.make_async_remote_copy(
                src_ref=acts.at[leaves, 2 * core + m],
                dst_ref=acts.at[leaves, 2 * core + m],
                send_sem=pass_send.at[m],
                recv_sem=pass_recv.at[m],
                device_id=(section, sibling),
                device_id_type=MESH,
            )
        )
        pass_copies[m].start()

    def arrive(block, carry):
        across = by_y(lax.div(block, PER_Z), lax.rem(block, PER_Z))

        @pl.when(jnp.logical_and(across, core_of(block) == core))
        def _():
            gather_copy(place_of(block), True).wait_recv()

        return carry

    lax.fori_loop(0, 40, arrive, 0)

    for m in range(MB):
        own_locals[m].wait()
        own_copies[m].wait_recv()
        pass_copies[m].wait_recv()

    def project(n, carry):
        batch, part = lax.div(n, 3), lax.rem(n, 3)
        rows = weights[pl.ds(4 * part, 4)].reshape(4 * CHUNK, width)
        proj[batch, pl.ds(pl.multiple_of(part * 256, 256), 256), :] = nt(rows, acts[0, batch])
        return carry

    lax.fori_loop(0, 12, project, 0)

    def cotangent(n, carry):
        batch, part = lax.div(n, 2), lax.rem(n, 2)
        rows = weights[pl.ds(QKV_BLOCKS + 4 * part, 4)].reshape(4 * CHUNK, width)
        dctx[batch, pl.ds(pl.multiple_of(part * 256, 256), 256), :] = nt(rows, acts[1, batch]).astype(BF16)
        return carry

    lax.fori_loop(0, 8, cotangent, 0)

    cosine, sine = cos_ref[...], sin_ref[...]
    half = HEAD_SIZE // 2

    def rotate(value):
        a, b = value[:half], value[half:]
        return jnp.concatenate([a * cosine - b * sine, b * cosine + a * sine], axis=0)

    def rotate_back(value):
        a, b = value[:half], value[half:]
        return jnp.concatenate([a * cosine + b * sine, b * cosine - a * sine], axis=0)

    def attention(n, carry):
        batch, group = lax.div(n, 2), lax.rem(n, 2)
        key_rows = pl.ds(pl.multiple_of(K_AT + HEAD_SIZE * group, HEAD_SIZE), HEAD_SIZE)
        value_rows = pl.ds(pl.multiple_of(V_AT + HEAD_SIZE * group, HEAD_SIZE), HEAD_SIZE)
        key_t = rotate(proj[batch, key_rows, :])
        value_t = proj[batch, value_rows, :]
        key = key_t.T.astype(BF16)
        value = value_t.T.astype(BF16)
        key_t = key_t.astype(BF16)
        value_t = value_t.astype(BF16)
        kept = lax.broadcasted_iota(jnp.int32, (SEQ, SEQ), 0) <= lax.broadcasted_iota(jnp.int32, (SEQ, SEQ), 1)
        dkey = jnp.zeros((HEAD_SIZE, SEQ), F32)
        dvalue = jnp.zeros((HEAD_SIZE, SEQ), F32)
        for head in range(4):
            first = 256 * group + HEAD_SIZE * head
            rows = pl.ds(pl.multiple_of(first, HEAD_SIZE), HEAD_SIZE)
            query_t = (rotate(proj[batch, rows, :]) * HEAD_SIZE**-0.5).astype(BF16)
            scores = jnp.where(kept, nn(key, query_t), -1e30)
            raised = jnp.exp(scores - jnp.max(scores, axis=0, keepdims=True))
            probs = raised * (1.0 / jnp.sum(raised, axis=0, keepdims=True))
            probs_b = probs.astype(BF16)
            context_rows = pl.ds(pl.multiple_of(O_AT + first, HEAD_SIZE), HEAD_SIZE)
            lhs[batch, context_rows, :] = nn(value_t, probs_b).astype(BF16)
            cot = dctx[batch, rows, :]
            dprobs = nn(value, cot)
            dvalue = dvalue + nt(cot, probs_b)
            delta = jnp.sum(dprobs * probs, axis=0, keepdims=True)
            dscores = (probs * (dprobs - delta)).astype(BF16)
            dquery = nn(key_t, dscores) * HEAD_SIZE**-0.5
            lhs[batch, rows, :] = rotate_back(dquery).astype(BF16)
            dkey = dkey + nt(query_t, dscores)
        lhs[batch, key_rows, :] = rotate_back(dkey).astype(BF16)
        lhs[batch, value_rows, :] = dvalue.astype(BF16)
        return carry

    lax.fori_loop(0, 8, attention, 0)

    def sum_copy(place, going_up):
        landing, arrived = (from_low, low_recv) if going_up else (from_high, high_recv)
        return pltpu.make_async_remote_copy(
            src_ref=stage.at[place],
            dst_ref=landing.at[place],
            send_sem=sum_send.at[place],
            recv_sem=arrived.at[place],
            device_id=(section, up if going_up else down),
            device_id_type=MESH,
        )

    def give_copy(place, which):
        return pltpu.make_async_remote_copy(
            src_ref=stage.at[place],
            dst_ref=given.at[my_y, place],
            send_sem=give_send.at[place],
            recv_sem=give_recv.at[LOCAL * my_y + place],
            device_id=(partner, 4 * z + 2 * lax.div(which, 3) + core),
            device_id_type=MESH,
        )

    def keeper_of(which, quarter):
        inside = CHUNK * which + PIECE * quarter
        keeper = lax.div(inside, SHARD)
        return keeper, lax.div(inside - SHARD * keeper, PIECE)

    def final_copy(which, quarter):
        keeper, piece = keeper_of(which, quarter)
        return pltpu.make_async_remote_copy(
            src_ref=stage.at[place_of(PER_Z * z + which), pl.ds(PIECE * quarter, PIECE)],
            dst_ref=final.at[my_y, pl.ds(pl.multiple_of(PIECE * piece, PIECE), PIECE)],
            send_sem=final_send.at[4 * which + quarter],
            recv_sem=final_recv.at[PIECES * my_y + piece],
            device_id=(partner, 4 * z + keeper),
            device_id_type=MESH,
        )

    def relay_final(which, quarter, local):
        _, piece = keeper_of(which, quarter)
        source = given.at[0, place_of(PER_Z * z + which), pl.ds(PIECE * quarter, PIECE)]
        target = final.at[0, pl.ds(pl.multiple_of(PIECE * piece, PIECE), PIECE)]
        if local:
            return pltpu.make_async_copy(source, target, final_recv.at[piece])
        return pltpu.make_async_remote_copy(
            src_ref=source,
            dst_ref=target,
            send_sem=final_send.at[4 * which + quarter],
            recv_sem=final_recv.at[piece],
            device_id=(section, sibling),
            device_id_type=MESH,
        )

    def relay_sum_copy(place, going_up):
        landing, arrived = (from_low, low_recv) if going_up else (from_high, high_recv)
        return pltpu.make_async_remote_copy(
            src_ref=given.at[0, place],
            dst_ref=landing.at[place],
            send_sem=sum_send.at[place],
            recv_sem=arrived.at[place],
            device_id=(section, up if going_up else down),
            device_id_type=MESH,
        )

    def sum_step(n):
        m = n - PER_Z
        middle = jnp.logical_and(n >= PER_Z, n < 35)
        last = n >= 35
        away = jnp.where(n < PER_Z, 4, jnp.where(middle, 3 - lax.div(m, 10), 0))
        which = jnp.where(n < PER_Z, n, jnp.where(middle, lax.div(lax.rem(m, 10), 2), n - 35))
        falling = jnp.logical_and(middle, lax.rem(m, 2) == 1)
        home = lax.rem(jnp.where(falling, z - away, z + away) + N_Z, N_Z)
        block = PER_Z * home + which
        odd = more_down(home, which)
        mine = core_of(block) == core
        across = by_y(home, which)
        mine_give = jnp.logical_and(mine, across)
        mine_relay = jnp.logical_and(mine_give, lax.div(which, 3) == my_y)
        mine_ring = jnp.logical_and(mine, jnp.logical_not(across))
        rises = jnp.where(middle, jnp.logical_not(falling), odd == 0)
        has_low = jnp.logical_or(last, jnp.logical_and(rises, away < 4 - odd))
        has_high = jnp.logical_or(last, jnp.logical_and(jnp.logical_not(rises), away < 3 + odd))
        go_up = jnp.logical_and(rises, jnp.logical_not(last))
        go_down = jnp.logical_and(jnp.logical_not(rises), jnp.logical_not(last))
        return place_of(block), which, mine_ring, mine_give, mine_relay, has_low, has_high, go_up, go_down, last

    def block_gradient(place):
        rows = pl.ds(pl.multiple_of(place * CHUNK, CHUNK), CHUNK)
        side = jnp.where(place >= QKV_BLOCKS, 1, 0)
        for tile in range(4):
            columns = slice(tile * width // 4, (tile + 1) * width // 4)
            value = nn(lhs[0, rows, :], acts[side, 0, :, columns])
            for batch in range(1, 2 * MB):
                value = value + nn(lhs[batch, rows, :], acts[side, batch, :, columns])
            total[:, columns] = value

    def give(n):
        place, which, _, mine_give, _, _, _, _, _, _ = sum_step(n)

        @pl.when(mine_give)
        def _():
            block_gradient(place)
            stage[place] = total[...].astype(BF16)
            give_copy(place, which).start()

    def reduce(n):
        place, which, mine_ring, _, mine_relay, has_low, has_high, go_up, go_down, last = sum_step(n)

        @pl.when(mine_ring)
        def _():
            block_gradient(place)

        @pl.when(mine_relay)
        def _():
            for source in range(2):
                pltpu.make_async_remote_copy(
                    src_ref=given.at[source, place],
                    dst_ref=given.at[source, place],
                    send_sem=give_send.at[place],
                    recv_sem=give_recv.at[LOCAL * source + place],
                    device_id=(partner, dp),
                    device_id_type=MESH,
                ).wait_recv()
            total[...] = given[0, place].astype(F32) + given[1, place].astype(F32)

        active = jnp.logical_or(mine_ring, mine_relay)

        @pl.when(jnp.logical_and(active, has_low))
        def _():
            sum_copy(place, True).wait_recv()
            total[...] += from_low[place].astype(F32)

        @pl.when(jnp.logical_and(active, has_high))
        def _():
            sum_copy(place, False).wait_recv()
            total[...] += from_high[place].astype(F32)

        @pl.when(mine_ring)
        def _():
            stage[place] = total[...].astype(BF16)

        @pl.when(mine_relay)
        def _():
            given[0, place] = total[...].astype(BF16)

        for going_up, goes in ((True, go_up), (False, go_down)):

            @pl.when(jnp.logical_and(mine_ring, goes))
            def _(going_up=going_up):
                sum_copy(place, going_up).start()

            @pl.when(jnp.logical_and(mine_relay, goes))
            def _(going_up=going_up):
                relay_sum_copy(place, going_up).start()

        @pl.when(jnp.logical_and(mine_ring, last))
        def _():
            for quarter in range(CHUNK // PIECE):
                final_copy(which, quarter).start()

        for quarter in range(CHUNK // PIECE):
            keeper, _ = keeper_of(which, quarter)
            here = lax.rem(keeper, 2) == core

            @pl.when(jnp.logical_and(jnp.logical_and(mine_relay, last), here))
            def _(quarter=quarter):
                relay_final(which, quarter, True).start()

            @pl.when(jnp.logical_and(jnp.logical_and(mine_relay, last), jnp.logical_not(here)))
            def _(quarter=quarter):
                relay_final(which, quarter, False).start()

    def lead(n, carry):
        give(n)
        return carry

    def both(n, carry):
        @pl.when(n < 40)
        def _():
            give(n)

        reduce(n - LEAD)
        return carry

    lax.fori_loop(0, LEAD, lead, 0)
    lax.fori_loop(LEAD, 40 + LEAD, both, 0)

    for copy in id_copies + pick_copies + own_copies + pass_copies:
        copy.wait_send()
    for piece in range(PIECES):
        across, _, there = piece_way(piece)

        @pl.when(jnp.logical_not(across))
        def _(piece=piece):
            for half_y in range(2):
                first_copy(piece, half_y).wait_send()

        @pl.when(there)
        def _(piece=piece):
            relay_piece(piece, False).wait_send()

    def drain(n, carry):
        place, mine_ring, mine_relay, send_up, send_down = gather_step(n)
        for going_up, goes in ((True, send_up), (False, send_down)):

            @pl.when(jnp.logical_and(mine_ring, goes))
            def _(going_up=going_up):
                gather_copy(place, going_up).wait_send()

            @pl.when(jnp.logical_and(mine_relay, goes))
            def _(going_up=going_up):
                relay_copy(place, going_up).wait_send()

        @pl.when(mine_relay)
        def _():
            for half_y in range(2):
                relay_over(place, half_y).wait_send()

        place, which, mine_ring, mine_give, mine_relay, _, _, _, _, last = sum_step(n)
        active = jnp.logical_or(mine_ring, mine_relay)

        @pl.when(jnp.logical_and(active, jnp.logical_not(last)))
        def _():
            sum_copy(place, True).wait_send()

        @pl.when(mine_give)
        def _():
            give_copy(place, which).wait_send()

        for quarter in range(CHUNK // PIECE):
            keeper, _ = keeper_of(which, quarter)
            away_core = lax.rem(keeper, 2) != core
            sent_on = jnp.logical_or(mine_ring, jnp.logical_and(mine_relay, away_core))

            @pl.when(jnp.logical_and(last, sent_on))
            def _(quarter=quarter):
                final_copy(which, quarter).wait_send()

        return carry

    lax.fori_loop(0, 40, drain, 0)

    def final_wait(piece, source):
        rows = pl.ds(PIECE * piece, PIECE)
        pltpu.make_async_remote_copy(
            src_ref=final.at[source, rows],
            dst_ref=final.at[source, rows],
            send_sem=final_send.at[0],
            recv_sem=final_recv.at[PIECES * source + piece],
            device_id=(section, sibling),
            device_id_type=MESH,
        ).wait_recv()

    for piece in range(PIECES):
        rows = pl.ds(PIECE * piece, PIECE)
        across, _, _ = piece_way(piece)
        final_wait(piece, 0)
        grad_ref[rows, :] = final[0, rows, :].astype(F32)

        @pl.when(jnp.logical_not(across))
        def _(piece=piece, rows=rows):
            final_wait(piece, 1)
            grad_ref[rows, :] += final[1, rows, :].astype(F32)


def summed_gradient(params, sent, back, ids):
    width = params.shape[-1]
    frequency = rope_base ** (-np.arange(HEAD_SIZE // 2, dtype=np.float64) * 2.0 / HEAD_SIZE)
    angles = frequency[:, None] * np.arange(SEQ, dtype=np.float64)[None, :]
    cosine = jnp.asarray(np.cos(angles), F32)
    sine = jnp.asarray(np.sin(angles), F32)
    wide_ids = jnp.broadcast_to(ids.reshape(MB, 1), (MB, 128))
    wide_ids = jnp.concatenate([wide_ids, jnp.zeros((8 - MB, 128), jnp.int32)], axis=0)
    dma = pltpu.SemaphoreType.DMA
    in_vmem = pl.BlockSpec(memory_space=pltpu.VMEM)
    anywhere = pl.BlockSpec(memory_space=pl.ANY)
    return pl.pallas_call(
        kernel,
        out_shape=jax.ShapeDtypeStruct((SHARD, width), F32),
        in_specs=[anywhere, anywhere, anywhere, in_vmem, in_vmem, in_vmem],
        out_specs=in_vmem,
        scratch_shapes=[
            pltpu.VMEM((SHARD, width), BF16),
            pltpu.VMEM((LOG, SEQ, width), BF16),
            pltpu.VMEM((LOG, SEQ, width), BF16),
            pltpu.VMEM((8, 128), jnp.int32),
            pltpu.VMEM((8, 128), jnp.int32),
            pltpu.SMEM((8, 128), jnp.int32),
            pltpu.SMEM((8, 128), jnp.int32),
            pltpu.VMEM((LOCAL, CHUNK, width), BF16),
            pltpu.VMEM((LOCAL, CHUNK, width), BF16),
            pltpu.VMEM((2, 2 * MB, SEQ, width), BF16),
            pltpu.VMEM((2, MB, SEQ, width), BF16),
            pltpu.VMEM((2 * MB, O_AT, SEQ), F32),
            pltpu.VMEM((2 * MB, Q_ROWS, SEQ), BF16),
            pltpu.VMEM((2 * MB, LOCAL * CHUNK, SEQ), BF16),
            pltpu.VMEM((CHUNK, width), F32),
            pltpu.VMEM((LOCAL, CHUNK, width), BF16),
            pltpu.VMEM((2, LOCAL, CHUNK, width), BF16),
            pltpu.VMEM((LOCAL, CHUNK, width), BF16),
            pltpu.VMEM((LOCAL, CHUNK, width), BF16),
            pltpu.VMEM((2, SHARD, width), BF16),
            dma((3,)),
            dma((2,)),
            dma((2,)),
            dma((2,)),
            dma((2 * PIECES,)),
            dma((LOCAL,)),
            dma((LOCAL,)),
            dma((LOCAL,)),
            dma((LOCAL,)),
            dma((LOCAL,)),
            dma((2 * LOCAL,)),
            dma((LOCAL,)),
            dma((MB,)),
            dma((MB,)),
            dma((MB,)),
            dma((MB,)),
            dma((MB,)),
            dma((MB,)),
            dma((MB,)),
            dma((LOCAL,)),
            dma((LOCAL,)),
            dma((LOCAL,)),
            dma((LOCAL,)),
            dma((2 * LOCAL,)),
            dma((4 * PER_Z,)),
            dma((2 * PIECES,)),
        ],
        compiler_params=pltpu.CompilerParams(
            collective_id=0, has_side_effects=True, vmem_limit_bytes=60 * 1024 * 1024
        ),
    )(params, sent, back, wide_ids, cosine, sine)


def apply_adam(weights, first_moment, second_moment, gradient):
    first_new = 0.9 * first_moment + 0.1 * gradient
    second_new = 0.999 * second_moment + 0.001 * gradient * gradient
    fix_first = 1.0 - 0.9**STEP
    fix_second = 1.0 - 0.999**STEP
    update = first_new / fix_first / (jnp.sqrt(second_new / fix_second) + 1e-08)
    current = weights.astype(F32)
    renewed = (current - learn_rate * (update + decay_rate * current)).astype(BF16)
    return (renewed, first_new, second_new)


def shards(params, moment_one, moment_two, sent_rows, back_rows, slot_ids):
    summed = summed_gradient(params[0], sent_rows[0, 0], back_rows[0, 0], slot_ids[0, 0])
    renewed, first_new, second_new = apply_adam(params[0], moment_one[0], moment_two[0], summed / N_DP)
    return (renewed[None], first_new[None], second_new[None])


def solution(mesh):
    in_specs = (
        P("section", "dp", None),
        P("section", "dp", None),
        P("section", "dp", None),
        P("section", "dp", None, None, None),
        P("section", "dp", None, None, None),
        P("section", "dp", None),
    )
    out_specs = (P("section", "dp", None), P("section", "dp", None), P("section", "dp", None))
    return jax.shard_map(shards, mesh=mesh, in_specs=in_specs, out_specs=out_specs, check_vma=False)
```

```python
import jax
import jax.numpy as jnp
import numpy as np
from jax import lax
from jax.experimental import pallas as pl
from jax.experimental.pallas import tpu as pltpu
from jax.sharding import PartitionSpec as P

HEAD_SIZE = 64
QUERY_HEADS = 16
KEY_VALUE_HEADS = 4
STEP = 100
SEQ = 192
LOG = 4
MB = 2
PROWS = 2560

N_SECTION = 8
N_DP = 32
N_Z = 8
CHUNK = 64
PER_Z = 5
LOCAL = 20
SHARD = 80
LEAD = 12
PIECE = 16
PIECES = SHARD // PIECE
Q_ROWS = 512
K_AT = 512
V_AT = 640
O_AT = 768
QKV_BLOCKS = 12

rope_base = 500000.0
learn_rate = 0.0003
decay_rate = 0.1

MESH = pl.DeviceIdType.MESH
BF16 = jnp.bfloat16
F32 = jnp.float32


def nn(a, b):
    return lax.dot_general(a, b, (((1,), (0,)), ((), ())), preferred_element_type=F32)


def nt(a, b):
    return lax.dot_general(a, b, (((1,), (1,)), ((), ())), preferred_element_type=F32)


def core_of(block):
    return jnp.where(
        block < 16,
        lax.div(block, 8),
        jnp.where(block < 24, lax.rem(lax.div(block - 16, 2), 2), lax.div(block - 24, 8)),
    )


def place_of(block):
    return jnp.where(
        block < 16,
        lax.rem(block, 8),
        jnp.where(
            block < 24,
            8 + 2 * lax.div(block - 16, 4) + lax.rem(block - 16, 2),
            12 + lax.rem(block - 24, 8),
        ),
    )


def by_y(home, which):
    even = lax.rem(home, 2) == 0
    stays = jnp.logical_or(which == 2, which == jnp.where(even, 0, 4))
    return jnp.logical_not(stays)


def in_order(home, turn, ring_first):
    even = lax.rem(home, 2) == 0
    turn = jnp.where(ring_first, lax.rem(turn + 3, PER_Z), turn)
    of_even = jnp.where(turn < 2, 2 * turn + 1, jnp.where(turn == 2, 4, 2 * turn - 6))
    of_odd = jnp.where(turn < 2, turn, jnp.where(turn == 2, 3, 2 * turn - 4))
    return jnp.where(even, of_even, of_odd)


def more_down(home, which):
    even = lax.rem(home, 2) == 0
    lone = which == jnp.where(even, 1, 3)
    second = jnp.logical_or(which == 4, which == jnp.where(even, 2, 1))
    return jnp.where(lone, lax.rem(lax.div(home, 2), 2), jnp.where(second, 1, 0))


def kernel(
    params_hbm,
    sent_hbm,
    back_hbm,
    ids_ref,
    cos_ref,
    sin_ref,
    grad_ref,
    shard,
    sent,
    back,
    ids_next,
    ids_prev,
    ids_one,
    ids_two,
    weights,
    relay,
    acts,
    picked,
    proj,
    dctx,
    lhs,
    total,
    stage,
    given,
    from_low,
    from_high,
    final,
    sem_local,
    sem_ids,
    sem_ids_send,
    sem_ids_recv,
    first_send,
    gather_up,
    gather_down,
    gather_recv,
    relay_up,
    relay_down,
    relay_out,
    relay_recv,
    own_local,
    own_send,
    own_recv,
    pick_send,
    pick_recv,
    pass_send,
    pass_recv,
    sum_send,
    low_recv,
    high_recv,
    give_send,
    give_recv,
    final_send,
    final_recv,
):
    section = lax.axis_index("section")
    dp = lax.axis_index("dp")
    z = lax.div(dp, 4)
    core = lax.rem(dp, 2)
    my_y = lax.rem(lax.div(dp, 2), 2)
    odd_section = lax.rem(section, 2)
    partner = section + 1 - 2 * odd_section
    sibling = dp + 1 - 2 * core
    up = lax.rem(dp + 4, N_DP)
    down = lax.rem(dp + N_DP - 4, N_DP)
    before = lax.rem(section + N_SECTION - 1, N_SECTION)
    after = lax.rem(section + 1, N_SECTION)
    before_two = lax.rem(section + N_SECTION - 2, N_SECTION)
    after_two = lax.rem(section + 2, N_SECTION)
    width = weights.shape[2]

    loads = [
        pltpu.make_async_copy(params_hbm, shard, sem_local.at[0]),
        pltpu.make_async_copy(sent_hbm, sent, sem_local.at[1]),
        pltpu.make_async_copy(back_hbm, back, sem_local.at[2]),
    ]
    for load in loads:
        load.start()

    barrier = pltpu.get_barrier_semaphore()
    beyond = jnp.where(odd_section == 0, before, after)
    peers = [(section, sibling), (section, up), (section, down), (before_two, dp), (after_two, dp), (beyond, dp)]
    for quarter in range(4):
        peers.append((partner, 4 * z + quarter))
    for peer in peers:
        pl.semaphore_signal(barrier, inc=1, device_id=peer, device_id_type=MESH)
    pl.semaphore_wait(barrier, len(peers))

    id_copies = [
        pltpu.make_async_remote_copy(
            src_ref=ids_ref,
            dst_ref=ids_next,
            send_sem=sem_ids_send.at[0],
            recv_sem=sem_ids_recv.at[0],
            device_id=(before, dp),
            device_id_type=MESH,
        ),
        pltpu.make_async_remote_copy(
            src_ref=ids_ref,
            dst_ref=ids_prev,
            send_sem=sem_ids_send.at[1],
            recv_sem=sem_ids_recv.at[1],
            device_id=(after, dp),
            device_id_type=MESH,
        ),
    ]
    for copy in id_copies:
        copy.start()

    loads[0].wait()

    def first_copy(piece, half):
        row = SHARD * dp + PIECE * piece
        block = lax.div(row, CHUNK)
        return pltpu.make_async_remote_copy(
            src_ref=shard.at[pl.ds(PIECE * piece, PIECE)],
            dst_ref=weights.at[place_of(block), pl.ds(pl.multiple_of(lax.rem(row, CHUNK), PIECE), PIECE)],
            send_sem=first_send.at[2 * piece + half],
            recv_sem=gather_recv.at[place_of(block)],
            device_id=(partner, 4 * z + 2 * half + core_of(block)),
            device_id_type=MESH,
        )

    def relay_piece(piece, local):
        row = SHARD * dp + PIECE * piece
        block = lax.div(row, CHUNK)
        source = shard.at[pl.ds(PIECE * piece, PIECE)]
        target = relay.at[place_of(block), pl.ds(pl.multiple_of(lax.rem(row, CHUNK), PIECE), PIECE)]
        arrived = relay_recv.at[place_of(block)]
        if local:
            return pltpu.make_async_copy(source, target, arrived)
        return pltpu.make_async_remote_copy(
            src_ref=source,
            dst_ref=target,
            send_sem=first_send.at[2 * piece],
            recv_sem=arrived,
            device_id=(section, sibling),
            device_id_type=MESH,
        )

    def piece_way(piece):
        block = lax.div(SHARD * dp + PIECE * piece, CHUNK)
        across = by_y(z, block - PER_Z * z)
        here = core_of(block) == core
        return across, jnp.logical_and(across, here), jnp.logical_and(across, jnp.logical_not(here))

    for piece in range(PIECES):
        across, here, there = piece_way(piece)

        @pl.when(jnp.logical_not(across))
        def _(piece=piece):
            for half in range(2):
                first_copy(piece, half).start()

        @pl.when(here)
        def _(piece=piece):
            relay_piece(piece, True).start()

        @pl.when(there)
        def _(piece=piece):
            relay_piece(piece, False).start()

    stays, leaves = odd_section, 1 - odd_section
    target_section = jnp.where(odd_section == 0, before_two, after_two)
    id_copies[0].wait_recv()
    to_one = pltpu.make_async_copy(ids_next, ids_one, sem_ids.at[0])
    to_one.start()
    to_one.wait()
    id_copies[1].wait_recv()
    to_two = pltpu.make_async_copy(ids_prev, ids_two, sem_ids.at[1])
    to_two.start()
    to_two.wait()
    loads[1].wait()
    loads[2].wait()
    own_copies = []
    own_locals = []
    pick_copies = []
    for m in range(MB):
        wanted_one, wanted_two = ids_one[m, 0], ids_two[m, 0]

        def pick_rows(n, carry, m=m, wanted_one=wanted_one, wanted_two=wanted_two):
            rows = pl.ds(pl.multiple_of(n * 16, 16), 16)
            value = sent[wanted_one, rows, :].astype(F32)
            scaling = lax.rsqrt(jnp.mean(value * value, axis=-1, keepdims=True) + 1e-05)
            picked[0, m, rows, :] = (value * scaling).astype(BF16)
            picked[1, m, rows, :] = back[wanted_two, rows, :]
            return carry

        lax.fori_loop(0, SEQ // 16, pick_rows, 0)
        pick_copies.append(
            pltpu.make_async_remote_copy(
                src_ref=picked.at[leaves, m],
                dst_ref=acts.at[leaves, 2 * core + m],
                send_sem=pick_send.at[m],
                recv_sem=pick_recv.at[m],
                device_id=(target_section, dp),
                device_id_type=MESH,
            )
        )
        own_copies.append(
            pltpu.make_async_remote_copy(
                src_ref=picked.at[stays, m],
                dst_ref=acts.at[stays, 2 * core + m],
                send_sem=own_send.at[m],
                recv_sem=own_recv.at[m],
                device_id=(section, sibling),
                device_id_type=MESH,
            )
        )
        own_locals.append(
            pltpu.make_async_copy(picked.at[stays, m], acts.at[stays, 2 * core + m], own_local.at[m])
        )
        pick_copies[m].start()
        own_copies[m].start()
        own_locals[m].start()

    def gather_copy(place, going_up):
        return pltpu.make_async_remote_copy(
            src_ref=weights.at[place],
            dst_ref=weights.at[place],
            send_sem=(gather_up if going_up else gather_down).at[place],
            recv_sem=gather_recv.at[place],
            device_id=(section, up if going_up else down),
            device_id_type=MESH,
        )

    def relay_copy(place, going_up):
        return pltpu.make_async_remote_copy(
            src_ref=relay.at[place],
            dst_ref=relay.at[place],
            send_sem=(relay_up if going_up else relay_down).at[place],
            recv_sem=relay_recv.at[place],
            device_id=(section, up if going_up else down),
            device_id_type=MESH,
        )

    def relay_over(place, half):
        return pltpu.make_async_remote_copy(
            src_ref=relay.at[place],
            dst_ref=weights.at[place],
            send_sem=relay_out.at[LOCAL * half + place],
            recv_sem=gather_recv.at[place],
            device_id=(partner, 4 * z + 2 * half + core),
            device_id_type=MESH,
        )

    def gather_step(n):
        m = n - PER_Z
        middle = jnp.logical_and(n >= PER_Z, n < 35)
        away = jnp.where(n < PER_Z, 0, jnp.where(middle, 1 + lax.div(m, 10), 4))
        turn = jnp.where(n < PER_Z, n, jnp.where(middle, lax.div(lax.rem(m, 10), 2), n - 35))
        rising = jnp.logical_and(middle, lax.rem(m, 2) == 0)
        home = lax.rem(jnp.where(rising, z - away, z + away) + N_Z, N_Z)
        which = in_order(home, turn, False)
        block = PER_Z * home + which
        odd = more_down(home, which)
        mine = core_of(block) == core
        across = by_y(home, which)
        mine_relay = jnp.logical_and(jnp.logical_and(mine, across), lax.div(which, 3) == my_y)
        mine_ring = jnp.logical_and(mine, jnp.logical_not(across))
        start = n < PER_Z
        falling = jnp.logical_and(middle, jnp.logical_not(rising))
        send_up = jnp.logical_or(start, jnp.logical_and(rising, away < 4 - odd))
        send_down = jnp.logical_or(start, jnp.logical_and(falling, away < 3 + odd))
        return place_of(block), mine_ring, mine_relay, send_up, send_down

    def gather(n, carry):
        place, mine_ring, mine_relay, send_up, send_down = gather_step(n)

        @pl.when(mine_ring)
        def _():
            gather_copy(place, True).wait_recv()

        @pl.when(jnp.logical_and(mine_ring, send_up))
        def _():
            gather_copy(place, True).start()

        @pl.when(jnp.logical_and(mine_ring, send_down))
        def _():
            gather_copy(place, False).start()

        @pl.when(mine_relay)
        def _():
            relay_copy(place, True).wait_recv()

        @pl.when(jnp.logical_and(mine_relay, send_up))
        def _():
            relay_copy(place, True).start()

        @pl.when(jnp.logical_and(mine_relay, send_down))
        def _():
            relay_copy(place, False).start()

        @pl.when(mine_relay)
        def _():
            for half_y in range(2):
                relay_over(place, half_y).start()

        return carry

    lax.fori_loop(0, 40, gather, 0)

    pass_copies = []
    for m in range(MB):
        pick_copies[m].wait_recv()
        pass_copies.append(
            pltpu.make_async_remote_copy(
                src_ref=acts.at[leaves, 2 * core + m],
                dst_ref=acts.at[leaves, 2 * core + m],
                send_sem=pass_send.at[m],
                recv_sem=pass_recv.at[m],
                device_id=(section, sibling),
                device_id_type=MESH,
            )
        )
        pass_copies[m].start()

    def arrive(block, carry):
        across = by_y(lax.div(block, PER_Z), lax.rem(block, PER_Z))

        @pl.when(jnp.logical_and(across, core_of(block) == core))
        def _():
            gather_copy(place_of(block), True).wait_recv()

        return carry

    lax.fori_loop(0, 40, arrive, 0)

    for m in range(MB):
        own_locals[m].wait()
        own_copies[m].wait_recv()
        pass_copies[m].wait_recv()

    def project(n, carry):
        batch, part = lax.div(n, 3), lax.rem(n, 3)
        rows = weights[pl.ds(4 * part, 4)].reshape(4 * CHUNK, width)
        proj[batch, pl.ds(pl.multiple_of(part * 256, 256), 256), :] = nt(rows, acts[0, batch])
        return carry

    lax.fori_loop(0, 12, project, 0)

    def cotangent(n, carry):
        batch, part = lax.div(n, 2), lax.rem(n, 2)
        rows = weights[pl.ds(QKV_BLOCKS + 4 * part, 4)].reshape(4 * CHUNK, width)
        dctx[batch, pl.ds(pl.multiple_of(part * 256, 256), 256), :] = nt(rows, acts[1, batch]).astype(BF16)
        return carry

    lax.fori_loop(0, 8, cotangent, 0)

    cosine, sine = cos_ref[...], sin_ref[...]
    half = HEAD_SIZE // 2

    def rotate(value):
        a, b = value[:half], value[half:]
        return jnp.concatenate([a * cosine - b * sine, b * cosine + a * sine], axis=0)

    def rotate_back(value):
        a, b = value[:half], value[half:]
        return jnp.concatenate([a * cosine + b * sine, b * cosine - a * sine], axis=0)

    def attention(n, carry):
        batch, group = lax.div(n, 2), lax.rem(n, 2)
        key_rows = pl.ds(pl.multiple_of(K_AT + HEAD_SIZE * group, HEAD_SIZE), HEAD_SIZE)
        value_rows = pl.ds(pl.multiple_of(V_AT + HEAD_SIZE * group, HEAD_SIZE), HEAD_SIZE)
        key_t = rotate(proj[batch, key_rows, :])
        value_t = proj[batch, value_rows, :]
        key = key_t.T.astype(BF16)
        value = value_t.T.astype(BF16)
        key_t = key_t.astype(BF16)
        value_t = value_t.astype(BF16)
        kept = lax.broadcasted_iota(jnp.int32, (SEQ, SEQ), 0) <= lax.broadcasted_iota(jnp.int32, (SEQ, SEQ), 1)
        dkey = jnp.zeros((HEAD_SIZE, SEQ), F32)
        dvalue = jnp.zeros((HEAD_SIZE, SEQ), F32)
        for head in range(4):
            first = 256 * group + HEAD_SIZE * head
            rows = pl.ds(pl.multiple_of(first, HEAD_SIZE), HEAD_SIZE)
            query_t = (rotate(proj[batch, rows, :]) * HEAD_SIZE**-0.5).astype(BF16)
            scores = jnp.where(kept, nn(key, query_t), -1e30)
            raised = jnp.exp(scores - jnp.max(scores, axis=0, keepdims=True))
            probs = raised * (1.0 / jnp.sum(raised, axis=0, keepdims=True))
            probs_b = probs.astype(BF16)
            context_rows = pl.ds(pl.multiple_of(O_AT + first, HEAD_SIZE), HEAD_SIZE)
            lhs[batch, context_rows, :] = nn(value_t, probs_b).astype(BF16)
            cot = dctx[batch, rows, :]
            dprobs = nn(value, cot)
            dvalue = dvalue + nt(cot, probs_b)
            delta = jnp.sum(dprobs * probs, axis=0, keepdims=True)
            dscores = (probs * (dprobs - delta)).astype(BF16)
            dquery = nn(key_t, dscores) * HEAD_SIZE**-0.5
            lhs[batch, rows, :] = rotate_back(dquery).astype(BF16)
            dkey = dkey + nt(query_t, dscores)
        lhs[batch, key_rows, :] = rotate_back(dkey).astype(BF16)
        lhs[batch, value_rows, :] = dvalue.astype(BF16)
        return carry

    lax.fori_loop(0, 8, attention, 0)

    def sum_copy(place, going_up):
        landing, arrived = (from_low, low_recv) if going_up else (from_high, high_recv)
        return pltpu.make_async_remote_copy(
            src_ref=stage.at[place],
            dst_ref=landing.at[place],
            send_sem=sum_send.at[place],
            recv_sem=arrived.at[place],
            device_id=(section, up if going_up else down),
            device_id_type=MESH,
        )

    def give_copy(place, which):
        return pltpu.make_async_remote_copy(
            src_ref=stage.at[place],
            dst_ref=given.at[my_y, place],
            send_sem=give_send.at[place],
            recv_sem=give_recv.at[LOCAL * my_y + place],
            device_id=(partner, 4 * z + 2 * lax.div(which, 3) + core),
            device_id_type=MESH,
        )

    def keeper_of(which, quarter):
        inside = CHUNK * which + PIECE * quarter
        keeper = lax.div(inside, SHARD)
        return keeper, lax.div(inside - SHARD * keeper, PIECE)

    def final_copy(which, quarter):
        keeper, piece = keeper_of(which, quarter)
        return pltpu.make_async_remote_copy(
            src_ref=stage.at[place_of(PER_Z * z + which), pl.ds(PIECE * quarter, PIECE)],
            dst_ref=final.at[my_y, pl.ds(pl.multiple_of(PIECE * piece, PIECE), PIECE)],
            send_sem=final_send.at[4 * which + quarter],
            recv_sem=final_recv.at[PIECES * my_y + piece],
            device_id=(partner, 4 * z + keeper),
            device_id_type=MESH,
        )

    def relay_final(which, quarter, local):
        _, piece = keeper_of(which, quarter)
        source = given.at[0, place_of(PER_Z * z + which), pl.ds(PIECE * quarter, PIECE)]
        target = final.at[0, pl.ds(pl.multiple_of(PIECE * piece, PIECE), PIECE)]
        if local:
            return pltpu.make_async_copy(source, target, final_recv.at[piece])
        return pltpu.make_async_remote_copy(
            src_ref=source,
            dst_ref=target,
            send_sem=final_send.at[4 * which + quarter],
            recv_sem=final_recv.at[piece],
            device_id=(section, sibling),
            device_id_type=MESH,
        )

    def relay_sum_copy(place, going_up):
        landing, arrived = (from_low, low_recv) if going_up else (from_high, high_recv)
        return pltpu.make_async_remote_copy(
            src_ref=given.at[0, place],
            dst_ref=landing.at[place],
            send_sem=sum_send.at[place],
            recv_sem=arrived.at[place],
            device_id=(section, up if going_up else down),
            device_id_type=MESH,
        )

    def sum_step(n):
        m = n - PER_Z
        middle = jnp.logical_and(n >= PER_Z, n < 35)
        last = n >= 35
        away = jnp.where(n < PER_Z, 4, jnp.where(middle, 3 - lax.div(m, 10), 0))
        turn = jnp.where(n < PER_Z, n, jnp.where(middle, lax.div(lax.rem(m, 10), 2), n - 35))
        falling = jnp.logical_and(middle, lax.rem(m, 2) == 1)
        home = lax.rem(jnp.where(falling, z - away, z + away) + N_Z, N_Z)
        which = in_order(home, turn, True)
        block = PER_Z * home + which
        odd = more_down(home, which)
        mine = core_of(block) == core
        across = by_y(home, which)
        mine_give = jnp.logical_and(mine, across)
        mine_relay = jnp.logical_and(mine_give, lax.div(which, 3) == my_y)
        mine_ring = jnp.logical_and(mine, jnp.logical_not(across))
        rises = jnp.where(middle, jnp.logical_not(falling), odd == 0)
        has_low = jnp.logical_or(last, jnp.logical_and(rises, away < 4 - odd))
        has_high = jnp.logical_or(last, jnp.logical_and(jnp.logical_not(rises), away < 3 + odd))
        go_up = jnp.logical_and(rises, jnp.logical_not(last))
        go_down = jnp.logical_and(jnp.logical_not(rises), jnp.logical_not(last))
        return place_of(block), which, mine_ring, mine_give, mine_relay, has_low, has_high, go_up, go_down, last

    def block_gradient(place):
        rows = pl.ds(pl.multiple_of(place * CHUNK, CHUNK), CHUNK)
        side = jnp.where(place >= QKV_BLOCKS, 1, 0)
        for tile in range(4):
            columns = slice(tile * width // 4, (tile + 1) * width // 4)
            value = nn(lhs[0, rows, :], acts[side, 0, :, columns])
            for batch in range(1, 2 * MB):
                value = value + nn(lhs[batch, rows, :], acts[side, batch, :, columns])
            total[:, columns] = value

    def give(n):
        place, which, _, mine_give, _, _, _, _, _, _ = sum_step(n)

        @pl.when(mine_give)
        def _():
            block_gradient(place)
            stage[place] = total[...].astype(BF16)
            give_copy(place, which).start()

    def reduce(n):
        place, which, mine_ring, _, mine_relay, has_low, has_high, go_up, go_down, last = sum_step(n)

        @pl.when(mine_ring)
        def _():
            block_gradient(place)

        @pl.when(mine_relay)
        def _():
            for source in range(2):
                pltpu.make_async_remote_copy(
                    src_ref=given.at[source, place],
                    dst_ref=given.at[source, place],
                    send_sem=give_send.at[place],
                    recv_sem=give_recv.at[LOCAL * source + place],
                    device_id=(partner, dp),
                    device_id_type=MESH,
                ).wait_recv()
            total[...] = given[0, place].astype(F32) + given[1, place].astype(F32)

        active = jnp.logical_or(mine_ring, mine_relay)

        @pl.when(jnp.logical_and(active, has_low))
        def _():
            sum_copy(place, True).wait_recv()
            total[...] += from_low[place].astype(F32)

        @pl.when(jnp.logical_and(active, has_high))
        def _():
            sum_copy(place, False).wait_recv()
            total[...] += from_high[place].astype(F32)

        @pl.when(mine_ring)
        def _():
            stage[place] = total[...].astype(BF16)

        @pl.when(mine_relay)
        def _():
            given[0, place] = total[...].astype(BF16)

        for going_up, goes in ((True, go_up), (False, go_down)):

            @pl.when(jnp.logical_and(mine_ring, goes))
            def _(going_up=going_up):
                sum_copy(place, going_up).start()

            @pl.when(jnp.logical_and(mine_relay, goes))
            def _(going_up=going_up):
                relay_sum_copy(place, going_up).start()

        @pl.when(jnp.logical_and(mine_ring, last))
        def _():
            for quarter in range(CHUNK // PIECE):
                final_copy(which, quarter).start()

        for quarter in range(CHUNK // PIECE):
            keeper, _ = keeper_of(which, quarter)
            here = lax.rem(keeper, 2) == core

            @pl.when(jnp.logical_and(jnp.logical_and(mine_relay, last), here))
            def _(quarter=quarter):
                relay_final(which, quarter, True).start()

            @pl.when(jnp.logical_and(jnp.logical_and(mine_relay, last), jnp.logical_not(here)))
            def _(quarter=quarter):
                relay_final(which, quarter, False).start()

    def lead(n, carry):
        give(n)
        return carry

    def both(n, carry):
        @pl.when(n < 40)
        def _():
            give(n)

        reduce(n - LEAD)
        return carry

    lax.fori_loop(0, LEAD, lead, 0)
    lax.fori_loop(LEAD, 40 + LEAD, both, 0)

    for copy in id_copies + pick_copies + own_copies + pass_copies:
        copy.wait_send()
    for piece in range(PIECES):
        across, _, there = piece_way(piece)

        @pl.when(jnp.logical_not(across))
        def _(piece=piece):
            for half_y in range(2):
                first_copy(piece, half_y).wait_send()

        @pl.when(there)
        def _(piece=piece):
            relay_piece(piece, False).wait_send()

    def drain(n, carry):
        place, mine_ring, mine_relay, send_up, send_down = gather_step(n)
        for going_up, goes in ((True, send_up), (False, send_down)):

            @pl.when(jnp.logical_and(mine_ring, goes))
            def _(going_up=going_up):
                gather_copy(place, going_up).wait_send()

            @pl.when(jnp.logical_and(mine_relay, goes))
            def _(going_up=going_up):
                relay_copy(place, going_up).wait_send()

        @pl.when(mine_relay)
        def _():
            for half_y in range(2):
                relay_over(place, half_y).wait_send()

        place, which, mine_ring, mine_give, mine_relay, _, _, _, _, last = sum_step(n)
        active = jnp.logical_or(mine_ring, mine_relay)

        @pl.when(jnp.logical_and(active, jnp.logical_not(last)))
        def _():
            sum_copy(place, True).wait_send()

        @pl.when(mine_give)
        def _():
            give_copy(place, which).wait_send()

        for quarter in range(CHUNK // PIECE):
            keeper, _ = keeper_of(which, quarter)
            away_core = lax.rem(keeper, 2) != core
            sent_on = jnp.logical_or(mine_ring, jnp.logical_and(mine_relay, away_core))

            @pl.when(jnp.logical_and(last, sent_on))
            def _(quarter=quarter):
                final_copy(which, quarter).wait_send()

        return carry

    lax.fori_loop(0, 40, drain, 0)

    def final_wait(piece, source):
        rows = pl.ds(PIECE * piece, PIECE)
        pltpu.make_async_remote_copy(
            src_ref=final.at[source, rows],
            dst_ref=final.at[source, rows],
            send_sem=final_send.at[0],
            recv_sem=final_recv.at[PIECES * source + piece],
            device_id=(section, sibling),
            device_id_type=MESH,
        ).wait_recv()

    for piece in range(PIECES):
        rows = pl.ds(PIECE * piece, PIECE)
        across, _, _ = piece_way(piece)
        final_wait(piece, 0)
        grad_ref[rows, :] = final[0, rows, :].astype(F32)

        @pl.when(jnp.logical_not(across))
        def _(piece=piece, rows=rows):
            final_wait(piece, 1)
            grad_ref[rows, :] += final[1, rows, :].astype(F32)


def summed_gradient(params, sent, back, ids):
    width = params.shape[-1]
    frequency = rope_base ** (-np.arange(HEAD_SIZE // 2, dtype=np.float64) * 2.0 / HEAD_SIZE)
    angles = frequency[:, None] * np.arange(SEQ, dtype=np.float64)[None, :]
    cosine = jnp.asarray(np.cos(angles), F32)
    sine = jnp.asarray(np.sin(angles), F32)
    wide_ids = jnp.broadcast_to(ids.reshape(MB, 1), (MB, 128))
    wide_ids = jnp.concatenate([wide_ids, jnp.zeros((8 - MB, 128), jnp.int32)], axis=0)
    dma = pltpu.SemaphoreType.DMA
    in_vmem = pl.BlockSpec(memory_space=pltpu.VMEM)
    anywhere = pl.BlockSpec(memory_space=pl.ANY)
    return pl.pallas_call(
        kernel,
        out_shape=jax.ShapeDtypeStruct((SHARD, width), F32),
        in_specs=[anywhere, anywhere, anywhere, in_vmem, in_vmem, in_vmem],
        out_specs=in_vmem,
        scratch_shapes=[
            pltpu.VMEM((SHARD, width), BF16),
            pltpu.VMEM((LOG, SEQ, width), BF16),
            pltpu.VMEM((LOG, SEQ, width), BF16),
            pltpu.VMEM((8, 128), jnp.int32),
            pltpu.VMEM((8, 128), jnp.int32),
            pltpu.SMEM((8, 128), jnp.int32),
            pltpu.SMEM((8, 128), jnp.int32),
            pltpu.VMEM((LOCAL, CHUNK, width), BF16),
            pltpu.VMEM((LOCAL, CHUNK, width), BF16),
            pltpu.VMEM((2, 2 * MB, SEQ, width), BF16),
            pltpu.VMEM((2, MB, SEQ, width), BF16),
            pltpu.VMEM((2 * MB, O_AT, SEQ), F32),
            pltpu.VMEM((2 * MB, Q_ROWS, SEQ), BF16),
            pltpu.VMEM((2 * MB, LOCAL * CHUNK, SEQ), BF16),
            pltpu.VMEM((CHUNK, width), F32),
            pltpu.VMEM((LOCAL, CHUNK, width), BF16),
            pltpu.VMEM((2, LOCAL, CHUNK, width), BF16),
            pltpu.VMEM((LOCAL, CHUNK, width), BF16),
            pltpu.VMEM((LOCAL, CHUNK, width), BF16),
            pltpu.VMEM((2, SHARD, width), BF16),
            dma((3,)),
            dma((2,)),
            dma((2,)),
            dma((2,)),
            dma((2 * PIECES,)),
            dma((LOCAL,)),
            dma((LOCAL,)),
            dma((LOCAL,)),
            dma((LOCAL,)),
            dma((LOCAL,)),
            dma((2 * LOCAL,)),
            dma((LOCAL,)),
            dma((MB,)),
            dma((MB,)),
            dma((MB,)),
            dma((MB,)),
            dma((MB,)),
            dma((MB,)),
            dma((MB,)),
            dma((LOCAL,)),
            dma((LOCAL,)),
            dma((LOCAL,)),
            dma((LOCAL,)),
            dma((2 * LOCAL,)),
            dma((4 * PER_Z,)),
            dma((2 * PIECES,)),
        ],
        compiler_params=pltpu.CompilerParams(
            collective_id=0, has_side_effects=True, vmem_limit_bytes=60 * 1024 * 1024
        ),
    )(params, sent, back, wide_ids, cosine, sine)


def apply_adam(weights, first_moment, second_moment, gradient):
    first_new = 0.9 * first_moment + 0.1 * gradient
    second_new = 0.999 * second_moment + 0.001 * gradient * gradient
    fix_first = 1.0 - 0.9**STEP
    fix_second = 1.0 - 0.999**STEP
    update = first_new / fix_first / (jnp.sqrt(second_new / fix_second) + 1e-08)
    current = weights.astype(F32)
    renewed = (current - learn_rate * (update + decay_rate * current)).astype(BF16)
    return (renewed, first_new, second_new)


def shards(params, moment_one, moment_two, sent_rows, back_rows, slot_ids):
    summed = summed_gradient(params[0], sent_rows[0, 0], back_rows[0, 0], slot_ids[0, 0])
    renewed, first_new, second_new = apply_adam(params[0], moment_one[0], moment_two[0], summed / N_DP)
    return (renewed[None], first_new[None], second_new[None])


def solution(mesh):
    in_specs = (
        P("section", "dp", None),
        P("section", "dp", None),
        P("section", "dp", None),
        P("section", "dp", None, None, None),
        P("section", "dp", None, None, None),
        P("section", "dp", None),
    )
    out_specs = (P("section", "dp", None), P("section", "dp", None), P("section", "dp", None))
    return jax.shard_map(shards, mesh=mesh, in_specs=in_specs, out_specs=out_specs, check_vma=False)
```

```python
import jax
import jax.numpy as jnp
import numpy as np
from jax import lax
from jax.experimental import pallas as pl
from jax.experimental.pallas import tpu as pltpu
from jax.sharding import PartitionSpec as P

HEAD_SIZE = 64
QUERY_HEADS = 16
KEY_VALUE_HEADS = 4
STEP = 100
SEQ = 192
LOG = 4
MB = 2
PROWS = 2560

N_SECTION = 8
N_DP = 32
N_Z = 8
CHUNK = 64
PER_Z = 5
LOCAL = 20
SHARD = 80
LEAD = 12
STACK = 4
PIECE = 16
PIECES = SHARD // PIECE
Q_ROWS = 512
K_AT = 512
V_AT = 640
O_AT = 768
QKV_BLOCKS = 12

rope_base = 500000.0
learn_rate = 0.0003
decay_rate = 0.1

MESH = pl.DeviceIdType.MESH
BF16 = jnp.bfloat16
F32 = jnp.float32


def nn(a, b):
    return lax.dot_general(a, b, (((1,), (0,)), ((), ())), preferred_element_type=F32)


def nt(a, b):
    return lax.dot_general(a, b, (((1,), (1,)), ((), ())), preferred_element_type=F32)


def core_of(block):
    return jnp.where(
        block < 16,
        lax.div(block, 8),
        jnp.where(block < 24, lax.rem(lax.div(block - 16, 2), 2), lax.div(block - 24, 8)),
    )


def place_of(block):
    return jnp.where(
        block < 16,
        lax.rem(block, 8),
        jnp.where(
            block < 24,
            8 + 2 * lax.div(block - 16, 4) + lax.rem(block - 16, 2),
            12 + lax.rem(block - 24, 8),
        ),
    )


def by_y(home, which):
    even = lax.rem(home, 2) == 0
    stays = jnp.logical_or(which == 2, which == jnp.where(even, 0, 4))
    return jnp.logical_not(stays)


def in_order(home, turn, ring_first):
    even = lax.rem(home, 2) == 0
    turn = jnp.where(ring_first, lax.rem(turn + 3, PER_Z), turn)
    of_even = jnp.where(turn < 2, 2 * turn + 1, jnp.where(turn == 2, 4, 2 * turn - 6))
    of_odd = jnp.where(turn < 2, turn, jnp.where(turn == 2, 3, 2 * turn - 4))
    return jnp.where(even, of_even, of_odd)


def more_down(home, which):
    even = lax.rem(home, 2) == 0
    lone = which == jnp.where(even, 1, 3)
    second = jnp.logical_or(which == 4, which == jnp.where(even, 2, 1))
    return jnp.where(lone, lax.rem(lax.div(home, 2), 2), jnp.where(second, 1, 0))


def kernel(
    params_hbm,
    sent_hbm,
    back_hbm,
    ids_ref,
    cos_ref,
    sin_ref,
    grad_ref,
    shard,
    sent,
    back,
    ids_next,
    ids_prev,
    ids_one,
    ids_two,
    weights,
    relay,
    acts,
    picked,
    proj,
    dctx,
    lhs,
    total,
    stage,
    given,
    from_low,
    from_high,
    final,
    sem_local,
    sem_ids,
    sem_ids_send,
    sem_ids_recv,
    first_send,
    gather_up,
    gather_down,
    gather_recv,
    relay_up,
    relay_down,
    relay_out,
    relay_recv,
    own_local,
    own_send,
    own_recv,
    pick_send,
    pick_recv,
    pass_send,
    pass_recv,
    sum_send,
    low_recv,
    high_recv,
    give_send,
    give_recv,
    final_send,
    final_recv,
):
    section = lax.axis_index("section")
    dp = lax.axis_index("dp")
    z = lax.div(dp, 4)
    core = lax.rem(dp, 2)
    my_y = lax.rem(lax.div(dp, 2), 2)
    odd_section = lax.rem(section, 2)
    partner = section + 1 - 2 * odd_section
    sibling = dp + 1 - 2 * core
    up = lax.rem(dp + 4, N_DP)
    down = lax.rem(dp + N_DP - 4, N_DP)
    before = lax.rem(section + N_SECTION - 1, N_SECTION)
    after = lax.rem(section + 1, N_SECTION)
    before_two = lax.rem(section + N_SECTION - 2, N_SECTION)
    after_two = lax.rem(section + 2, N_SECTION)
    width = weights.shape[2]

    loads = [
        pltpu.make_async_copy(params_hbm, shard, sem_local.at[0]),
        pltpu.make_async_copy(sent_hbm, sent, sem_local.at[1]),
        pltpu.make_async_copy(back_hbm, back, sem_local.at[2]),
    ]
    for load in loads:
        load.start()

    barrier = pltpu.get_barrier_semaphore()
    beyond = jnp.where(odd_section == 0, before, after)
    peers = [(section, sibling), (section, up), (section, down), (before_two, dp), (after_two, dp), (beyond, dp)]
    for quarter in range(4):
        peers.append((partner, 4 * z + quarter))
    for peer in peers:
        pl.semaphore_signal(barrier, inc=1, device_id=peer, device_id_type=MESH)
    pl.semaphore_wait(barrier, len(peers))

    id_copies = [
        pltpu.make_async_remote_copy(
            src_ref=ids_ref,
            dst_ref=ids_next,
            send_sem=sem_ids_send.at[0],
            recv_sem=sem_ids_recv.at[0],
            device_id=(before, dp),
            device_id_type=MESH,
        ),
        pltpu.make_async_remote_copy(
            src_ref=ids_ref,
            dst_ref=ids_prev,
            send_sem=sem_ids_send.at[1],
            recv_sem=sem_ids_recv.at[1],
            device_id=(after, dp),
            device_id_type=MESH,
        ),
    ]
    for copy in id_copies:
        copy.start()

    loads[0].wait()

    def first_copy(piece, half):
        row = SHARD * dp + PIECE * piece
        block = lax.div(row, CHUNK)
        return pltpu.make_async_remote_copy(
            src_ref=shard.at[pl.ds(PIECE * piece, PIECE)],
            dst_ref=weights.at[place_of(block), pl.ds(pl.multiple_of(lax.rem(row, CHUNK), PIECE), PIECE)],
            send_sem=first_send.at[2 * piece + half],
            recv_sem=gather_recv.at[place_of(block)],
            device_id=(partner, 4 * z + 2 * half + core_of(block)),
            device_id_type=MESH,
        )

    def relay_piece(piece, local):
        row = SHARD * dp + PIECE * piece
        block = lax.div(row, CHUNK)
        source = shard.at[pl.ds(PIECE * piece, PIECE)]
        target = relay.at[place_of(block), pl.ds(pl.multiple_of(lax.rem(row, CHUNK), PIECE), PIECE)]
        arrived = relay_recv.at[place_of(block)]
        if local:
            return pltpu.make_async_copy(source, target, arrived)
        return pltpu.make_async_remote_copy(
            src_ref=source,
            dst_ref=target,
            send_sem=first_send.at[2 * piece],
            recv_sem=arrived,
            device_id=(section, sibling),
            device_id_type=MESH,
        )

    def piece_way(piece):
        block = lax.div(SHARD * dp + PIECE * piece, CHUNK)
        across = by_y(z, block - PER_Z * z)
        here = core_of(block) == core
        return across, jnp.logical_and(across, here), jnp.logical_and(across, jnp.logical_not(here))

    for piece in range(PIECES):
        across, here, there = piece_way(piece)

        @pl.when(jnp.logical_not(across))
        def _(piece=piece):
            for half in range(2):
                first_copy(piece, half).start()

        @pl.when(here)
        def _(piece=piece):
            relay_piece(piece, True).start()

        @pl.when(there)
        def _(piece=piece):
            relay_piece(piece, False).start()

    def gather_copy(place, going_up):
        return pltpu.make_async_remote_copy(
            src_ref=weights.at[place],
            dst_ref=weights.at[place],
            send_sem=(gather_up if going_up else gather_down).at[place],
            recv_sem=gather_recv.at[place],
            device_id=(section, up if going_up else down),
            device_id_type=MESH,
        )

    def relay_copy(place, going_up):
        return pltpu.make_async_remote_copy(
            src_ref=relay.at[place],
            dst_ref=relay.at[place],
            send_sem=(relay_up if going_up else relay_down).at[place],
            recv_sem=relay_recv.at[place],
            device_id=(section, up if going_up else down),
            device_id_type=MESH,
        )

    def relay_over(place, half):
        return pltpu.make_async_remote_copy(
            src_ref=relay.at[place],
            dst_ref=weights.at[place],
            send_sem=relay_out.at[LOCAL * half + place],
            recv_sem=gather_recv.at[place],
            device_id=(partner, 4 * z + 2 * half + core),
            device_id_type=MESH,
        )

    def gather_step(n):
        m = n - PER_Z
        middle = jnp.logical_and(n >= PER_Z, n < 35)
        away = jnp.where(n < PER_Z, 0, jnp.where(middle, 1 + lax.div(m, 10), 4))
        turn = jnp.where(n < PER_Z, n, jnp.where(middle, lax.div(lax.rem(m, 10), 2), n - 35))
        rising = jnp.logical_and(middle, lax.rem(m, 2) == 0)
        home = lax.rem(jnp.where(rising, z - away, z + away) + N_Z, N_Z)
        which = in_order(home, turn, False)
        block = PER_Z * home + which
        odd = more_down(home, which)
        mine = core_of(block) == core
        across = by_y(home, which)
        mine_relay = jnp.logical_and(jnp.logical_and(mine, across), lax.div(which, 3) == my_y)
        mine_ring = jnp.logical_and(mine, jnp.logical_not(across))
        start = n < PER_Z
        falling = jnp.logical_and(middle, jnp.logical_not(rising))
        send_up = jnp.logical_or(start, jnp.logical_and(rising, away < 4 - odd))
        send_down = jnp.logical_or(start, jnp.logical_and(falling, away < 3 + odd))
        return place_of(block), mine_ring, mine_relay, send_up, send_down

    def gather(n, carry):
        place, mine_ring, mine_relay, send_up, send_down = gather_step(n)

        @pl.when(mine_ring)
        def _():
            gather_copy(place, True).wait_recv()

        @pl.when(jnp.logical_and(mine_ring, send_up))
        def _():
            gather_copy(place, True).start()

        @pl.when(jnp.logical_and(mine_ring, send_down))
        def _():
            gather_copy(place, False).start()

        @pl.when(mine_relay)
        def _():
            relay_copy(place, True).wait_recv()

        @pl.when(jnp.logical_and(mine_relay, send_up))
        def _():
            relay_copy(place, True).start()

        @pl.when(jnp.logical_and(mine_relay, send_down))
        def _():
            relay_copy(place, False).start()

        @pl.when(mine_relay)
        def _():
            for half_y in range(2):
                relay_over(place, half_y).start()

        return carry

    lax.fori_loop(0, 3, gather, 0)

    stays, leaves = odd_section, 1 - odd_section
    target_section = jnp.where(odd_section == 0, before_two, after_two)
    id_copies[0].wait_recv()
    to_one = pltpu.make_async_copy(ids_next, ids_one, sem_ids.at[0])
    to_one.start()
    to_one.wait()
    id_copies[1].wait_recv()
    to_two = pltpu.make_async_copy(ids_prev, ids_two, sem_ids.at[1])
    to_two.start()
    to_two.wait()
    loads[1].wait()
    loads[2].wait()
    own_copies = []
    own_locals = []
    pick_copies = []
    for m in range(MB):
        wanted_one, wanted_two = ids_one[m, 0], ids_two[m, 0]

        def pick_rows(n, carry, m=m, wanted_one=wanted_one, wanted_two=wanted_two):
            rows = pl.ds(pl.multiple_of(n * 16, 16), 16)
            value = sent[wanted_one, rows, :].astype(F32)
            scaling = lax.rsqrt(jnp.mean(value * value, axis=-1, keepdims=True) + 1e-05)
            picked[0, m, rows, :] = (value * scaling).astype(BF16)
            picked[1, m, rows, :] = back[wanted_two, rows, :]
            return carry

        lax.fori_loop(0, SEQ // 16, pick_rows, 0)
        pick_copies.append(
            pltpu.make_async_remote_copy(
                src_ref=picked.at[leaves, m],
                dst_ref=acts.at[leaves, 2 * core + m],
                send_sem=pick_send.at[m],
                recv_sem=pick_recv.at[m],
                device_id=(target_section, dp),
                device_id_type=MESH,
            )
        )
        own_copies.append(
            pltpu.make_async_remote_copy(
                src_ref=picked.at[stays, m],
                dst_ref=acts.at[stays, 2 * core + m],
                send_sem=own_send.at[m],
                recv_sem=own_recv.at[m],
                device_id=(section, sibling),
                device_id_type=MESH,
            )
        )
        own_locals.append(
            pltpu.make_async_copy(picked.at[stays, m], acts.at[stays, 2 * core + m], own_local.at[m])
        )
        pick_copies[m].start()
        own_copies[m].start()
        own_locals[m].start()

    lax.fori_loop(3, 40, gather, 0)

    pass_copies = []
    for m in range(MB):
        pick_copies[m].wait_recv()
        pass_copies.append(
            pltpu.make_async_remote_copy(
                src_ref=acts.at[leaves, 2 * core + m],
                dst_ref=acts.at[leaves, 2 * core + m],
                send_sem=pass_send.at[m],
                recv_sem=pass_recv.at[m],
                device_id=(section, sibling),
                device_id_type=MESH,
            )
        )
        pass_copies[m].start()

    def arrive(block, carry):
        across = by_y(lax.div(block, PER_Z), lax.rem(block, PER_Z))

        @pl.when(jnp.logical_and(across, core_of(block) == core))
        def _():
            gather_copy(place_of(block), True).wait_recv()

        return carry

    lax.fori_loop(0, 40, arrive, 0)

    for m in range(MB):
        own_locals[m].wait()
        own_copies[m].wait_recv()
        pass_copies[m].wait_recv()

    def project(batch, carry):
        rows = weights[:QKV_BLOCKS].reshape(O_AT, width)
        proj[batch] = nt(rows, acts[0, batch])
        return carry

    lax.fori_loop(0, 2 * MB, project, 0)

    def cotangent(batch, carry):
        rows = weights[QKV_BLOCKS:].reshape(Q_ROWS, width)
        dctx[batch] = nt(rows, acts[1, batch]).astype(BF16)
        return carry

    lax.fori_loop(0, 2 * MB, cotangent, 0)

    cosine, sine = cos_ref[...], sin_ref[...]
    half = HEAD_SIZE // 2

    def rotate(value):
        a, b = value[:half], value[half:]
        return jnp.concatenate([a * cosine - b * sine, b * cosine + a * sine], axis=0)

    def rotate_back(value):
        a, b = value[:half], value[half:]
        return jnp.concatenate([a * cosine + b * sine, b * cosine - a * sine], axis=0)

    def attention(n, carry):
        batch, group = lax.div(n, 2), lax.rem(n, 2)
        key_rows = pl.ds(pl.multiple_of(K_AT + HEAD_SIZE * group, HEAD_SIZE), HEAD_SIZE)
        value_rows = pl.ds(pl.multiple_of(V_AT + HEAD_SIZE * group, HEAD_SIZE), HEAD_SIZE)
        key_t = rotate(proj[batch, key_rows, :])
        value_t = proj[batch, value_rows, :]
        key = key_t.T.astype(BF16)
        value = value_t.T.astype(BF16)
        key_t = key_t.astype(BF16)
        value_t = value_t.astype(BF16)
        ones = jnp.ones((16, SEQ), BF16)
        value_ones = jnp.concatenate([value_t, ones], axis=0)
        kept = lax.broadcasted_iota(jnp.int32, (SEQ, SEQ), 0) <= lax.broadcasted_iota(jnp.int32, (SEQ, SEQ), 1)
        kept = jnp.concatenate([kept.astype(jnp.int32)] * STACK, axis=1) > 0
        dkey = jnp.zeros((HEAD_SIZE, SEQ), F32)
        dvalue = jnp.zeros((HEAD_SIZE, SEQ), F32)
        for stack in range(4 // STACK):
            firsts = [256 * group + HEAD_SIZE * (STACK * stack + head) for head in range(STACK)]
            rows = [pl.ds(pl.multiple_of(first, HEAD_SIZE), HEAD_SIZE) for first in firsts]
            query_t = [(rotate(proj[batch, row, :]) * HEAD_SIZE**-0.5) for row in rows]
            query_t = jnp.concatenate(query_t, axis=1).astype(BF16)
            scores = jnp.where(kept, nn(key, query_t), -1e30)
            raised = jnp.exp(scores - jnp.max(scores, axis=0, keepdims=True))
            raised_b = raised.astype(BF16)
            context = nn(value_ones, raised_b)
            inverse = 1.0 / context[HEAD_SIZE : HEAD_SIZE + 1]
            context = context[:HEAD_SIZE] * inverse
            cot = jnp.concatenate([dctx[batch, row, :].astype(F32) for row in rows], axis=1)
            delta = jnp.sum(cot * context, axis=0, keepdims=True) * inverse
            cot = (cot * inverse).astype(BF16)
            dscores = (raised * (nn(value, cot) - delta)).astype(BF16)
            dvalue = dvalue + nt(cot, raised_b)
            dquery = nn(key_t, dscores) * HEAD_SIZE**-0.5
            dkey = dkey + nt(query_t, dscores)
            for head in range(STACK):
                lanes = slice(SEQ * head, SEQ * (head + 1))
                context_rows = pl.ds(pl.multiple_of(O_AT + firsts[head], HEAD_SIZE), HEAD_SIZE)
                lhs[batch, context_rows, :] = context[:, lanes].astype(BF16)
                lhs[batch, rows[head], :] = rotate_back(dquery[:, lanes]).astype(BF16)
        lhs[batch, key_rows, :] = rotate_back(dkey).astype(BF16)
        lhs[batch, value_rows, :] = dvalue.astype(BF16)
        return carry

    lax.fori_loop(0, 8, attention, 0)

    def sum_copy(place, going_up):
        landing, arrived = (from_low, low_recv) if going_up else (from_high, high_recv)
        return pltpu.make_async_remote_copy(
            src_ref=stage.at[place],
            dst_ref=landing.at[place],
            send_sem=sum_send.at[place],
            recv_sem=arrived.at[place],
            device_id=(section, up if going_up else down),
            device_id_type=MESH,
        )

    def give_copy(place, which):
        return pltpu.make_async_remote_copy(
            src_ref=stage.at[place],
            dst_ref=given.at[my_y, place],
            send_sem=give_send.at[place],
            recv_sem=give_recv.at[LOCAL * my_y + place],
            device_id=(partner, 4 * z + 2 * lax.div(which, 3) + core),
            device_id_type=MESH,
        )

    def keeper_of(which, quarter):
        inside = CHUNK * which + PIECE * quarter
        keeper = lax.div(inside, SHARD)
        return keeper, lax.div(inside - SHARD * keeper, PIECE)

    def final_copy(which, quarter):
        keeper, piece = keeper_of(which, quarter)
        return pltpu.make_async_remote_copy(
            src_ref=stage.at[place_of(PER_Z * z + which), pl.ds(PIECE * quarter, PIECE)],
            dst_ref=final.at[my_y, pl.ds(pl.multiple_of(PIECE * piece, PIECE), PIECE)],
            send_sem=final_send.at[4 * which + quarter],
            recv_sem=final_recv.at[PIECES * my_y + piece],
            device_id=(partner, 4 * z + keeper),
            device_id_type=MESH,
        )

    def relay_final(which, quarter, local):
        _, piece = keeper_of(which, quarter)
        source = given.at[0, place_of(PER_Z * z + which), pl.ds(PIECE * quarter, PIECE)]
        target = final.at[0, pl.ds(pl.multiple_of(PIECE * piece, PIECE), PIECE)]
        if local:
            return pltpu.make_async_copy(source, target, final_recv.at[piece])
        return pltpu.make_async_remote_copy(
            src_ref=source,
            dst_ref=target,
            send_sem=final_send.at[4 * which + quarter],
            recv_sem=final_recv.at[piece],
            device_id=(section, sibling),
            device_id_type=MESH,
        )

    def relay_sum_copy(place, going_up):
        landing, arrived = (from_low, low_recv) if going_up else (from_high, high_recv)
        return pltpu.make_async_remote_copy(
            src_ref=given.at[0, place],
            dst_ref=landing.at[place],
            send_sem=sum_send.at[place],
            recv_sem=arrived.at[place],
            device_id=(section, up if going_up else down),
            device_id_type=MESH,
        )

    def sum_step(n):
        m = n - PER_Z
        middle = jnp.logical_and(n >= PER_Z, n < 35)
        last = n >= 35
        away = jnp.where(n < PER_Z, 4, jnp.where(middle, 3 - lax.div(m, 10), 0))
        turn = jnp.where(n < PER_Z, n, jnp.where(middle, lax.div(lax.rem(m, 10), 2), n - 35))
        falling = jnp.logical_and(middle, lax.rem(m, 2) == 1)
        home = lax.rem(jnp.where(falling, z - away, z + away) + N_Z, N_Z)
        which = in_order(home, turn, True)
        block = PER_Z * home + which
        odd = more_down(home, which)
        mine = core_of(block) == core
        across = by_y(home, which)
        mine_give = jnp.logical_and(mine, across)
        mine_relay = jnp.logical_and(mine_give, lax.div(which, 3) == my_y)
        mine_ring = jnp.logical_and(mine, jnp.logical_not(across))
        rises = jnp.where(middle, jnp.logical_not(falling), odd == 0)
        has_low = jnp.logical_or(last, jnp.logical_and(rises, away < 4 - odd))
        has_high = jnp.logical_or(last, jnp.logical_and(jnp.logical_not(rises), away < 3 + odd))
        go_up = jnp.logical_and(rises, jnp.logical_not(last))
        go_down = jnp.logical_and(jnp.logical_not(rises), jnp.logical_not(last))
        return place_of(block), which, mine_ring, mine_give, mine_relay, has_low, has_high, go_up, go_down, last

    def block_gradient(place):
        rows = pl.ds(pl.multiple_of(place * CHUNK, CHUNK), CHUNK)
        side = jnp.where(place >= QKV_BLOCKS, 1, 0)
        for tile in range(4):
            columns = slice(tile * width // 4, (tile + 1) * width // 4)
            value = nn(lhs[0, rows, :], acts[side, 0, :, columns])
            for batch in range(1, 2 * MB):
                value = value + nn(lhs[batch, rows, :], acts[side, batch, :, columns])
            total[:, columns] = value

    def give(n):
        place, which, _, mine_give, _, _, _, _, _, _ = sum_step(n)

        @pl.when(mine_give)
        def _():
            block_gradient(place)
            stage[place] = total[...].astype(BF16)
            give_copy(place, which).start()

    def reduce(n):
        place, which, mine_ring, _, mine_relay, has_low, has_high, go_up, go_down, last = sum_step(n)

        @pl.when(mine_ring)
        def _():
            block_gradient(place)

        @pl.when(mine_relay)
        def _():
            for source in range(2):
                pltpu.make_async_remote_copy(
                    src_ref=given.at[source, place],
                    dst_ref=given.at[source, place],
                    send_sem=give_send.at[place],
                    recv_sem=give_recv.at[LOCAL * source + place],
                    device_id=(partner, dp),
                    device_id_type=MESH,
                ).wait_recv()
            total[...] = given[0, place].astype(F32) + given[1, place].astype(F32)

        active = jnp.logical_or(mine_ring, mine_relay)

        @pl.when(jnp.logical_and(active, has_low))
        def _():
            sum_copy(place, True).wait_recv()
            total[...] += from_low[place].astype(F32)

        @pl.when(jnp.logical_and(active, has_high))
        def _():
            sum_copy(place, False).wait_recv()
            total[...] += from_high[place].astype(F32)

        @pl.when(mine_ring)
        def _():
            stage[place] = total[...].astype(BF16)

        @pl.when(mine_relay)
        def _():
            given[0, place] = total[...].astype(BF16)

        for going_up, goes in ((True, go_up), (False, go_down)):

            @pl.when(jnp.logical_and(mine_ring, goes))
            def _(going_up=going_up):
                sum_copy(place, going_up).start()

            @pl.when(jnp.logical_and(mine_relay, goes))
            def _(going_up=going_up):
                relay_sum_copy(place, going_up).start()

        @pl.when(jnp.logical_and(mine_ring, last))
        def _():
            for quarter in range(CHUNK // PIECE):
                final_copy(which, quarter).start()

        for quarter in range(CHUNK // PIECE):
            keeper, _ = keeper_of(which, quarter)
            here = lax.rem(keeper, 2) == core

            @pl.when(jnp.logical_and(jnp.logical_and(mine_relay, last), here))
            def _(quarter=quarter):
                relay_final(which, quarter, True).start()

            @pl.when(jnp.logical_and(jnp.logical_and(mine_relay, last), jnp.logical_not(here)))
            def _(quarter=quarter):
                relay_final(which, quarter, False).start()

    def lead(n, carry):
        give(n)
        return carry

    def both(n, carry):
        @pl.when(n < 40)
        def _():
            give(n)

        reduce(n - LEAD)
        return carry

    lax.fori_loop(0, LEAD, lead, 0)
    lax.fori_loop(LEAD, 40 + LEAD, both, 0)

    for copy in id_copies + pick_copies + own_copies + pass_copies:
        copy.wait_send()
    for piece in range(PIECES):
        across, _, there = piece_way(piece)

        @pl.when(jnp.logical_not(across))
        def _(piece=piece):
            for half_y in range(2):
                first_copy(piece, half_y).wait_send()

        @pl.when(there)
        def _(piece=piece):
            relay_piece(piece, False).wait_send()

    def drain(n, carry):
        place, mine_ring, mine_relay, send_up, send_down = gather_step(n)
        for going_up, goes in ((True, send_up), (False, send_down)):

            @pl.when(jnp.logical_and(mine_ring, goes))
            def _(going_up=going_up):
                gather_copy(place, going_up).wait_send()

            @pl.when(jnp.logical_and(mine_relay, goes))
            def _(going_up=going_up):
                relay_copy(place, going_up).wait_send()

        @pl.when(mine_relay)
        def _():
            for half_y in range(2):
                relay_over(place, half_y).wait_send()

        place, which, mine_ring, mine_give, mine_relay, _, _, _, _, last = sum_step(n)
        active = jnp.logical_or(mine_ring, mine_relay)

        @pl.when(jnp.logical_and(active, jnp.logical_not(last)))
        def _():
            sum_copy(place, True).wait_send()

        @pl.when(mine_give)
        def _():
            give_copy(place, which).wait_send()

        for quarter in range(CHUNK // PIECE):
            keeper, _ = keeper_of(which, quarter)
            away_core = lax.rem(keeper, 2) != core
            sent_on = jnp.logical_or(mine_ring, jnp.logical_and(mine_relay, away_core))

            @pl.when(jnp.logical_and(last, sent_on))
            def _(quarter=quarter):
                final_copy(which, quarter).wait_send()

        return carry

    lax.fori_loop(0, 40, drain, 0)

    def final_wait(piece, source):
        rows = pl.ds(PIECE * piece, PIECE)
        pltpu.make_async_remote_copy(
            src_ref=final.at[source, rows],
            dst_ref=final.at[source, rows],
            send_sem=final_send.at[0],
            recv_sem=final_recv.at[PIECES * source + piece],
            device_id=(section, sibling),
            device_id_type=MESH,
        ).wait_recv()

    for piece in range(PIECES):
        rows = pl.ds(PIECE * piece, PIECE)
        across, _, _ = piece_way(piece)
        final_wait(piece, 0)
        grad_ref[rows, :] = final[0, rows, :].astype(F32)

        @pl.when(jnp.logical_not(across))
        def _(piece=piece, rows=rows):
            final_wait(piece, 1)
            grad_ref[rows, :] += final[1, rows, :].astype(F32)


def summed_gradient(params, sent, back, ids):
    width = params.shape[-1]
    frequency = rope_base ** (-np.arange(HEAD_SIZE // 2, dtype=np.float64) * 2.0 / HEAD_SIZE)
    angles = frequency[:, None] * np.arange(SEQ, dtype=np.float64)[None, :]
    cosine = jnp.asarray(np.cos(angles), F32)
    sine = jnp.asarray(np.sin(angles), F32)
    wide_ids = jnp.broadcast_to(ids.reshape(1, MB, 1), (4, MB, 128)).reshape(8, 128)
    dma = pltpu.SemaphoreType.DMA
    in_vmem = pl.BlockSpec(memory_space=pltpu.VMEM)
    anywhere = pl.BlockSpec(memory_space=pl.ANY)
    return pl.pallas_call(
        kernel,
        out_shape=jax.ShapeDtypeStruct((SHARD, width), F32),
        in_specs=[anywhere, anywhere, anywhere, in_vmem, in_vmem, in_vmem],
        out_specs=in_vmem,
        scratch_shapes=[
            pltpu.VMEM((SHARD, width), BF16),
            pltpu.VMEM((LOG, SEQ, width), BF16),
            pltpu.VMEM((LOG, SEQ, width), BF16),
            pltpu.VMEM((8, 128), jnp.int32),
            pltpu.VMEM((8, 128), jnp.int32),
            pltpu.SMEM((8, 128), jnp.int32),
            pltpu.SMEM((8, 128), jnp.int32),
            pltpu.VMEM((LOCAL, CHUNK, width), BF16),
            pltpu.VMEM((LOCAL, CHUNK, width), BF16),
            pltpu.VMEM((2, 2 * MB, SEQ, width), BF16),
            pltpu.VMEM((2, MB, SEQ, width), BF16),
            pltpu.VMEM((2 * MB, O_AT, SEQ), F32),
            pltpu.VMEM((2 * MB, Q_ROWS, SEQ), BF16),
            pltpu.VMEM((2 * MB, LOCAL * CHUNK, SEQ), BF16),
            pltpu.VMEM((CHUNK, width), F32),
            pltpu.VMEM((LOCAL, CHUNK, width), BF16),
            pltpu.VMEM((2, LOCAL, CHUNK, width), BF16),
            pltpu.VMEM((LOCAL, CHUNK, width), BF16),
            pltpu.VMEM((LOCAL, CHUNK, width), BF16),
            pltpu.VMEM((2, SHARD, width), BF16),
            dma((3,)),
            dma((2,)),
            dma((2,)),
            dma((2,)),
            dma((2 * PIECES,)),
            dma((LOCAL,)),
            dma((LOCAL,)),
            dma((LOCAL,)),
            dma((LOCAL,)),
            dma((LOCAL,)),
            dma((2 * LOCAL,)),
            dma((LOCAL,)),
            dma((MB,)),
            dma((MB,)),
            dma((MB,)),
            dma((MB,)),
            dma((MB,)),
            dma((MB,)),
            dma((MB,)),
            dma((LOCAL,)),
            dma((LOCAL,)),
            dma((LOCAL,)),
            dma((LOCAL,)),
            dma((2 * LOCAL,)),
            dma((4 * PER_Z,)),
            dma((2 * PIECES,)),
        ],
        compiler_params=pltpu.CompilerParams(
            collective_id=0, has_side_effects=True, vmem_limit_bytes=60 * 1024 * 1024
        ),
    )(params, sent, back, wide_ids, cosine, sine)


def apply_adam(weights, first_moment, second_moment, gradient):
    first_new = 0.9 * first_moment + 0.1 * gradient
    second_new = 0.999 * second_moment + 0.001 * gradient * gradient
    fix_first = 1.0 - 0.9**STEP
    fix_second = 1.0 - 0.999**STEP
    update = first_new / fix_first / (jnp.sqrt(second_new / fix_second) + 1e-08)
    current = weights.astype(F32)
    renewed = (current - learn_rate * (update + decay_rate * current)).astype(BF16)
    return (renewed, first_new, second_new)


def shards(params, moment_one, moment_two, sent_rows, back_rows, slot_ids):
    summed = summed_gradient(params[0], sent_rows[0, 0], back_rows[0, 0], slot_ids[0, 0])
    renewed, first_new, second_new = apply_adam(params[0], moment_one[0], moment_two[0], summed / N_DP)
    return (renewed[None], first_new[None], second_new[None])


def solution(mesh):
    in_specs = (
        P("section", "dp", None),
        P("section", "dp", None),
        P("section", "dp", None),
        P("section", "dp", None, None, None),
        P("section", "dp", None, None, None),
        P("section", "dp", None),
    )
    out_specs = (P("section", "dp", None), P("section", "dp", None), P("section", "dp", None))
    return jax.shard_map(shards, mesh=mesh, in_specs=in_specs, out_specs=out_specs, check_vma=False)
```

```python
import jax
import jax.numpy as jnp
import numpy as np
from jax import lax
from jax.experimental import pallas as pl
from jax.experimental.pallas import tpu as pltpu
from jax.sharding import PartitionSpec as P

HEAD_SIZE = 64
QUERY_HEADS = 16
KEY_VALUE_HEADS = 4
STEP = 100
SEQ = 192
LOG = 4
MB = 2
PROWS = 2560

N_SECTION = 8
N_DP = 32
N_Z = 8
CHUNK = 64
PER_Z = 5
LOCAL = 20
SHARD = 80
LEAD = 12
STACK = 4
PARTS = 1
PART = CHUNK // PARTS
PIECE = 16
PIECES = SHARD // PIECE
Q_ROWS = 512
K_AT = 512
V_AT = 640
O_AT = 768
QKV_BLOCKS = 12

rope_base = 500000.0
learn_rate = 0.0003
decay_rate = 0.1

MESH = pl.DeviceIdType.MESH
BF16 = jnp.bfloat16
F32 = jnp.float32


def nn(a, b):
    return lax.dot_general(a, b, (((1,), (0,)), ((), ())), preferred_element_type=F32)


def nt(a, b):
    return lax.dot_general(a, b, (((1,), (1,)), ((), ())), preferred_element_type=F32)


def half(value):
    return lax.shift_right_logical(value, 1)


def low_bit(value):
    return lax.bitwise_and(value, 1)


def round_z(value):
    return lax.bitwise_and(value + N_Z, N_Z - 1)


def core_of(block):
    return jnp.where(
        block < 16,
        jnp.where(block < 8, 0, 1),
        jnp.where(block < 24, low_bit(half(block)), jnp.where(block < 32, 0, 1)),
    )


def place_of(block):
    return jnp.where(
        block < 16,
        lax.bitwise_and(block, 7),
        jnp.where(
            block < 24,
            jnp.where(block < 20, 8, 10) + low_bit(block),
            12 + lax.bitwise_and(block, 7),
        ),
    )


def tens(value):
    return jnp.where(value < 10, 0, jnp.where(value < 20, 1, 2))


def by_y(home, which):
    even = low_bit(home) == 0
    stays = jnp.logical_or(which == 2, which == jnp.where(even, 0, 4))
    return jnp.logical_not(stays)


def in_order(home, turn, ring_first):
    even = low_bit(home) == 0
    turn = jnp.where(ring_first, jnp.where(turn < 2, turn + 3, turn - 2), turn)
    of_even = jnp.where(turn < 2, 2 * turn + 1, jnp.where(turn == 2, 4, 2 * turn - 6))
    of_odd = jnp.where(turn < 2, turn, jnp.where(turn == 2, 3, 2 * turn - 4))
    return jnp.where(even, of_even, of_odd)


def more_down(home, which):
    even = low_bit(home) == 0
    lone = which == jnp.where(even, 1, 3)
    second = jnp.logical_or(which == 4, which == jnp.where(even, 2, 1))
    return jnp.where(lone, low_bit(half(home)), jnp.where(second, 1, 0))


def kernel(
    params_hbm,
    sent_hbm,
    back_hbm,
    ids_ref,
    cos_ref,
    sin_ref,
    grad_ref,
    shard,
    sent,
    back,
    ids_next,
    ids_prev,
    ids_one,
    ids_two,
    weights,
    relay,
    acts,
    picked,
    proj,
    dctx,
    lhs,
    total,
    stage,
    given,
    from_low,
    from_high,
    final,
    sem_local,
    sem_ids,
    sem_ids_send,
    sem_ids_recv,
    first_send,
    gather_up,
    gather_down,
    gather_recv,
    relay_up,
    relay_down,
    relay_out,
    relay_recv,
    own_local,
    own_send,
    own_recv,
    pick_send,
    pick_recv,
    pass_send,
    pass_recv,
    sum_send,
    low_recv,
    high_recv,
    give_send,
    give_recv,
    final_send,
    final_recv,
):
    section = lax.axis_index("section")
    dp = lax.axis_index("dp")
    z = lax.div(dp, 4)
    core = lax.rem(dp, 2)
    my_y = lax.rem(lax.div(dp, 2), 2)
    odd_section = lax.rem(section, 2)
    partner = section + 1 - 2 * odd_section
    sibling = dp + 1 - 2 * core
    up = lax.rem(dp + 4, N_DP)
    down = lax.rem(dp + N_DP - 4, N_DP)
    before = lax.rem(section + N_SECTION - 1, N_SECTION)
    after = lax.rem(section + 1, N_SECTION)
    before_two = lax.rem(section + N_SECTION - 2, N_SECTION)
    after_two = lax.rem(section + 2, N_SECTION)
    width = weights.shape[2]

    loads = [
        pltpu.make_async_copy(params_hbm, shard, sem_local.at[0]),
        pltpu.make_async_copy(sent_hbm, sent, sem_local.at[1]),
        pltpu.make_async_copy(back_hbm, back, sem_local.at[2]),
    ]
    for load in loads:
        load.start()

    barrier = pltpu.get_barrier_semaphore()
    beyond = jnp.where(odd_section == 0, before, after)
    peers = [(section, sibling), (section, up), (section, down), (before_two, dp), (after_two, dp), (beyond, dp)]
    for quarter in range(4):
        peers.append((partner, 4 * z + quarter))
    for peer in peers:
        pl.semaphore_signal(barrier, inc=1, device_id=peer, device_id_type=MESH)
    pl.semaphore_wait(barrier, len(peers))

    id_copies = [
        pltpu.make_async_remote_copy(
            src_ref=ids_ref,
            dst_ref=ids_next,
            send_sem=sem_ids_send.at[0],
            recv_sem=sem_ids_recv.at[0],
            device_id=(before, dp),
            device_id_type=MESH,
        ),
        pltpu.make_async_remote_copy(
            src_ref=ids_ref,
            dst_ref=ids_prev,
            send_sem=sem_ids_send.at[1],
            recv_sem=sem_ids_recv.at[1],
            device_id=(after, dp),
            device_id_type=MESH,
        ),
    ]
    for copy in id_copies:
        copy.start()

    loads[0].wait()

    def first_copy(piece, half):
        row = SHARD * dp + PIECE * piece
        block = lax.div(row, CHUNK)
        return pltpu.make_async_remote_copy(
            src_ref=shard.at[pl.ds(PIECE * piece, PIECE)],
            dst_ref=weights.at[place_of(block), pl.ds(pl.multiple_of(lax.rem(row, CHUNK), PIECE), PIECE)],
            send_sem=first_send.at[2 * piece + half],
            recv_sem=gather_recv.at[place_of(block)],
            device_id=(partner, 4 * z + 2 * half + core_of(block)),
            device_id_type=MESH,
        )

    def relay_piece(piece, local):
        row = SHARD * dp + PIECE * piece
        block = lax.div(row, CHUNK)
        source = shard.at[pl.ds(PIECE * piece, PIECE)]
        target = relay.at[place_of(block), pl.ds(pl.multiple_of(lax.rem(row, CHUNK), PIECE), PIECE)]
        arrived = relay_recv.at[place_of(block)]
        if local:
            return pltpu.make_async_copy(source, target, arrived)
        return pltpu.make_async_remote_copy(
            src_ref=source,
            dst_ref=target,
            send_sem=first_send.at[2 * piece],
            recv_sem=arrived,
            device_id=(section, sibling),
            device_id_type=MESH,
        )

    def piece_way(piece):
        block = lax.div(SHARD * dp + PIECE * piece, CHUNK)
        across = by_y(z, block - PER_Z * z)
        here = core_of(block) == core
        return across, jnp.logical_and(across, here), jnp.logical_and(across, jnp.logical_not(here))

    for piece in range(PIECES):
        across, here, there = piece_way(piece)

        @pl.when(jnp.logical_not(across))
        def _(piece=piece):
            for half in range(2):
                first_copy(piece, half).start()

        @pl.when(here)
        def _(piece=piece):
            relay_piece(piece, True).start()

        @pl.when(there)
        def _(piece=piece):
            relay_piece(piece, False).start()

    def gather_copy(place, going_up):
        return pltpu.make_async_remote_copy(
            src_ref=weights.at[place],
            dst_ref=weights.at[place],
            send_sem=(gather_up if going_up else gather_down).at[place],
            recv_sem=gather_recv.at[place],
            device_id=(section, up if going_up else down),
            device_id_type=MESH,
        )

    def relay_copy(place, going_up):
        return pltpu.make_async_remote_copy(
            src_ref=relay.at[place],
            dst_ref=relay.at[place],
            send_sem=(relay_up if going_up else relay_down).at[place],
            recv_sem=relay_recv.at[place],
            device_id=(section, up if going_up else down),
            device_id_type=MESH,
        )

    def relay_over(place, half):
        return pltpu.make_async_remote_copy(
            src_ref=relay.at[place],
            dst_ref=weights.at[place],
            send_sem=relay_out.at[LOCAL * half + place],
            recv_sem=gather_recv.at[place],
            device_id=(partner, 4 * z + 2 * half + core),
            device_id_type=MESH,
        )

    def gather_step(n):
        m = n - PER_Z
        middle = jnp.logical_and(n >= PER_Z, n < 35)
        away = jnp.where(n < PER_Z, 0, jnp.where(middle, 1 + tens(m), 4))
        turn = jnp.where(n < PER_Z, n, jnp.where(middle, half(m - 10 * tens(m)), n - 35))
        rising = jnp.logical_and(middle, low_bit(m) == 0)
        home = round_z(jnp.where(rising, z - away, z + away))
        which = in_order(home, turn, False)
        block = PER_Z * home + which
        odd = more_down(home, which)
        mine = core_of(block) == core
        across = by_y(home, which)
        mine_relay = jnp.logical_and(jnp.logical_and(mine, across), jnp.where(which < 3, 0, 1) == my_y)
        mine_ring = jnp.logical_and(mine, jnp.logical_not(across))
        start = n < PER_Z
        falling = jnp.logical_and(middle, jnp.logical_not(rising))
        send_up = jnp.logical_or(start, jnp.logical_and(rising, away < 4 - odd))
        send_down = jnp.logical_or(start, jnp.logical_and(falling, away < 3 + odd))
        return place_of(block), mine_ring, mine_relay, send_up, send_down

    def gather(n, carry):
        place, mine_ring, mine_relay, send_up, send_down = gather_step(n)

        @pl.when(mine_ring)
        def _():
            gather_copy(place, True).wait_recv()

            @pl.when(send_up)
            def _():
                gather_copy(place, True).start()

            @pl.when(send_down)
            def _():
                gather_copy(place, False).start()

        @pl.when(mine_relay)
        def _():
            relay_copy(place, True).wait_recv()

            @pl.when(send_up)
            def _():
                relay_copy(place, True).start()

            @pl.when(send_down)
            def _():
                relay_copy(place, False).start()

            for half_y in range(2):
                relay_over(place, half_y).start()

        return carry

    lax.fori_loop(0, 3, gather, 0)

    stays, leaves = odd_section, 1 - odd_section
    target_section = jnp.where(odd_section == 0, before_two, after_two)
    id_copies[0].wait_recv()
    to_one = pltpu.make_async_copy(ids_next, ids_one, sem_ids.at[0])
    to_one.start()
    to_one.wait()
    id_copies[1].wait_recv()
    to_two = pltpu.make_async_copy(ids_prev, ids_two, sem_ids.at[1])
    to_two.start()
    to_two.wait()
    loads[1].wait()
    loads[2].wait()
    own_copies = []
    own_locals = []
    pick_copies = []
    for m in range(MB):
        wanted_one, wanted_two = ids_one[m, 0], ids_two[m, 0]

        def pick_rows(n, carry, m=m, wanted_one=wanted_one, wanted_two=wanted_two):
            rows = pl.ds(pl.multiple_of(n * 16, 16), 16)
            value = sent[wanted_one, rows, :].astype(F32)
            scaling = lax.rsqrt(jnp.mean(value * value, axis=-1, keepdims=True) + 1e-05)
            picked[0, m, rows, :] = (value * scaling).astype(BF16)
            picked[1, m, rows, :] = back[wanted_two, rows, :]
            return carry

        lax.fori_loop(0, SEQ // 16, pick_rows, 0)
        pick_copies.append(
            pltpu.make_async_remote_copy(
                src_ref=picked.at[leaves, m],
                dst_ref=acts.at[leaves, 2 * core + m],
                send_sem=pick_send.at[m],
                recv_sem=pick_recv.at[m],
                device_id=(target_section, dp),
                device_id_type=MESH,
            )
        )
        own_copies.append(
            pltpu.make_async_remote_copy(
                src_ref=picked.at[stays, m],
                dst_ref=acts.at[stays, 2 * core + m],
                send_sem=own_send.at[m],
                recv_sem=own_recv.at[m],
                device_id=(section, sibling),
                device_id_type=MESH,
            )
        )
        own_locals.append(
            pltpu.make_async_copy(picked.at[stays, m], acts.at[stays, 2 * core + m], own_local.at[m])
        )
        pick_copies[m].start()
        own_copies[m].start()
        own_locals[m].start()

    lax.fori_loop(3, 40, gather, 0)

    pass_copies = []
    for m in range(MB):
        pick_copies[m].wait_recv()
        pass_copies.append(
            pltpu.make_async_remote_copy(
                src_ref=acts.at[leaves, 2 * core + m],
                dst_ref=acts.at[leaves, 2 * core + m],
                send_sem=pass_send.at[m],
                recv_sem=pass_recv.at[m],
                device_id=(section, sibling),
                device_id_type=MESH,
            )
        )
        pass_copies[m].start()

    def arrive(block, carry):
        across = by_y(lax.div(block, PER_Z), lax.rem(block, PER_Z))

        @pl.when(jnp.logical_and(across, core_of(block) == core))
        def _():
            gather_copy(place_of(block), True).wait_recv()

        return carry

    lax.fori_loop(0, 40, arrive, 0)

    for m in range(MB):
        own_locals[m].wait()
        own_copies[m].wait_recv()
        pass_copies[m].wait_recv()

    def project(batch, carry):
        rows = weights[:QKV_BLOCKS].reshape(O_AT, width)
        proj[batch] = nt(rows, acts[0, batch])
        return carry

    lax.fori_loop(0, 2 * MB, project, 0)

    def cotangent(batch, carry):
        rows = weights[QKV_BLOCKS:].reshape(Q_ROWS, width)
        dctx[batch] = nt(rows, acts[1, batch]).astype(BF16)
        return carry

    lax.fori_loop(0, 2 * MB, cotangent, 0)

    cosine, sine = cos_ref[...], sin_ref[...]
    middle_row = HEAD_SIZE // 2

    def rotate(value):
        a, b = value[:middle_row], value[middle_row:]
        return jnp.concatenate([a * cosine - b * sine, b * cosine + a * sine], axis=0)

    def rotate_back(value):
        a, b = value[:middle_row], value[middle_row:]
        return jnp.concatenate([a * cosine + b * sine, b * cosine - a * sine], axis=0)

    def attention(n, carry):
        batch, group = lax.div(n, 2), lax.rem(n, 2)
        key_rows = pl.ds(pl.multiple_of(K_AT + HEAD_SIZE * group, HEAD_SIZE), HEAD_SIZE)
        value_rows = pl.ds(pl.multiple_of(V_AT + HEAD_SIZE * group, HEAD_SIZE), HEAD_SIZE)
        key_t = rotate(proj[batch, key_rows, :])
        value_t = proj[batch, value_rows, :]
        key = key_t.T.astype(BF16)
        value = value_t.T.astype(BF16)
        key_t = key_t.astype(BF16)
        value_t = value_t.astype(BF16)
        ones = jnp.ones((16, SEQ), BF16)
        value_ones = jnp.concatenate([value_t, ones], axis=0)
        kept = lax.broadcasted_iota(jnp.int32, (SEQ, SEQ), 0) <= lax.broadcasted_iota(jnp.int32, (SEQ, SEQ), 1)
        kept = jnp.concatenate([kept.astype(jnp.int32)] * STACK, axis=1) > 0
        dkey = jnp.zeros((HEAD_SIZE, SEQ), F32)
        dvalue = jnp.zeros((HEAD_SIZE, SEQ), F32)
        for stack in range(4 // STACK):
            firsts = [256 * group + HEAD_SIZE * (STACK * stack + head) for head in range(STACK)]
            rows = [pl.ds(pl.multiple_of(first, HEAD_SIZE), HEAD_SIZE) for first in firsts]
            query_t = [(rotate(proj[batch, row, :]) * HEAD_SIZE**-0.5) for row in rows]
            query_t = jnp.concatenate(query_t, axis=1).astype(BF16)
            scores = jnp.where(kept, nn(key, query_t), -1e30)
            raised = jnp.exp(scores - jnp.max(scores, axis=0, keepdims=True))
            raised_b = raised.astype(BF16)
            context = nn(value_ones, raised_b)
            inverse = 1.0 / context[HEAD_SIZE : HEAD_SIZE + 1]
            context = context[:HEAD_SIZE] * inverse
            cot = jnp.concatenate([dctx[batch, row, :].astype(F32) for row in rows], axis=1)
            delta = jnp.sum(cot * context, axis=0, keepdims=True) * inverse
            cot = (cot * inverse).astype(BF16)
            dscores = (raised * (nn(value, cot) - delta)).astype(BF16)
            dvalue = dvalue + nt(cot, raised_b)
            dquery = nn(key_t, dscores) * HEAD_SIZE**-0.5
            dkey = dkey + nt(query_t, dscores)
            for head in range(STACK):
                lanes = slice(SEQ * head, SEQ * (head + 1))
                context_rows = pl.ds(pl.multiple_of(O_AT + firsts[head], HEAD_SIZE), HEAD_SIZE)
                lhs[batch, context_rows, :] = context[:, lanes].astype(BF16)
                lhs[batch, rows[head], :] = rotate_back(dquery[:, lanes]).astype(BF16)
        lhs[batch, key_rows, :] = rotate_back(dkey).astype(BF16)
        lhs[batch, value_rows, :] = dvalue.astype(BF16)
        return carry

    lax.fori_loop(0, 8, attention, 0)

    def part_rows(part):
        return pl.ds(PART * part, PART)

    def sum_copy(place, part, going_up, source):
        landing, arrived = (from_low, low_recv) if going_up else (from_high, high_recv)
        return pltpu.make_async_remote_copy(
            src_ref=source.at[place, part_rows(part)],
            dst_ref=landing.at[place, part_rows(part)],
            send_sem=sum_send.at[PARTS * place + part],
            recv_sem=arrived.at[PARTS * place + part],
            device_id=(section, up if going_up else down),
            device_id_type=MESH,
        )

    def give_copy(place, part, which):
        return pltpu.make_async_remote_copy(
            src_ref=stage.at[place, part_rows(part)],
            dst_ref=given.at[my_y, place, part_rows(part)],
            send_sem=give_send.at[PARTS * place + part],
            recv_sem=give_recv.at[PARTS * (LOCAL * my_y + place) + part],
            device_id=(partner, 4 * z + 2 * jnp.where(which < 3, 0, 1) + core),
            device_id_type=MESH,
        )

    def given_wait(place, part, source):
        pltpu.make_async_remote_copy(
            src_ref=given.at[source, place, part_rows(part)],
            dst_ref=given.at[source, place, part_rows(part)],
            send_sem=give_send.at[PARTS * place + part],
            recv_sem=give_recv.at[PARTS * (LOCAL * source + place) + part],
            device_id=(partner, dp),
            device_id_type=MESH,
        ).wait_recv()

    def keeper_of(which, quarter):
        inside = CHUNK * which + PIECE * quarter
        keeper = lax.div(inside, SHARD)
        return keeper, lax.div(inside - SHARD * keeper, PIECE)

    def final_copy(which, quarter):
        keeper, piece = keeper_of(which, quarter)
        return pltpu.make_async_remote_copy(
            src_ref=stage.at[place_of(PER_Z * z + which), pl.ds(PIECE * quarter, PIECE)],
            dst_ref=final.at[my_y, pl.ds(pl.multiple_of(PIECE * piece, PIECE), PIECE)],
            send_sem=final_send.at[4 * which + quarter],
            recv_sem=final_recv.at[PIECES * my_y + piece],
            device_id=(partner, 4 * z + keeper),
            device_id_type=MESH,
        )

    def relay_final(which, quarter, local):
        _, piece = keeper_of(which, quarter)
        source = given.at[0, place_of(PER_Z * z + which), pl.ds(PIECE * quarter, PIECE)]
        target = final.at[0, pl.ds(pl.multiple_of(PIECE * piece, PIECE), PIECE)]
        if local:
            return pltpu.make_async_copy(source, target, final_recv.at[piece])
        return pltpu.make_async_remote_copy(
            src_ref=source,
            dst_ref=target,
            send_sem=final_send.at[4 * which + quarter],
            recv_sem=final_recv.at[piece],
            device_id=(section, sibling),
            device_id_type=MESH,
        )

    def sum_step(n):
        m = n - PER_Z
        middle = jnp.logical_and(n >= PER_Z, n < 35)
        last = n >= 35
        away = jnp.where(n < PER_Z, 4, jnp.where(middle, 3 - tens(m), 0))
        turn = jnp.where(n < PER_Z, n, jnp.where(middle, half(m - 10 * tens(m)), n - 35))
        falling = jnp.logical_and(middle, low_bit(m) == 1)
        home = round_z(jnp.where(falling, z - away, z + away))
        which = in_order(home, turn, True)
        block = PER_Z * home + which
        odd = more_down(home, which)
        mine = core_of(block) == core
        across = by_y(home, which)
        mine_give = jnp.logical_and(mine, across)
        mine_relay = jnp.logical_and(mine_give, jnp.where(which < 3, 0, 1) == my_y)
        mine_ring = jnp.logical_and(mine, jnp.logical_not(across))
        rises = jnp.where(middle, jnp.logical_not(falling), odd == 0)
        has_low = jnp.logical_or(last, jnp.logical_and(rises, away < 4 - odd))
        has_high = jnp.logical_or(last, jnp.logical_and(jnp.logical_not(rises), away < 3 + odd))
        go_up = jnp.logical_and(rises, jnp.logical_not(last))
        go_down = jnp.logical_and(jnp.logical_not(rises), jnp.logical_not(last))
        return place_of(block), which, mine_ring, mine_give, mine_relay, has_low, has_high, go_up, go_down, last

    def block_gradient(place):
        rows = pl.ds(pl.multiple_of(place * CHUNK, CHUNK), CHUNK)
        side = jnp.where(place >= QKV_BLOCKS, 1, 0)
        for tile in range(4):
            columns = slice(tile * width // 4, (tile + 1) * width // 4)
            value = nn(lhs[0, rows, :], acts[side, 0, :, columns])
            for batch in range(1, 2 * MB):
                value = value + nn(lhs[batch, rows, :], acts[side, batch, :, columns])
            total[:, columns] = value

    def give(n):
        place, which, _, mine_give, _, _, _, _, _, _ = sum_step(n)

        @pl.when(mine_give)
        def _():
            block_gradient(place)
            stage[place] = total[...].astype(BF16)
            for part in range(PARTS):
                give_copy(place, part, which).start()

    def reduce(n):
        place, which, mine_ring, _, mine_relay, has_low, has_high, go_up, go_down, last = sum_step(n)

        def pass_on(part, buffer, keep):
            rows = part_rows(part)
            for going_up, has, landing in ((True, has_low, from_low), (False, has_high, from_high)):

                @pl.when(has)
                def _(going_up=going_up, landing=landing):
                    sum_copy(place, part, going_up, buffer).wait_recv()
                    total[rows, :] += landing[place, rows, :].astype(F32)

            buffer[place, rows, :] = total[rows, :].astype(BF16)
            for going_up, goes in ((True, go_up), (False, go_down)):

                @pl.when(goes)
                def _(going_up=going_up):
                    sum_copy(place, part, going_up, buffer).start()

            @pl.when(last)
            def _():
                for quarter in range(PART // PIECE * part, PART // PIECE * (part + 1)):
                    keep(quarter)

        def keep_ring(quarter):
            final_copy(which, quarter).start()

        def keep_relay(quarter):
            keeper, _ = keeper_of(which, quarter)
            here = low_bit(keeper) == core

            @pl.when(here)
            def _():
                relay_final(which, quarter, True).start()

            @pl.when(jnp.logical_not(here))
            def _():
                relay_final(which, quarter, False).start()

        @pl.when(mine_ring)
        def _():
            block_gradient(place)
            for part in range(PARTS):
                pass_on(part, stage, keep_ring)

        @pl.when(mine_relay)
        def _():
            for part in range(PARTS):
                rows = part_rows(part)
                for source in range(2):
                    given_wait(place, part, source)
                total[rows, :] = given[0, place, rows, :].astype(F32) + given[1, place, rows, :].astype(F32)
                pass_on(part, given.at[0], keep_relay)

    def gather_sent(n):
        place, mine_ring, mine_relay, send_up, send_down = gather_step(n)
        for going_up, goes in ((True, send_up), (False, send_down)):

            @pl.when(jnp.logical_and(mine_ring, goes))
            def _(going_up=going_up):
                gather_copy(place, going_up).wait_send()

            @pl.when(jnp.logical_and(mine_relay, goes))
            def _(going_up=going_up):
                relay_copy(place, going_up).wait_send()

        @pl.when(mine_relay)
        def _():
            for half_y in range(2):
                relay_over(place, half_y).wait_send()

    def lead(n, carry):
        give(n)
        gather_sent(n)
        return carry

    def both(n, carry):
        @pl.when(n < 40)
        def _():
            give(n)
            gather_sent(n)

        reduce(n - LEAD)
        return carry

    lax.fori_loop(0, LEAD, lead, 0)
    lax.fori_loop(LEAD, 40 + LEAD, both, 0)

    for copy in id_copies + pick_copies + own_copies + pass_copies:
        copy.wait_send()
    for piece in range(PIECES):
        across, _, there = piece_way(piece)

        @pl.when(jnp.logical_not(across))
        def _(piece=piece):
            for half_y in range(2):
                first_copy(piece, half_y).wait_send()

        @pl.when(there)
        def _(piece=piece):
            relay_piece(piece, False).wait_send()

    def drain(n, carry):
        place, which, mine_ring, mine_give, mine_relay, _, _, _, _, last = sum_step(n)

        @pl.when(mine_give)
        def _():
            for part in range(PARTS):
                give_copy(place, part, which).wait_send()

        @pl.when(jnp.logical_and(jnp.logical_or(mine_ring, mine_relay), jnp.logical_not(last)))
        def _():
            for part in range(PARTS):
                sum_copy(place, part, True, stage).wait_send()

        @pl.when(last)
        def _():
            for quarter in range(CHUNK // PIECE):
                keeper, _ = keeper_of(which, quarter)
                away_core = low_bit(keeper) != core

                @pl.when(jnp.logical_or(mine_ring, jnp.logical_and(mine_relay, away_core)))
                def _(quarter=quarter):
                    final_copy(which, quarter).wait_send()

        return carry

    lax.fori_loop(0, 40, drain, 0)

    def final_wait(piece, source):
        rows = pl.ds(PIECE * piece, PIECE)
        pltpu.make_async_remote_copy(
            src_ref=final.at[source, rows],
            dst_ref=final.at[source, rows],
            send_sem=final_send.at[0],
            recv_sem=final_recv.at[PIECES * source + piece],
            device_id=(section, sibling),
            device_id_type=MESH,
        ).wait_recv()

    for piece in range(PIECES):
        rows = pl.ds(PIECE * piece, PIECE)
        across, _, _ = piece_way(piece)
        final_wait(piece, 0)
        grad_ref[rows, :] = final[0, rows, :].astype(F32)

        @pl.when(jnp.logical_not(across))
        def _(piece=piece, rows=rows):
            final_wait(piece, 1)
            grad_ref[rows, :] += final[1, rows, :].astype(F32)


def summed_gradient(params, sent, back, ids):
    width = params.shape[-1]
    frequency = rope_base ** (-np.arange(HEAD_SIZE // 2, dtype=np.float64) * 2.0 / HEAD_SIZE)
    angles = frequency[:, None] * np.arange(SEQ, dtype=np.float64)[None, :]
    cosine = jnp.asarray(np.cos(angles), F32)
    sine = jnp.asarray(np.sin(angles), F32)
    wide_ids = jnp.broadcast_to(ids.reshape(1, MB, 1), (4, MB, 128)).reshape(8, 128)
    dma = pltpu.SemaphoreType.DMA
    in_vmem = pl.BlockSpec(memory_space=pltpu.VMEM)
    anywhere = pl.BlockSpec(memory_space=pl.ANY)
    return pl.pallas_call(
        kernel,
        out_shape=jax.ShapeDtypeStruct((SHARD, width), F32),
        in_specs=[anywhere, anywhere, anywhere, in_vmem, in_vmem, in_vmem],
        out_specs=in_vmem,
        scratch_shapes=[
            pltpu.VMEM((SHARD, width), BF16),
            pltpu.VMEM((LOG, SEQ, width), BF16),
            pltpu.VMEM((LOG, SEQ, width), BF16),
            pltpu.VMEM((8, 128), jnp.int32),
            pltpu.VMEM((8, 128), jnp.int32),
            pltpu.SMEM((8, 128), jnp.int32),
            pltpu.SMEM((8, 128), jnp.int32),
            pltpu.VMEM((LOCAL, CHUNK, width), BF16),
            pltpu.VMEM((LOCAL, CHUNK, width), BF16),
            pltpu.VMEM((2, 2 * MB, SEQ, width), BF16),
            pltpu.VMEM((2, MB, SEQ, width), BF16),
            pltpu.VMEM((2 * MB, O_AT, SEQ), F32),
            pltpu.VMEM((2 * MB, Q_ROWS, SEQ), BF16),
            pltpu.VMEM((2 * MB, LOCAL * CHUNK, SEQ), BF16),
            pltpu.VMEM((CHUNK, width), F32),
            pltpu.VMEM((LOCAL, CHUNK, width), BF16),
            pltpu.VMEM((2, LOCAL, CHUNK, width), BF16),
            pltpu.VMEM((LOCAL, CHUNK, width), BF16),
            pltpu.VMEM((LOCAL, CHUNK, width), BF16),
            pltpu.VMEM((2, SHARD, width), BF16),
            dma((3,)),
            dma((2,)),
            dma((2,)),
            dma((2,)),
            dma((2 * PIECES,)),
            dma((LOCAL,)),
            dma((LOCAL,)),
            dma((LOCAL,)),
            dma((LOCAL,)),
            dma((LOCAL,)),
            dma((2 * LOCAL,)),
            dma((LOCAL,)),
            dma((MB,)),
            dma((MB,)),
            dma((MB,)),
            dma((MB,)),
            dma((MB,)),
            dma((MB,)),
            dma((MB,)),
            dma((PARTS * LOCAL,)),
            dma((PARTS * LOCAL,)),
            dma((PARTS * LOCAL,)),
            dma((PARTS * LOCAL,)),
            dma((2 * PARTS * LOCAL,)),
            dma((4 * PER_Z,)),
            dma((2 * PIECES,)),
        ],
        compiler_params=pltpu.CompilerParams(
            collective_id=0, has_side_effects=True, vmem_limit_bytes=60 * 1024 * 1024
        ),
    )(params, sent, back, wide_ids, cosine, sine)


def apply_adam(weights, first_moment, second_moment, gradient):
    first_new = 0.9 * first_moment + 0.1 * gradient
    second_new = 0.999 * second_moment + 0.001 * gradient * gradient
    fix_first = 1.0 - 0.9**STEP
    fix_second = 1.0 - 0.999**STEP
    update = first_new / fix_first / (jnp.sqrt(second_new / fix_second) + 1e-08)
    current = weights.astype(F32)
    renewed = (current - learn_rate * (update + decay_rate * current)).astype(BF16)
    return (renewed, first_new, second_new)


def shards(params, moment_one, moment_two, sent_rows, back_rows, slot_ids):
    summed = summed_gradient(params[0], sent_rows[0, 0], back_rows[0, 0], slot_ids[0, 0])
    renewed, first_new, second_new = apply_adam(params[0], moment_one[0], moment_two[0], summed / N_DP)
    return (renewed[None], first_new[None], second_new[None])


def solution(mesh):
    in_specs = (
        P("section", "dp", None),
        P("section", "dp", None),
        P("section", "dp", None),
        P("section", "dp", None, None, None),
        P("section", "dp", None, None, None),
        P("section", "dp", None),
    )
    out_specs = (P("section", "dp", None), P("section", "dp", None), P("section", "dp", None))
    return jax.shard_map(shards, mesh=mesh, in_specs=in_specs, out_specs=out_specs, check_vma=False)
```

```python
import jax
import jax.numpy as jnp
import numpy as np
from jax import lax
from jax.experimental import pallas as pl
from jax.experimental.pallas import tpu as pltpu
from jax.sharding import PartitionSpec as P

HEAD_SIZE = 64
QUERY_HEADS = 16
KEY_VALUE_HEADS = 4
STEP = 100
SEQ = 192
LOG = 4
MB = 2
PROWS = 2560

N_SECTION = 8
N_DP = 32
N_Z = 8
CHUNK = 64
PER_Z = 5
LOCAL = 20
SHARD = 80
LEAD = 10
LAG = 16
STACK = 4
PARTS = 1
PART = CHUNK // PARTS
PIECE = 16
PIECES = SHARD // PIECE
Q_ROWS = 512
K_AT = 512
V_AT = 640
O_AT = 768
QKV_BLOCKS = 12

rope_base = 500000.0
learn_rate = 0.0003
decay_rate = 0.1

MESH = pl.DeviceIdType.MESH
BF16 = jnp.bfloat16
F32 = jnp.float32


def nn(a, b):
    return lax.dot_general(a, b, (((1,), (0,)), ((), ())), preferred_element_type=F32)


def nt(a, b):
    return lax.dot_general(a, b, (((1,), (1,)), ((), ())), preferred_element_type=F32)


def half(value):
    return lax.shift_right_logical(value, 1)


def low_bit(value):
    return lax.bitwise_and(value, 1)


def round_z(value):
    return lax.bitwise_and(value + N_Z, N_Z - 1)


def core_of(block):
    return jnp.where(
        block < 16,
        jnp.where(block < 8, 0, 1),
        jnp.where(block < 24, low_bit(half(block)), jnp.where(block < 32, 0, 1)),
    )


def place_of(block):
    return jnp.where(
        block < 16,
        lax.bitwise_and(block, 7),
        jnp.where(
            block < 24,
            jnp.where(block < 20, 8, 10) + low_bit(block),
            12 + lax.bitwise_and(block, 7),
        ),
    )


def tens(value):
    return jnp.where(value < 10, 0, jnp.where(value < 20, 1, 2))


def by_y(home, which):
    even = low_bit(home) == 0
    stays = jnp.logical_or(which == 2, which == jnp.where(even, 0, 4))
    return jnp.logical_not(stays)


def in_order(home, turn, ring_first):
    even = low_bit(home) == 0
    turn = jnp.where(ring_first, jnp.where(turn < 2, turn + 3, turn - 2), turn)
    of_even = jnp.where(turn < 2, 2 * turn + 1, jnp.where(turn == 2, 4, 2 * turn - 6))
    of_odd = jnp.where(turn < 2, turn, jnp.where(turn == 2, 3, 2 * turn - 4))
    return jnp.where(even, of_even, of_odd)


def more_down(home, which):
    even = low_bit(home) == 0
    lone = which == jnp.where(even, 1, 3)
    second = jnp.logical_or(which == 4, which == jnp.where(even, 2, 1))
    return jnp.where(lone, low_bit(half(home)), jnp.where(second, 1, 0))


def kernel(
    params_hbm,
    sent_hbm,
    back_hbm,
    ids_ref,
    cos_ref,
    sin_ref,
    grad_ref,
    shard,
    sent,
    back,
    ids_own,
    ids_next,
    ids_prev,
    ids_one,
    ids_two,
    weights,
    relay,
    acts,
    picked,
    proj,
    dctx,
    lhs,
    total,
    stage,
    given,
    from_low,
    from_high,
    final,
    sem_local,
    sem_ids,
    sem_ids_send,
    sem_ids_recv,
    first_send,
    gather_up,
    gather_down,
    gather_recv,
    relay_up,
    relay_down,
    relay_out,
    relay_recv,
    own_local,
    own_send,
    own_recv,
    pick_send,
    pick_recv,
    pass_send,
    pass_recv,
    sum_send,
    low_recv,
    high_recv,
    give_send,
    give_recv,
    final_send,
    final_recv,
):
    section = lax.axis_index("section")
    dp = lax.axis_index("dp")
    z = lax.div(dp, 4)
    core = lax.rem(dp, 2)
    my_y = lax.rem(lax.div(dp, 2), 2)
    odd_section = lax.rem(section, 2)
    partner = section + 1 - 2 * odd_section
    sibling = dp + 1 - 2 * core
    up = lax.rem(dp + 4, N_DP)
    down = lax.rem(dp + N_DP - 4, N_DP)
    before = lax.rem(section + N_SECTION - 1, N_SECTION)
    after = lax.rem(section + 1, N_SECTION)
    before_two = lax.rem(section + N_SECTION - 2, N_SECTION)
    after_two = lax.rem(section + 2, N_SECTION)
    width = weights.shape[2]

    loads = [
        pltpu.make_async_copy(params_hbm, shard, sem_local.at[0]),
        pltpu.make_async_copy(sent_hbm, sent, sem_local.at[1]),
        pltpu.make_async_copy(back_hbm, back, sem_local.at[2]),
    ]
    for load in loads:
        load.start()

    row_of = lax.broadcasted_iota(jnp.int32, (8, 128), 0)
    ids_own[...] = jnp.where(row_of == 0, ids_ref[0, 0], ids_ref[0, 1])

    barrier = pltpu.get_barrier_semaphore()
    beyond = jnp.where(odd_section == 0, before, after)
    peers = [(section, sibling), (section, up), (section, down), (before_two, dp), (after_two, dp), (beyond, dp)]
    for quarter in range(4):
        peers.append((partner, 4 * z + quarter))
    for peer in peers:
        pl.semaphore_signal(barrier, inc=1, device_id=peer, device_id_type=MESH)
    pl.semaphore_wait(barrier, len(peers))

    id_copies = [
        pltpu.make_async_remote_copy(
            src_ref=ids_own,
            dst_ref=ids_next,
            send_sem=sem_ids_send.at[0],
            recv_sem=sem_ids_recv.at[0],
            device_id=(before, dp),
            device_id_type=MESH,
        ),
        pltpu.make_async_remote_copy(
            src_ref=ids_own,
            dst_ref=ids_prev,
            send_sem=sem_ids_send.at[1],
            recv_sem=sem_ids_recv.at[1],
            device_id=(after, dp),
            device_id_type=MESH,
        ),
    ]
    for copy in id_copies:
        copy.start()

    loads[0].wait()

    def first_copy(piece, half):
        row = SHARD * dp + PIECE * piece
        block = lax.div(row, CHUNK)
        return pltpu.make_async_remote_copy(
            src_ref=shard.at[pl.ds(PIECE * piece, PIECE)],
            dst_ref=weights.at[place_of(block), pl.ds(pl.multiple_of(lax.rem(row, CHUNK), PIECE), PIECE)],
            send_sem=first_send.at[2 * piece + half],
            recv_sem=gather_recv.at[place_of(block)],
            device_id=(partner, 4 * z + 2 * half + core_of(block)),
            device_id_type=MESH,
        )

    def relay_piece(piece, local):
        row = SHARD * dp + PIECE * piece
        block = lax.div(row, CHUNK)
        source = shard.at[pl.ds(PIECE * piece, PIECE)]
        target = relay.at[place_of(block), pl.ds(pl.multiple_of(lax.rem(row, CHUNK), PIECE), PIECE)]
        arrived = relay_recv.at[place_of(block)]
        if local:
            return pltpu.make_async_copy(source, target, arrived)
        return pltpu.make_async_remote_copy(
            src_ref=source,
            dst_ref=target,
            send_sem=first_send.at[2 * piece],
            recv_sem=arrived,
            device_id=(section, sibling),
            device_id_type=MESH,
        )

    def piece_way(piece):
        block = lax.div(SHARD * dp + PIECE * piece, CHUNK)
        across = by_y(z, block - PER_Z * z)
        here = core_of(block) == core
        return across, jnp.logical_and(across, here), jnp.logical_and(across, jnp.logical_not(here))

    for piece in range(PIECES):
        across, here, there = piece_way(piece)

        @pl.when(jnp.logical_not(across))
        def _(piece=piece):
            for half in range(2):
                first_copy(piece, half).start()

        @pl.when(here)
        def _(piece=piece):
            relay_piece(piece, True).start()

        @pl.when(there)
        def _(piece=piece):
            relay_piece(piece, False).start()

    def gather_copy(place, going_up):
        return pltpu.make_async_remote_copy(
            src_ref=weights.at[place],
            dst_ref=weights.at[place],
            send_sem=(gather_up if going_up else gather_down).at[place],
            recv_sem=gather_recv.at[place],
            device_id=(section, up if going_up else down),
            device_id_type=MESH,
        )

    def relay_copy(place, going_up):
        return pltpu.make_async_remote_copy(
            src_ref=relay.at[place],
            dst_ref=relay.at[place],
            send_sem=(relay_up if going_up else relay_down).at[place],
            recv_sem=relay_recv.at[place],
            device_id=(section, up if going_up else down),
            device_id_type=MESH,
        )

    def relay_over(place, half):
        return pltpu.make_async_remote_copy(
            src_ref=relay.at[place],
            dst_ref=weights.at[place],
            send_sem=relay_out.at[LOCAL * half + place],
            recv_sem=gather_recv.at[place],
            device_id=(partner, 4 * z + 2 * half + core),
            device_id_type=MESH,
        )

    def gather_step(n):
        m = n - PER_Z
        middle = jnp.logical_and(n >= PER_Z, n < 35)
        away = jnp.where(n < PER_Z, 0, jnp.where(middle, 1 + tens(m), 4))
        turn = jnp.where(n < PER_Z, n, jnp.where(middle, half(m - 10 * tens(m)), n - 35))
        rising = jnp.logical_and(middle, low_bit(m) == 0)
        home = round_z(jnp.where(rising, z - away, z + away))
        which = in_order(home, turn, False)
        block = PER_Z * home + which
        odd = more_down(home, which)
        mine = core_of(block) == core
        across = by_y(home, which)
        mine_relay = jnp.logical_and(jnp.logical_and(mine, across), jnp.where(which < 3, 0, 1) == my_y)
        mine_ring = jnp.logical_and(mine, jnp.logical_not(across))
        start = n < PER_Z
        falling = jnp.logical_and(middle, jnp.logical_not(rising))
        send_up = jnp.logical_or(start, jnp.logical_and(rising, away < 4 - odd))
        send_down = jnp.logical_or(start, jnp.logical_and(falling, away < 3 + odd))
        return place_of(block), mine_ring, mine_relay, send_up, send_down

    def gather(n, carry):
        place, mine_ring, mine_relay, send_up, send_down = gather_step(n)

        @pl.when(mine_ring)
        def _():
            gather_copy(place, True).wait_recv()

            @pl.when(send_up)
            def _():
                gather_copy(place, True).start()

            @pl.when(send_down)
            def _():
                gather_copy(place, False).start()

        @pl.when(mine_relay)
        def _():
            relay_copy(place, True).wait_recv()

            @pl.when(send_up)
            def _():
                relay_copy(place, True).start()

            @pl.when(send_down)
            def _():
                relay_copy(place, False).start()

            for half_y in range(2):
                relay_over(place, half_y).start()

        return carry

    lax.fori_loop(0, 3, gather, 0)

    stays, leaves = odd_section, 1 - odd_section
    target_section = jnp.where(odd_section == 0, before_two, after_two)
    id_copies[0].wait_recv()
    to_one = pltpu.make_async_copy(ids_next, ids_one, sem_ids.at[0])
    to_one.start()
    to_one.wait()
    id_copies[1].wait_recv()
    to_two = pltpu.make_async_copy(ids_prev, ids_two, sem_ids.at[1])
    to_two.start()
    to_two.wait()
    loads[1].wait()
    loads[2].wait()
    own_copies = []
    own_locals = []
    pick_copies = []
    for m in range(MB):
        wanted_one, wanted_two = ids_one[m, 0], ids_two[m, 0]

        def pick_rows(n, carry, m=m, wanted_one=wanted_one, wanted_two=wanted_two):
            rows = pl.ds(pl.multiple_of(n * 16, 16), 16)
            value = sent[wanted_one, rows, :].astype(F32)
            scaling = lax.rsqrt(jnp.mean(value * value, axis=-1, keepdims=True) + 1e-05)
            picked[0, m, rows, :] = (value * scaling).astype(BF16)
            picked[1, m, rows, :] = back[wanted_two, rows, :]
            return carry

        lax.fori_loop(0, SEQ // 16, pick_rows, 0)
        pick_copies.append(
            pltpu.make_async_remote_copy(
                src_ref=picked.at[leaves, m],
                dst_ref=acts.at[leaves, 2 * core + m],
                send_sem=pick_send.at[m],
                recv_sem=pick_recv.at[m],
                device_id=(target_section, dp),
                device_id_type=MESH,
            )
        )
        own_copies.append(
            pltpu.make_async_remote_copy(
                src_ref=picked.at[stays, m],
                dst_ref=acts.at[stays, 2 * core + m],
                send_sem=own_send.at[m],
                recv_sem=own_recv.at[m],
                device_id=(section, sibling),
                device_id_type=MESH,
            )
        )
        own_locals.append(
            pltpu.make_async_copy(picked.at[stays, m], acts.at[stays, 2 * core + m], own_local.at[m])
        )
        pick_copies[m].start()
        own_copies[m].start()
        own_locals[m].start()

    lax.fori_loop(3, 40, gather, 0)

    pass_copies = []
    for m in range(MB):
        pick_copies[m].wait_recv()
        pass_copies.append(
            pltpu.make_async_remote_copy(
                src_ref=acts.at[leaves, 2 * core + m],
                dst_ref=acts.at[leaves, 2 * core + m],
                send_sem=pass_send.at[m],
                recv_sem=pass_recv.at[m],
                device_id=(section, sibling),
                device_id_type=MESH,
            )
        )
        pass_copies[m].start()

    def arrive(block, carry):
        across = by_y(lax.div(block, PER_Z), lax.rem(block, PER_Z))

        @pl.when(jnp.logical_and(across, core_of(block) == core))
        def _():
            gather_copy(place_of(block), True).wait_recv()

        return carry

    lax.fori_loop(0, 40, arrive, 0)

    for m in range(MB):
        own_locals[m].wait()
        own_copies[m].wait_recv()
        pass_copies[m].wait_recv()

    def project(batch, carry):
        rows = weights[:QKV_BLOCKS].reshape(O_AT, width)
        proj[batch] = nt(rows, acts[0, batch])
        return carry

    lax.fori_loop(0, 2 * MB, project, 0)

    def cotangent(batch, carry):
        rows = weights[QKV_BLOCKS:].reshape(Q_ROWS, width)
        dctx[batch] = nt(rows, acts[1, batch]).astype(BF16)
        return carry

    lax.fori_loop(0, 2 * MB, cotangent, 0)

    cosine, sine = cos_ref[...], sin_ref[...]
    middle_row = HEAD_SIZE // 2

    def rotate(value):
        a, b = value[:middle_row], value[middle_row:]
        return jnp.concatenate([a * cosine - b * sine, b * cosine + a * sine], axis=0)

    def rotate_back(value):
        a, b = value[:middle_row], value[middle_row:]
        return jnp.concatenate([a * cosine + b * sine, b * cosine - a * sine], axis=0)

    def attention(n, carry):
        batch, group = lax.div(n, 2), lax.rem(n, 2)
        key_rows = pl.ds(pl.multiple_of(K_AT + HEAD_SIZE * group, HEAD_SIZE), HEAD_SIZE)
        value_rows = pl.ds(pl.multiple_of(V_AT + HEAD_SIZE * group, HEAD_SIZE), HEAD_SIZE)
        key_t = rotate(proj[batch, key_rows, :])
        value_t = proj[batch, value_rows, :]
        key = key_t.T.astype(BF16)
        value = value_t.T.astype(BF16)
        key_t = key_t.astype(BF16)
        value_t = value_t.astype(BF16)
        ones = jnp.ones((16, SEQ), BF16)
        value_ones = jnp.concatenate([value_t, ones], axis=0)
        kept = lax.broadcasted_iota(jnp.int32, (SEQ, SEQ), 0) <= lax.broadcasted_iota(jnp.int32, (SEQ, SEQ), 1)
        kept = jnp.concatenate([kept.astype(jnp.int32)] * STACK, axis=1) > 0
        dkey = jnp.zeros((HEAD_SIZE, SEQ), F32)
        dvalue = jnp.zeros((HEAD_SIZE, SEQ), F32)
        for stack in range(4 // STACK):
            firsts = [256 * group + HEAD_SIZE * (STACK * stack + head) for head in range(STACK)]
            rows = [pl.ds(pl.multiple_of(first, HEAD_SIZE), HEAD_SIZE) for first in firsts]
            query_t = [(rotate(proj[batch, row, :]) * HEAD_SIZE**-0.5) for row in rows]
            query_t = jnp.concatenate(query_t, axis=1).astype(BF16)
            scores = jnp.where(kept, nn(key, query_t), -1e30)
            raised = jnp.exp(scores - jnp.max(scores, axis=0, keepdims=True))
            raised_b = raised.astype(BF16)
            context = nn(value_ones, raised_b)
            inverse = 1.0 / context[HEAD_SIZE : HEAD_SIZE + 1]
            context = context[:HEAD_SIZE] * inverse
            cot = jnp.concatenate([dctx[batch, row, :].astype(F32) for row in rows], axis=1)
            delta = jnp.sum(cot * context, axis=0, keepdims=True) * inverse
            cot = (cot * inverse).astype(BF16)
            dscores = (raised * (nn(value, cot) - delta)).astype(BF16)
            dvalue = dvalue + nt(cot, raised_b)
            dquery = nn(key_t, dscores) * HEAD_SIZE**-0.5
            dkey = dkey + nt(query_t, dscores)
            for head in range(STACK):
                lanes = slice(SEQ * head, SEQ * (head + 1))
                context_rows = pl.ds(pl.multiple_of(O_AT + firsts[head], HEAD_SIZE), HEAD_SIZE)
                lhs[batch, context_rows, :] = context[:, lanes].astype(BF16)
                lhs[batch, rows[head], :] = rotate_back(dquery[:, lanes]).astype(BF16)
        lhs[batch, key_rows, :] = rotate_back(dkey).astype(BF16)
        lhs[batch, value_rows, :] = dvalue.astype(BF16)
        return carry

    lax.fori_loop(0, 8, attention, 0)

    def part_rows(part):
        return pl.ds(PART * part, PART)

    def sum_copy(place, part, going_up, source):
        landing, arrived = (from_low, low_recv) if going_up else (from_high, high_recv)
        return pltpu.make_async_remote_copy(
            src_ref=source.at[place, part_rows(part)],
            dst_ref=landing.at[place, part_rows(part)],
            send_sem=sum_send.at[PARTS * place + part],
            recv_sem=arrived.at[PARTS * place + part],
            device_id=(section, up if going_up else down),
            device_id_type=MESH,
        )

    def give_copy(place, part, which):
        return pltpu.make_async_remote_copy(
            src_ref=stage.at[place, part_rows(part)],
            dst_ref=given.at[my_y, place, part_rows(part)],
            send_sem=give_send.at[PARTS * place + part],
            recv_sem=give_recv.at[PARTS * (LOCAL * my_y + place) + part],
            device_id=(partner, 4 * z + 2 * jnp.where(which < 3, 0, 1) + core),
            device_id_type=MESH,
        )

    def given_wait(place, part, source):
        pltpu.make_async_remote_copy(
            src_ref=given.at[source, place, part_rows(part)],
            dst_ref=given.at[source, place, part_rows(part)],
            send_sem=give_send.at[PARTS * place + part],
            recv_sem=give_recv.at[PARTS * (LOCAL * source + place) + part],
            device_id=(partner, dp),
            device_id_type=MESH,
        ).wait_recv()

    def keeper_of(which, quarter):
        inside = CHUNK * which + PIECE * quarter
        keeper = lax.div(inside, SHARD)
        return keeper, lax.div(inside - SHARD * keeper, PIECE)

    def final_copy(which, quarter):
        keeper, piece = keeper_of(which, quarter)
        return pltpu.make_async_remote_copy(
            src_ref=stage.at[place_of(PER_Z * z + which), pl.ds(PIECE * quarter, PIECE)],
            dst_ref=final.at[my_y, pl.ds(pl.multiple_of(PIECE * piece, PIECE), PIECE)],
            send_sem=final_send.at[4 * which + quarter],
            recv_sem=final_recv.at[PIECES * my_y + piece],
            device_id=(partner, 4 * z + keeper),
            device_id_type=MESH,
        )

    def relay_final(which, quarter, local):
        _, piece = keeper_of(which, quarter)
        source = given.at[0, place_of(PER_Z * z + which), pl.ds(PIECE * quarter, PIECE)]
        target = final.at[0, pl.ds(pl.multiple_of(PIECE * piece, PIECE), PIECE)]
        if local:
            return pltpu.make_async_copy(source, target, final_recv.at[piece])
        return pltpu.make_async_remote_copy(
            src_ref=source,
            dst_ref=target,
            send_sem=final_send.at[4 * which + quarter],
            recv_sem=final_recv.at[piece],
            device_id=(section, sibling),
            device_id_type=MESH,
        )

    def sum_step(n):
        m = n - PER_Z
        middle = jnp.logical_and(n >= PER_Z, n < 35)
        last = n >= 35
        away = jnp.where(n < PER_Z, 4, jnp.where(middle, 3 - tens(m), 0))
        turn = jnp.where(n < PER_Z, n, jnp.where(middle, half(m - 10 * tens(m)), n - 35))
        falling = jnp.logical_and(middle, low_bit(m) == 1)
        home = round_z(jnp.where(falling, z - away, z + away))
        which = in_order(home, turn, True)
        block = PER_Z * home + which
        odd = more_down(home, which)
        mine = core_of(block) == core
        across = by_y(home, which)
        mine_give = jnp.logical_and(mine, across)
        mine_relay = jnp.logical_and(mine_give, jnp.where(which < 3, 0, 1) == my_y)
        mine_ring = jnp.logical_and(mine, jnp.logical_not(across))
        rises = jnp.where(middle, jnp.logical_not(falling), odd == 0)
        has_low = jnp.logical_or(last, jnp.logical_and(rises, away < 4 - odd))
        has_high = jnp.logical_or(last, jnp.logical_and(jnp.logical_not(rises), away < 3 + odd))
        go_up = jnp.logical_and(rises, jnp.logical_not(last))
        go_down = jnp.logical_and(jnp.logical_not(rises), jnp.logical_not(last))
        return place_of(block), which, mine_ring, mine_give, mine_relay, has_low, has_high, go_up, go_down, last

    def block_gradient(place):
        rows = pl.ds(pl.multiple_of(place * CHUNK, CHUNK), CHUNK)
        side = jnp.where(place >= QKV_BLOCKS, 1, 0)
        for tile in range(4):
            columns = slice(tile * width // 4, (tile + 1) * width // 4)
            value = nn(lhs[0, rows, :], acts[side, 0, :, columns])
            for batch in range(1, 2 * MB):
                value = value + nn(lhs[batch, rows, :], acts[side, batch, :, columns])
            total[:, columns] = value

    def give(n):
        place, which, _, mine_give, _, _, _, _, _, _ = sum_step(n)

        @pl.when(mine_give)
        def _():
            block_gradient(place)
            stage[place] = total[...].astype(BF16)
            for part in range(PARTS):
                give_copy(place, part, which).start()

    def reduce(n):
        place, which, mine_ring, _, mine_relay, has_low, has_high, go_up, go_down, last = sum_step(n)

        def pass_on(part, buffer, keep):
            rows = part_rows(part)
            for going_up, has, landing in ((True, has_low, from_low), (False, has_high, from_high)):

                @pl.when(has)
                def _(going_up=going_up, landing=landing):
                    sum_copy(place, part, going_up, buffer).wait_recv()
                    total[rows, :] += landing[place, rows, :].astype(F32)

            buffer[place, rows, :] = total[rows, :].astype(BF16)
            for going_up, goes in ((True, go_up), (False, go_down)):

                @pl.when(goes)
                def _(going_up=going_up):
                    sum_copy(place, part, going_up, buffer).start()

            @pl.when(last)
            def _():
                for quarter in range(PART // PIECE * part, PART // PIECE * (part + 1)):
                    keep(quarter)

        def keep_ring(quarter):
            final_copy(which, quarter).start()

        def keep_relay(quarter):
            keeper, _ = keeper_of(which, quarter)
            here = low_bit(keeper) == core

            @pl.when(here)
            def _():
                relay_final(which, quarter, True).start()

            @pl.when(jnp.logical_not(here))
            def _():
                relay_final(which, quarter, False).start()

        @pl.when(mine_ring)
        def _():
            block_gradient(place)
            for part in range(PARTS):
                pass_on(part, stage, keep_ring)

        @pl.when(mine_relay)
        def _():
            for part in range(PARTS):
                rows = part_rows(part)
                for source in range(2):
                    given_wait(place, part, source)
                total[rows, :] = given[0, place, rows, :].astype(F32) + given[1, place, rows, :].astype(F32)
                pass_on(part, given.at[0], keep_relay)

    def gather_sent(n):
        place, mine_ring, mine_relay, send_up, send_down = gather_step(n)
        for going_up, goes in ((True, send_up), (False, send_down)):

            @pl.when(jnp.logical_and(mine_ring, goes))
            def _(going_up=going_up):
                gather_copy(place, going_up).wait_send()

            @pl.when(jnp.logical_and(mine_relay, goes))
            def _(going_up=going_up):
                relay_copy(place, going_up).wait_send()

        @pl.when(mine_relay)
        def _():
            for half_y in range(2):
                relay_over(place, half_y).wait_send()

    def drain(n, carry):
        place, which, mine_ring, mine_give, mine_relay, _, _, _, _, last = sum_step(n)

        @pl.when(mine_give)
        def _():
            for part in range(PARTS):
                give_copy(place, part, which).wait_send()

        @pl.when(jnp.logical_and(jnp.logical_or(mine_ring, mine_relay), jnp.logical_not(last)))
        def _():
            for part in range(PARTS):
                sum_copy(place, part, True, stage).wait_send()

        @pl.when(last)
        def _():
            for quarter in range(CHUNK // PIECE):
                keeper, _ = keeper_of(which, quarter)
                away_core = low_bit(keeper) != core

                @pl.when(jnp.logical_or(mine_ring, jnp.logical_and(mine_relay, away_core)))
                def _(quarter=quarter):
                    final_copy(which, quarter).wait_send()

        return carry

    def lead(n, carry):
        give(n)
        gather_sent(n)
        return carry

    def both(n, carry):
        @pl.when(n < 40)
        def _():
            give(n)
            gather_sent(n)

        reduce(n - LEAD)

        @pl.when(n >= LEAD + LAG)
        def _():
            drain(n - LEAD - LAG, 0)

        return carry

    lax.fori_loop(0, LEAD, lead, 0)
    lax.fori_loop(LEAD, 40 + LEAD, both, 0)

    for copy in id_copies + pick_copies + own_copies + pass_copies:
        copy.wait_send()
    for piece in range(PIECES):
        across, _, there = piece_way(piece)

        @pl.when(jnp.logical_not(across))
        def _(piece=piece):
            for half_y in range(2):
                first_copy(piece, half_y).wait_send()

        @pl.when(there)
        def _(piece=piece):
            relay_piece(piece, False).wait_send()

    lax.fori_loop(40 - LAG, 40, drain, 0)

    def final_wait(piece, source):
        rows = pl.ds(PIECE * piece, PIECE)
        pltpu.make_async_remote_copy(
            src_ref=final.at[source, rows],
            dst_ref=final.at[source, rows],
            send_sem=final_send.at[0],
            recv_sem=final_recv.at[PIECES * source + piece],
            device_id=(section, sibling),
            device_id_type=MESH,
        ).wait_recv()

    for piece in range(PIECES):
        rows = pl.ds(PIECE * piece, PIECE)
        across, _, _ = piece_way(piece)
        final_wait(piece, 0)
        grad_ref[rows, :] = final[0, rows, :].astype(F32)

        @pl.when(jnp.logical_not(across))
        def _(piece=piece, rows=rows):
            final_wait(piece, 1)
            grad_ref[rows, :] += final[1, rows, :].astype(F32)


def summed_gradient(params, sent, back, ids):
    width = params.shape[-1]
    frequency = rope_base ** (-np.arange(HEAD_SIZE // 2, dtype=np.float64) * 2.0 / HEAD_SIZE)
    angles = frequency[:, None] * np.arange(SEQ, dtype=np.float64)[None, :]
    cosine = jnp.asarray(np.cos(angles), F32)
    sine = jnp.asarray(np.sin(angles), F32)
    dma = pltpu.SemaphoreType.DMA
    in_vmem = pl.BlockSpec(memory_space=pltpu.VMEM)
    in_smem = pl.BlockSpec(memory_space=pltpu.SMEM)
    anywhere = pl.BlockSpec(memory_space=pl.ANY)
    return pl.pallas_call(
        kernel,
        out_shape=jax.ShapeDtypeStruct((SHARD, width), F32),
        in_specs=[anywhere, anywhere, anywhere, in_smem, in_vmem, in_vmem],
        out_specs=in_vmem,
        scratch_shapes=[
            pltpu.VMEM((SHARD, width), BF16),
            pltpu.VMEM((LOG, SEQ, width), BF16),
            pltpu.VMEM((LOG, SEQ, width), BF16),
            pltpu.VMEM((8, 128), jnp.int32),
            pltpu.VMEM((8, 128), jnp.int32),
            pltpu.VMEM((8, 128), jnp.int32),
            pltpu.SMEM((8, 128), jnp.int32),
            pltpu.SMEM((8, 128), jnp.int32),
            pltpu.VMEM((LOCAL, CHUNK, width), BF16),
            pltpu.VMEM((LOCAL, CHUNK, width), BF16),
            pltpu.VMEM((2, 2 * MB, SEQ, width), BF16),
            pltpu.VMEM((2, MB, SEQ, width), BF16),
            pltpu.VMEM((2 * MB, O_AT, SEQ), F32),
            pltpu.VMEM((2 * MB, Q_ROWS, SEQ), BF16),
            pltpu.VMEM((2 * MB, LOCAL * CHUNK, SEQ), BF16),
            pltpu.VMEM((CHUNK, width), F32),
            pltpu.VMEM((LOCAL, CHUNK, width), BF16),
            pltpu.VMEM((2, LOCAL, CHUNK, width), BF16),
            pltpu.VMEM((LOCAL, CHUNK, width), BF16),
            pltpu.VMEM((LOCAL, CHUNK, width), BF16),
            pltpu.VMEM((2, SHARD, width), BF16),
            dma((3,)),
            dma((2,)),
            dma((2,)),
            dma((2,)),
            dma((2 * PIECES,)),
            dma((LOCAL,)),
            dma((LOCAL,)),
            dma((LOCAL,)),
            dma((LOCAL,)),
            dma((LOCAL,)),
            dma((2 * LOCAL,)),
            dma((LOCAL,)),
            dma((MB,)),
            dma((MB,)),
            dma((MB,)),
            dma((MB,)),
            dma((MB,)),
            dma((MB,)),
            dma((MB,)),
            dma((PARTS * LOCAL,)),
            dma((PARTS * LOCAL,)),
            dma((PARTS * LOCAL,)),
            dma((PARTS * LOCAL,)),
            dma((2 * PARTS * LOCAL,)),
            dma((4 * PER_Z,)),
            dma((2 * PIECES,)),
        ],
        compiler_params=pltpu.CompilerParams(
            collective_id=0, has_side_effects=True, vmem_limit_bytes=60 * 1024 * 1024
        ),
    )(params, sent, back, ids.reshape(1, MB), cosine, sine)


def apply_adam(weights, first_moment, second_moment, gradient):
    first_new = 0.9 * first_moment + 0.1 * gradient
    second_new = 0.999 * second_moment + 0.001 * gradient * gradient
    fix_first = 1.0 - 0.9**STEP
    fix_second = 1.0 - 0.999**STEP
    update = first_new / fix_first / (jnp.sqrt(second_new / fix_second) + 1e-08)
    current = weights.astype(F32)
    renewed = (current - learn_rate * (update + decay_rate * current)).astype(BF16)
    return (renewed, first_new, second_new)


def shards(params, moment_one, moment_two, sent_rows, back_rows, slot_ids):
    summed = summed_gradient(params[0], sent_rows[0, 0], back_rows[0, 0], slot_ids[0, 0])
    renewed, first_new, second_new = apply_adam(params[0], moment_one[0], moment_two[0], summed / N_DP)
    return (renewed[None], first_new[None], second_new[None])


def solution(mesh):
    in_specs = (
        P("section", "dp", None),
        P("section", "dp", None),
        P("section", "dp", None),
        P("section", "dp", None, None, None),
        P("section", "dp", None, None, None),
        P("section", "dp", None),
    )
    out_specs = (P("section", "dp", None), P("section", "dp", None), P("section", "dp", None))
    return jax.shard_map(shards, mesh=mesh, in_specs=in_specs, out_specs=out_specs, check_vma=False)
```

```python
import jax
import jax.numpy as jnp
import numpy as np
from jax import lax
from jax.experimental import pallas as pl
from jax.experimental.pallas import tpu as pltpu
from jax.sharding import PartitionSpec as P

HEAD_SIZE = 64
QUERY_HEADS = 16
KEY_VALUE_HEADS = 4
STEP = 100
SEQ = 192
LOG = 4
MB = 2
PROWS = 2560

N_SECTION = 8
N_DP = 32
N_Z = 8
CHUNK = 64
PER_Z = 5
LOCAL = 20
SHARD = 80
LEAD = 10
LAG = 16
STACK = 4
PARTS = 1
PART = CHUNK // PARTS
PIECE = 16
PIECES = SHARD // PIECE
Q_ROWS = 512
K_AT = 512
V_AT = 640
O_AT = 768
QKV_BLOCKS = 12

rope_base = 500000.0
learn_rate = 0.0003
decay_rate = 0.1

MESH = pl.DeviceIdType.MESH
BF16 = jnp.bfloat16
F32 = jnp.float32


def nn(a, b):
    return lax.dot_general(a, b, (((1,), (0,)), ((), ())), preferred_element_type=F32)


def nt(a, b):
    return lax.dot_general(a, b, (((1,), (1,)), ((), ())), preferred_element_type=F32)


def half(value):
    return lax.shift_right_logical(value, 1)


def low_bit(value):
    return lax.bitwise_and(value, 1)


def round_z(value):
    return lax.bitwise_and(value + N_Z, N_Z - 1)


def core_of(block):
    return jnp.where(
        block < 16,
        jnp.where(block < 8, 0, 1),
        jnp.where(block < 24, low_bit(half(block)), jnp.where(block < 32, 0, 1)),
    )


def place_of(block):
    return jnp.where(
        block < 16,
        lax.bitwise_and(block, 7),
        jnp.where(
            block < 24,
            jnp.where(block < 20, 8, 10) + low_bit(block),
            12 + lax.bitwise_and(block, 7),
        ),
    )


def tens(value):
    return jnp.where(value < 10, 0, jnp.where(value < 20, 1, 2))


def by_y(home, which):
    even = low_bit(home) == 0
    stays = jnp.logical_or(which == 2, which == jnp.where(even, 0, 4))
    return jnp.logical_not(stays)


def in_order(home, turn, ring_first):
    even = low_bit(home) == 0
    turn = jnp.where(ring_first, jnp.where(turn < 2, turn + 3, turn - 2), turn)
    of_even = jnp.where(turn < 2, 2 * turn + 1, jnp.where(turn == 2, 4, 2 * turn - 6))
    of_odd = jnp.where(turn < 2, turn, jnp.where(turn == 2, 3, 2 * turn - 4))
    return jnp.where(even, of_even, of_odd)


def more_down(home, which):
    even = low_bit(home) == 0
    lone = which == jnp.where(even, 1, 3)
    second = jnp.logical_or(which == 4, which == jnp.where(even, 2, 1))
    return jnp.where(lone, low_bit(half(home)), jnp.where(second, 1, 0))


def kernel(
    params_hbm,
    sent_hbm,
    back_hbm,
    ids_ref,
    cos_ref,
    sin_ref,
    grad_ref,
    shard,
    sent,
    back,
    ids_own,
    ids_next,
    ids_prev,
    ids_one,
    ids_two,
    weights,
    relay,
    acts,
    picked,
    proj,
    dctx,
    lhs,
    total,
    stage,
    given,
    from_low,
    from_high,
    final,
    sem_local,
    sem_ids,
    sem_ids_send,
    sem_ids_recv,
    first_send,
    gather_up,
    gather_down,
    gather_recv,
    relay_up,
    relay_down,
    relay_out,
    relay_recv,
    own_local,
    own_send,
    own_recv,
    pick_send,
    pick_recv,
    pass_send,
    pass_recv,
    sum_send,
    low_recv,
    high_recv,
    give_send,
    give_recv,
    final_send,
    final_recv,
):
    section = lax.axis_index("section")
    dp = lax.axis_index("dp")
    z = lax.div(dp, 4)
    core = lax.rem(dp, 2)
    my_y = lax.rem(lax.div(dp, 2), 2)
    odd_section = lax.rem(section, 2)
    partner = section + 1 - 2 * odd_section
    sibling = dp + 1 - 2 * core
    up = lax.rem(dp + 4, N_DP)
    down = lax.rem(dp + N_DP - 4, N_DP)
    before = lax.rem(section + N_SECTION - 1, N_SECTION)
    after = lax.rem(section + 1, N_SECTION)
    before_two = lax.rem(section + N_SECTION - 2, N_SECTION)
    after_two = lax.rem(section + 2, N_SECTION)
    width = weights.shape[2]

    loads = [
        pltpu.make_async_copy(params_hbm, shard, sem_local.at[0]),
        pltpu.make_async_copy(sent_hbm, sent, sem_local.at[1]),
        pltpu.make_async_copy(back_hbm, back, sem_local.at[2]),
    ]
    for load in loads:
        load.start()

    row_of = lax.broadcasted_iota(jnp.int32, (8, 128), 0)
    ids_own[...] = jnp.where(row_of == 0, ids_ref[0, 0], ids_ref[0, 1])

    barrier = pltpu.get_barrier_semaphore()
    beyond = jnp.where(odd_section == 0, before, after)
    peers = [(section, sibling), (section, up), (section, down), (before_two, dp), (after_two, dp), (beyond, dp)]
    for quarter in range(4):
        peers.append((partner, 4 * z + quarter))
    for peer in peers:
        pl.semaphore_signal(barrier, inc=1, device_id=peer, device_id_type=MESH)
    pl.semaphore_wait(barrier, len(peers))

    id_copies = [
        pltpu.make_async_remote_copy(
            src_ref=ids_own,
            dst_ref=ids_next,
            send_sem=sem_ids_send.at[0],
            recv_sem=sem_ids_recv.at[0],
            device_id=(before, dp),
            device_id_type=MESH,
        ),
        pltpu.make_async_remote_copy(
            src_ref=ids_own,
            dst_ref=ids_prev,
            send_sem=sem_ids_send.at[1],
            recv_sem=sem_ids_recv.at[1],
            device_id=(after, dp),
            device_id_type=MESH,
        ),
    ]
    for copy in id_copies:
        copy.start()

    loads[0].wait()

    def first_copy(piece, half):
        row = SHARD * dp + PIECE * piece
        block = lax.div(row, CHUNK)
        return pltpu.make_async_remote_copy(
            src_ref=shard.at[pl.ds(PIECE * piece, PIECE)],
            dst_ref=weights.at[place_of(block), pl.ds(pl.multiple_of(lax.rem(row, CHUNK), PIECE), PIECE)],
            send_sem=first_send.at[2 * piece + half],
            recv_sem=gather_recv.at[place_of(block)],
            device_id=(partner, 4 * z + 2 * half + core_of(block)),
            device_id_type=MESH,
        )

    def relay_piece(piece, local):
        row = SHARD * dp + PIECE * piece
        block = lax.div(row, CHUNK)
        source = shard.at[pl.ds(PIECE * piece, PIECE)]
        target = relay.at[place_of(block), pl.ds(pl.multiple_of(lax.rem(row, CHUNK), PIECE), PIECE)]
        arrived = relay_recv.at[place_of(block)]
        if local:
            return pltpu.make_async_copy(source, target, arrived)
        return pltpu.make_async_remote_copy(
            src_ref=source,
            dst_ref=target,
            send_sem=first_send.at[2 * piece],
            recv_sem=arrived,
            device_id=(section, sibling),
            device_id_type=MESH,
        )

    def piece_way(piece):
        block = lax.div(SHARD * dp + PIECE * piece, CHUNK)
        across = by_y(z, block - PER_Z * z)
        here = core_of(block) == core
        return across, jnp.logical_and(across, here), jnp.logical_and(across, jnp.logical_not(here))

    for piece in range(PIECES):
        across, here, there = piece_way(piece)

        @pl.when(jnp.logical_not(across))
        def _(piece=piece):
            for half in range(2):
                first_copy(piece, half).start()

        @pl.when(here)
        def _(piece=piece):
            relay_piece(piece, True).start()

        @pl.when(there)
        def _(piece=piece):
            relay_piece(piece, False).start()

    def gather_copy(place, going_up):
        return pltpu.make_async_remote_copy(
            src_ref=weights.at[place],
            dst_ref=weights.at[place],
            send_sem=(gather_up if going_up else gather_down).at[place],
            recv_sem=gather_recv.at[place],
            device_id=(section, up if going_up else down),
            device_id_type=MESH,
        )

    def relay_copy(place, going_up):
        return pltpu.make_async_remote_copy(
            src_ref=relay.at[place],
            dst_ref=relay.at[place],
            send_sem=(relay_up if going_up else relay_down).at[place],
            recv_sem=relay_recv.at[place],
            device_id=(section, up if going_up else down),
            device_id_type=MESH,
        )

    def relay_over(place, half):
        return pltpu.make_async_remote_copy(
            src_ref=relay.at[place],
            dst_ref=weights.at[place],
            send_sem=relay_out.at[LOCAL * half + place],
            recv_sem=gather_recv.at[place],
            device_id=(partner, 4 * z + 2 * half + core),
            device_id_type=MESH,
        )

    def gather_step(n):
        m = n - PER_Z
        middle = jnp.logical_and(n >= PER_Z, n < 35)
        away = jnp.where(n < PER_Z, 0, jnp.where(middle, 1 + tens(m), 4))
        turn = jnp.where(n < PER_Z, n, jnp.where(middle, half(m - 10 * tens(m)), n - 35))
        rising = jnp.logical_and(middle, low_bit(m) == 0)
        home = round_z(jnp.where(rising, z - away, z + away))
        which = in_order(home, turn, False)
        block = PER_Z * home + which
        odd = more_down(home, which)
        mine = core_of(block) == core
        across = by_y(home, which)
        mine_relay = jnp.logical_and(jnp.logical_and(mine, across), jnp.where(which < 3, 0, 1) == my_y)
        mine_ring = jnp.logical_and(mine, jnp.logical_not(across))
        start = n < PER_Z
        falling = jnp.logical_and(middle, jnp.logical_not(rising))
        send_up = jnp.logical_or(start, jnp.logical_and(rising, away < 4 - odd))
        send_down = jnp.logical_or(start, jnp.logical_and(falling, away < 3 + odd))
        return place_of(block), mine_ring, mine_relay, send_up, send_down

    def gather(n, carry):
        place, mine_ring, mine_relay, send_up, send_down = gather_step(n)

        @pl.when(mine_ring)
        def _():
            gather_copy(place, True).wait_recv()

            @pl.when(send_up)
            def _():
                gather_copy(place, True).start()

            @pl.when(send_down)
            def _():
                gather_copy(place, False).start()

        @pl.when(mine_relay)
        def _():
            relay_copy(place, True).wait_recv()

            @pl.when(send_up)
            def _():
                relay_copy(place, True).start()

            @pl.when(send_down)
            def _():
                relay_copy(place, False).start()

            for half_y in range(2):
                relay_over(place, half_y).start()

        return carry

    lax.fori_loop(0, 5, gather, 0)

    stays, leaves = odd_section, 1 - odd_section
    target_section = jnp.where(odd_section == 0, before_two, after_two)
    id_copies[0].wait_recv()
    to_one = pltpu.make_async_copy(ids_next, ids_one, sem_ids.at[0])
    to_one.start()
    to_one.wait()
    id_copies[1].wait_recv()
    to_two = pltpu.make_async_copy(ids_prev, ids_two, sem_ids.at[1])
    to_two.start()
    to_two.wait()
    loads[1].wait()
    loads[2].wait()
    own_copies = []
    own_locals = []
    pick_copies = []
    for m in range(MB):
        wanted_one, wanted_two = ids_one[m, 0], ids_two[m, 0]

        def pick_rows(n, carry, m=m, wanted_one=wanted_one, wanted_two=wanted_two):
            rows = pl.ds(pl.multiple_of(n * 16, 16), 16)
            value = sent[wanted_one, rows, :].astype(F32)
            scaling = lax.rsqrt(jnp.mean(value * value, axis=-1, keepdims=True) + 1e-05)
            picked[0, m, rows, :] = (value * scaling).astype(BF16)
            picked[1, m, rows, :] = back[wanted_two, rows, :]
            return carry

        lax.fori_loop(0, SEQ // 16, pick_rows, 0)
        pick_copies.append(
            pltpu.make_async_remote_copy(
                src_ref=picked.at[leaves, m],
                dst_ref=acts.at[leaves, 2 * core + m],
                send_sem=pick_send.at[m],
                recv_sem=pick_recv.at[m],
                device_id=(target_section, dp),
                device_id_type=MESH,
            )
        )
        own_copies.append(
            pltpu.make_async_remote_copy(
                src_ref=picked.at[stays, m],
                dst_ref=acts.at[stays, 2 * core + m],
                send_sem=own_send.at[m],
                recv_sem=own_recv.at[m],
                device_id=(section, sibling),
                device_id_type=MESH,
            )
        )
        own_locals.append(
            pltpu.make_async_copy(picked.at[stays, m], acts.at[stays, 2 * core + m], own_local.at[m])
        )
        pick_copies[m].start()
        own_copies[m].start()
        own_locals[m].start()

    lax.fori_loop(5, 40, gather, 0)

    pass_copies = []
    for m in range(MB):
        pick_copies[m].wait_recv()
        pass_copies.append(
            pltpu.make_async_remote_copy(
                src_ref=acts.at[leaves, 2 * core + m],
                dst_ref=acts.at[leaves, 2 * core + m],
                send_sem=pass_send.at[m],
                recv_sem=pass_recv.at[m],
                device_id=(section, sibling),
                device_id_type=MESH,
            )
        )
        pass_copies[m].start()

    def arrive(block, carry):
        across = by_y(lax.div(block, PER_Z), lax.rem(block, PER_Z))

        @pl.when(jnp.logical_and(across, core_of(block) == core))
        def _():
            gather_copy(place_of(block), True).wait_recv()

        return carry

    lax.fori_loop(0, 40, arrive, 0)

    for m in range(MB):
        own_locals[m].wait()
        own_copies[m].wait_recv()
        pass_copies[m].wait_recv()

    def project(batch, carry):
        rows = weights[:QKV_BLOCKS].reshape(O_AT, width)
        proj[batch] = nt(rows, acts[0, batch])
        return carry

    lax.fori_loop(0, 2 * MB, project, 0)

    def cotangent(batch, carry):
        rows = weights[QKV_BLOCKS:].reshape(Q_ROWS, width)
        dctx[batch] = nt(rows, acts[1, batch]).astype(BF16)
        return carry

    lax.fori_loop(0, 2 * MB, cotangent, 0)

    cosine, sine = cos_ref[...], sin_ref[...]
    middle_row = HEAD_SIZE // 2

    def rotate(value):
        a, b = value[:middle_row], value[middle_row:]
        return jnp.concatenate([a * cosine - b * sine, b * cosine + a * sine], axis=0)

    def rotate_back(value):
        a, b = value[:middle_row], value[middle_row:]
        return jnp.concatenate([a * cosine + b * sine, b * cosine - a * sine], axis=0)

    def attention(n, carry):
        batch, group = lax.div(n, 2), lax.rem(n, 2)
        key_rows = pl.ds(pl.multiple_of(K_AT + HEAD_SIZE * group, HEAD_SIZE), HEAD_SIZE)
        value_rows = pl.ds(pl.multiple_of(V_AT + HEAD_SIZE * group, HEAD_SIZE), HEAD_SIZE)
        key_t = rotate(proj[batch, key_rows, :])
        value_t = proj[batch, value_rows, :]
        key = key_t.T.astype(BF16)
        value = value_t.T.astype(BF16)
        key_t = key_t.astype(BF16)
        value_t = value_t.astype(BF16)
        ones = jnp.ones((16, SEQ), BF16)
        value_ones = jnp.concatenate([value_t, ones], axis=0)
        kept = lax.broadcasted_iota(jnp.int32, (SEQ, SEQ), 0) <= lax.broadcasted_iota(jnp.int32, (SEQ, SEQ), 1)
        kept = jnp.concatenate([kept.astype(jnp.int32)] * STACK, axis=1) > 0
        dkey = jnp.zeros((HEAD_SIZE, SEQ), F32)
        dvalue = jnp.zeros((HEAD_SIZE, SEQ), F32)
        for stack in range(4 // STACK):
            firsts = [256 * group + HEAD_SIZE * (STACK * stack + head) for head in range(STACK)]
            rows = [pl.ds(pl.multiple_of(first, HEAD_SIZE), HEAD_SIZE) for first in firsts]
            query_t = [(rotate(proj[batch, row, :]) * HEAD_SIZE**-0.5) for row in rows]
            query_t = jnp.concatenate(query_t, axis=1).astype(BF16)
            scores = jnp.where(kept, nn(key, query_t), -1e30)
            raised = jnp.exp(scores - jnp.max(scores, axis=0, keepdims=True))
            raised_b = raised.astype(BF16)
            context = nn(value_ones, raised_b)
            inverse = 1.0 / context[HEAD_SIZE : HEAD_SIZE + 1]
            context = context[:HEAD_SIZE] * inverse
            cot = jnp.concatenate([dctx[batch, row, :].astype(F32) for row in rows], axis=1)
            delta = jnp.sum(cot * context, axis=0, keepdims=True) * inverse
            cot = (cot * inverse).astype(BF16)
            dscores = (raised * (nn(value, cot) - delta)).astype(BF16)
            dvalue = dvalue + nt(cot, raised_b)
            dquery = nn(key_t, dscores) * HEAD_SIZE**-0.5
            dkey = dkey + nt(query_t, dscores)
            for head in range(STACK):
                lanes = slice(SEQ * head, SEQ * (head + 1))
                context_rows = pl.ds(pl.multiple_of(O_AT + firsts[head], HEAD_SIZE), HEAD_SIZE)
                lhs[batch, context_rows, :] = context[:, lanes].astype(BF16)
                lhs[batch, rows[head], :] = rotate_back(dquery[:, lanes]).astype(BF16)
        lhs[batch, key_rows, :] = rotate_back(dkey).astype(BF16)
        lhs[batch, value_rows, :] = dvalue.astype(BF16)
        return carry

    lax.fori_loop(0, 8, attention, 0, unroll=2)

    def part_rows(part):
        return pl.ds(PART * part, PART)

    def sum_copy(place, part, going_up, source):
        landing, arrived = (from_low, low_recv) if going_up else (from_high, high_recv)
        return pltpu.make_async_remote_copy(
            src_ref=source.at[place, part_rows(part)],
            dst_ref=landing.at[place, part_rows(part)],
            send_sem=sum_send.at[PARTS * place + part],
            recv_sem=arrived.at[PARTS * place + part],
            device_id=(section, up if going_up else down),
            device_id_type=MESH,
        )

    def give_copy(place, part, which):
        return pltpu.make_async_remote_copy(
            src_ref=stage.at[place, part_rows(part)],
            dst_ref=given.at[my_y, place, part_rows(part)],
            send_sem=give_send.at[PARTS * place + part],
            recv_sem=give_recv.at[PARTS * (LOCAL * my_y + place) + part],
            device_id=(partner, 4 * z + 2 * jnp.where(which < 3, 0, 1) + core),
            device_id_type=MESH,
        )

    def given_wait(place, part, source):
        pltpu.make_async_remote_copy(
            src_ref=given.at[source, place, part_rows(part)],
            dst_ref=given.at[source, place, part_rows(part)],
            send_sem=give_send.at[PARTS * place + part],
            recv_sem=give_recv.at[PARTS * (LOCAL * source + place) + part],
            device_id=(partner, dp),
            device_id_type=MESH,
        ).wait_recv()

    def keeper_of(which, quarter):
        inside = CHUNK * which + PIECE * quarter
        keeper = lax.div(inside, SHARD)
        return keeper, lax.div(inside - SHARD * keeper, PIECE)

    def final_copy(which, quarter):
        keeper, piece = keeper_of(which, quarter)
        return pltpu.make_async_remote_copy(
            src_ref=stage.at[place_of(PER_Z * z + which), pl.ds(PIECE * quarter, PIECE)],
            dst_ref=final.at[my_y, pl.ds(pl.multiple_of(PIECE * piece, PIECE), PIECE)],
            send_sem=final_send.at[4 * which + quarter],
            recv_sem=final_recv.at[PIECES * my_y + piece],
            device_id=(partner, 4 * z + keeper),
            device_id_type=MESH,
        )

    def relay_final(which, quarter, local):
        _, piece = keeper_of(which, quarter)
        source = given.at[0, place_of(PER_Z * z + which), pl.ds(PIECE * quarter, PIECE)]
        target = final.at[0, pl.ds(pl.multiple_of(PIECE * piece, PIECE), PIECE)]
        if local:
            return pltpu.make_async_copy(source, target, final_recv.at[piece])
        return pltpu.make_async_remote_copy(
            src_ref=source,
            dst_ref=target,
            send_sem=final_send.at[4 * which + quarter],
            recv_sem=final_recv.at[piece],
            device_id=(section, sibling),
            device_id_type=MESH,
        )

    def sum_step(n):
        m = n - PER_Z
        middle = jnp.logical_and(n >= PER_Z, n < 35)
        last = n >= 35
        away = jnp.where(n < PER_Z, 4, jnp.where(middle, 3 - tens(m), 0))
        turn = jnp.where(n < PER_Z, n, jnp.where(middle, half(m - 10 * tens(m)), n - 35))
        falling = jnp.logical_and(middle, low_bit(m) == 1)
        home = round_z(jnp.where(falling, z - away, z + away))
        which = in_order(home, turn, True)
        block = PER_Z * home + which
        odd = more_down(home, which)
        mine = core_of(block) == core
        across = by_y(home, which)
        mine_give = jnp.logical_and(mine, across)
        mine_relay = jnp.logical_and(mine_give, jnp.where(which < 3, 0, 1) == my_y)
        mine_ring = jnp.logical_and(mine, jnp.logical_not(across))
        rises = jnp.where(middle, jnp.logical_not(falling), odd == 0)
        has_low = jnp.logical_or(last, jnp.logical_and(rises, away < 4 - odd))
        has_high = jnp.logical_or(last, jnp.logical_and(jnp.logical_not(rises), away < 3 + odd))
        go_up = jnp.logical_and(rises, jnp.logical_not(last))
        go_down = jnp.logical_and(jnp.logical_not(rises), jnp.logical_not(last))
        return place_of(block), which, mine_ring, mine_give, mine_relay, has_low, has_high, go_up, go_down, last

    def block_gradient(place):
        rows = pl.ds(pl.multiple_of(place * CHUNK, CHUNK), CHUNK)
        side = jnp.where(place >= QKV_BLOCKS, 1, 0)
        for tile in range(4):
            columns = slice(tile * width // 4, (tile + 1) * width // 4)
            value = nn(lhs[0, rows, :], acts[side, 0, :, columns])
            for batch in range(1, 2 * MB):
                value = value + nn(lhs[batch, rows, :], acts[side, batch, :, columns])
            total[:, columns] = value

    def give(n):
        place, which, _, mine_give, _, _, _, _, _, _ = sum_step(n)

        @pl.when(mine_give)
        def _():
            block_gradient(place)
            stage[place] = total[...].astype(BF16)
            for part in range(PARTS):
                give_copy(place, part, which).start()

    def reduce(n):
        place, which, mine_ring, _, mine_relay, has_low, has_high, go_up, go_down, last = sum_step(n)

        def pass_on(part, buffer, keep):
            rows = part_rows(part)
            for going_up, has, landing in ((True, has_low, from_low), (False, has_high, from_high)):

                @pl.when(has)
                def _(going_up=going_up, landing=landing):
                    sum_copy(place, part, going_up, buffer).wait_recv()
                    total[rows, :] += landing[place, rows, :].astype(F32)

            buffer[place, rows, :] = total[rows, :].astype(BF16)
            for going_up, goes in ((True, go_up), (False, go_down)):

                @pl.when(goes)
                def _(going_up=going_up):
                    sum_copy(place, part, going_up, buffer).start()

            @pl.when(last)
            def _():
                for quarter in range(PART // PIECE * part, PART // PIECE * (part + 1)):
                    keep(quarter)

        def keep_ring(quarter):
            final_copy(which, quarter).start()

        def keep_relay(quarter):
            keeper, _ = keeper_of(which, quarter)
            here = low_bit(keeper) == core

            @pl.when(here)
            def _():
                relay_final(which, quarter, True).start()

            @pl.when(jnp.logical_not(here))
            def _():
                relay_final(which, quarter, False).start()

        @pl.when(mine_ring)
        def _():
            block_gradient(place)
            for part in range(PARTS):
                pass_on(part, stage, keep_ring)

        @pl.when(mine_relay)
        def _():
            for part in range(PARTS):
                rows = part_rows(part)
                for source in range(2):
                    given_wait(place, part, source)
                total[rows, :] = given[0, place, rows, :].astype(F32) + given[1, place, rows, :].astype(F32)
                pass_on(part, given.at[0], keep_relay)

    def gather_sent(n):
        place, mine_ring, mine_relay, send_up, send_down = gather_step(n)
        for going_up, goes in ((True, send_up), (False, send_down)):

            @pl.when(jnp.logical_and(mine_ring, goes))
            def _(going_up=going_up):
                gather_copy(place, going_up).wait_send()

            @pl.when(jnp.logical_and(mine_relay, goes))
            def _(going_up=going_up):
                relay_copy(place, going_up).wait_send()

        @pl.when(mine_relay)
        def _():
            for half_y in range(2):
                relay_over(place, half_y).wait_send()

    def drain(n, carry):
        place, which, mine_ring, mine_give, mine_relay, _, _, _, _, last = sum_step(n)

        @pl.when(mine_give)
        def _():
            for part in range(PARTS):
                give_copy(place, part, which).wait_send()

        @pl.when(jnp.logical_and(jnp.logical_or(mine_ring, mine_relay), jnp.logical_not(last)))
        def _():
            for part in range(PARTS):
                sum_copy(place, part, True, stage).wait_send()

        @pl.when(last)
        def _():
            for quarter in range(CHUNK // PIECE):
                keeper, _ = keeper_of(which, quarter)
                away_core = low_bit(keeper) != core

                @pl.when(jnp.logical_or(mine_ring, jnp.logical_and(mine_relay, away_core)))
                def _(quarter=quarter):
                    final_copy(which, quarter).wait_send()

        return carry

    def lead(n, carry):
        give(n)
        gather_sent(n)
        return carry

    def both(n, carry):
        @pl.when(n < 40)
        def _():
            give(n)
            gather_sent(n)

        reduce(n - LEAD)

        @pl.when(n >= LEAD + LAG)
        def _():
            drain(n - LEAD - LAG, 0)

        return carry

    lax.fori_loop(0, LEAD, lead, 0)
    lax.fori_loop(LEAD, 40 + LEAD, both, 0)

    for copy in id_copies + pick_copies + own_copies + pass_copies:
        copy.wait_send()
    for piece in range(PIECES):
        across, _, there = piece_way(piece)

        @pl.when(jnp.logical_not(across))
        def _(piece=piece):
            for half_y in range(2):
                first_copy(piece, half_y).wait_send()

        @pl.when(there)
        def _(piece=piece):
            relay_piece(piece, False).wait_send()

    lax.fori_loop(40 - LAG, 40, drain, 0)

    def final_wait(piece, source):
        rows = pl.ds(PIECE * piece, PIECE)
        pltpu.make_async_remote_copy(
            src_ref=final.at[source, rows],
            dst_ref=final.at[source, rows],
            send_sem=final_send.at[0],
            recv_sem=final_recv.at[PIECES * source + piece],
            device_id=(section, sibling),
            device_id_type=MESH,
        ).wait_recv()

    for piece in range(PIECES):
        rows = pl.ds(PIECE * piece, PIECE)
        across, _, _ = piece_way(piece)
        final_wait(piece, 0)
        grad_ref[rows, :] = final[0, rows, :].astype(F32)

        @pl.when(jnp.logical_not(across))
        def _(piece=piece, rows=rows):
            final_wait(piece, 1)
            grad_ref[rows, :] += final[1, rows, :].astype(F32)


def summed_gradient(params, sent, back, ids):
    width = params.shape[-1]
    frequency = rope_base ** (-np.arange(HEAD_SIZE // 2, dtype=np.float64) * 2.0 / HEAD_SIZE)
    angles = frequency[:, None] * np.arange(SEQ, dtype=np.float64)[None, :]
    cosine = jnp.asarray(np.cos(angles), F32)
    sine = jnp.asarray(np.sin(angles), F32)
    dma = pltpu.SemaphoreType.DMA
    in_vmem = pl.BlockSpec(memory_space=pltpu.VMEM)
    in_smem = pl.BlockSpec(memory_space=pltpu.SMEM)
    anywhere = pl.BlockSpec(memory_space=pl.ANY)
    return pl.pallas_call(
        kernel,
        out_shape=jax.ShapeDtypeStruct((SHARD, width), F32),
        in_specs=[anywhere, anywhere, anywhere, in_smem, in_vmem, in_vmem],
        out_specs=in_vmem,
        scratch_shapes=[
            pltpu.VMEM((SHARD, width), BF16),
            pltpu.VMEM((LOG, SEQ, width), BF16),
            pltpu.VMEM((LOG, SEQ, width), BF16),
            pltpu.VMEM((8, 128), jnp.int32),
            pltpu.VMEM((8, 128), jnp.int32),
            pltpu.VMEM((8, 128), jnp.int32),
            pltpu.SMEM((8, 128), jnp.int32),
            pltpu.SMEM((8, 128), jnp.int32),
            pltpu.VMEM((LOCAL, CHUNK, width), BF16),
            pltpu.VMEM((LOCAL, CHUNK, width), BF16),
            pltpu.VMEM((2, 2 * MB, SEQ, width), BF16),
            pltpu.VMEM((2, MB, SEQ, width), BF16),
            pltpu.VMEM((2 * MB, O_AT, SEQ), F32),
            pltpu.VMEM((2 * MB, Q_ROWS, SEQ), BF16),
            pltpu.VMEM((2 * MB, LOCAL * CHUNK, SEQ), BF16),
            pltpu.VMEM((CHUNK, width), F32),
            pltpu.VMEM((LOCAL, CHUNK, width), BF16),
            pltpu.VMEM((2, LOCAL, CHUNK, width), BF16),
            pltpu.VMEM((LOCAL, CHUNK, width), BF16),
            pltpu.VMEM((LOCAL, CHUNK, width), BF16),
            pltpu.VMEM((2, SHARD, width), BF16),
            dma((3,)),
            dma((2,)),
            dma((2,)),
            dma((2,)),
            dma((2 * PIECES,)),
            dma((LOCAL,)),
            dma((LOCAL,)),
            dma((LOCAL,)),
            dma((LOCAL,)),
            dma((LOCAL,)),
            dma((2 * LOCAL,)),
            dma((LOCAL,)),
            dma((MB,)),
            dma((MB,)),
            dma((MB,)),
            dma((MB,)),
            dma((MB,)),
            dma((MB,)),
            dma((MB,)),
            dma((PARTS * LOCAL,)),
            dma((PARTS * LOCAL,)),
            dma((PARTS * LOCAL,)),
            dma((PARTS * LOCAL,)),
            dma((2 * PARTS * LOCAL,)),
            dma((4 * PER_Z,)),
            dma((2 * PIECES,)),
        ],
        compiler_params=pltpu.CompilerParams(
            collective_id=0, has_side_effects=True, vmem_limit_bytes=63 * 1024 * 1024
        ),
    )(params, sent, back, ids.reshape(1, MB), cosine, sine)


def apply_adam(weights, first_moment, second_moment, gradient):
    first_new = 0.9 * first_moment + 0.1 * gradient
    second_new = 0.999 * second_moment + 0.001 * gradient * gradient
    fix_first = 1.0 - 0.9**STEP
    fix_second = 1.0 - 0.999**STEP
    update = first_new / fix_first / (jnp.sqrt(second_new / fix_second) + 1e-08)
    current = weights.astype(F32)
    renewed = (current - learn_rate * (update + decay_rate * current)).astype(BF16)
    return (renewed, first_new, second_new)


def shards(params, moment_one, moment_two, sent_rows, back_rows, slot_ids):
    summed = summed_gradient(params[0], sent_rows[0, 0], back_rows[0, 0], slot_ids[0, 0])
    renewed, first_new, second_new = apply_adam(params[0], moment_one[0], moment_two[0], summed / N_DP)
    return (renewed[None], first_new[None], second_new[None])


def solution(mesh):
    in_specs = (
        P("section", "dp", None),
        P("section", "dp", None),
        P("section", "dp", None),
        P("section", "dp", None, None, None),
        P("section", "dp", None, None, None),
        P("section", "dp", None),
    )
    out_specs = (P("section", "dp", None), P("section", "dp", None), P("section", "dp", None))
    return jax.shard_map(shards, mesh=mesh, in_specs=in_specs, out_specs=out_specs, check_vma=False)
```

```python
import jax
import jax.numpy as jnp
import numpy as np
from jax import lax
from jax.experimental import pallas as pl
from jax.experimental.pallas import tpu as pltpu
from jax.sharding import PartitionSpec as P

HEAD_SIZE = 64
QUERY_HEADS = 16
KEY_VALUE_HEADS = 4
STEP = 100
SEQ = 192
LOG = 4
MB = 2
PROWS = 2560

N_SECTION = 8
N_DP = 32
N_Z = 8
CHUNK = 64
PER_Z = 5
LOCAL = 20
SHARD = 80
LEAD = 10
LAG = 16
STACK = 4
PARTS = 1
PART = CHUNK // PARTS
PIECE = 16
PIECES = SHARD // PIECE
Q_ROWS = 512
K_AT = 512
V_AT = 640
O_AT = 768
QKV_BLOCKS = 12

rope_base = 500000.0
learn_rate = 0.0003
decay_rate = 0.1

MESH = pl.DeviceIdType.MESH
BF16 = jnp.bfloat16
F32 = jnp.float32


def nn(a, b):
    return lax.dot_general(a, b, (((1,), (0,)), ((), ())), preferred_element_type=F32)


def nt(a, b):
    return lax.dot_general(a, b, (((1,), (1,)), ((), ())), preferred_element_type=F32)


def half(value):
    return lax.shift_right_logical(value, 1)


def low_bit(value):
    return lax.bitwise_and(value, 1)


def round_z(value):
    return lax.bitwise_and(value + N_Z, N_Z - 1)


def core_of(block):
    return jnp.where(
        block < 16,
        jnp.where(block < 8, 0, 1),
        jnp.where(block < 24, low_bit(half(block)), jnp.where(block < 32, 0, 1)),
    )


def place_of(block):
    return jnp.where(
        block < 16,
        lax.bitwise_and(block, 7),
        jnp.where(
            block < 24,
            jnp.where(block < 20, 8, 10) + low_bit(block),
            12 + lax.bitwise_and(block, 7),
        ),
    )


def tens(value):
    return jnp.where(value < 10, 0, jnp.where(value < 20, 1, 2))


def by_y(home, which):
    even = low_bit(home) == 0
    stays = jnp.logical_or(which == 2, which == jnp.where(even, 0, 4))
    return jnp.logical_not(stays)


def in_order(home, turn, ring_first):
    even = low_bit(home) == 0
    turn = jnp.where(ring_first, jnp.where(turn < 2, turn + 3, turn - 2), turn)
    of_even = jnp.where(turn < 2, 2 * turn + 1, jnp.where(turn == 2, 4, 2 * turn - 6))
    of_odd = jnp.where(turn < 2, turn, jnp.where(turn == 2, 3, 2 * turn - 4))
    return jnp.where(even, of_even, of_odd)


def more_down(home, which):
    even = low_bit(home) == 0
    lone = which == jnp.where(even, 1, 3)
    second = jnp.logical_or(which == 4, which == jnp.where(even, 2, 1))
    return jnp.where(lone, low_bit(half(home)), jnp.where(second, 1, 0))


def kernel(
    params_hbm,
    sent_hbm,
    back_hbm,
    ids_ref,
    cos_ref,
    sin_ref,
    grad_ref,
    shard,
    sent,
    back,
    ids_own,
    ids_next,
    ids_prev,
    ids_one,
    ids_two,
    weights,
    relay,
    acts,
    picked,
    proj,
    dctx,
    lhs,
    total,
    stage,
    given,
    from_low,
    from_high,
    final,
    sem_local,
    sem_ids,
    sem_ids_send,
    sem_ids_recv,
    first_send,
    gather_up,
    gather_down,
    gather_recv,
    relay_up,
    relay_down,
    relay_out,
    relay_recv,
    own_local,
    own_send,
    own_recv,
    pick_send,
    pick_recv,
    pass_send,
    pass_recv,
    sum_send,
    low_recv,
    high_recv,
    give_send,
    give_recv,
    final_send,
    final_recv,
):
    section = lax.axis_index("section")
    dp = lax.axis_index("dp")
    z = lax.div(dp, 4)
    core = lax.rem(dp, 2)
    my_y = lax.rem(lax.div(dp, 2), 2)
    odd_section = lax.rem(section, 2)
    partner = section + 1 - 2 * odd_section
    sibling = dp + 1 - 2 * core
    up = lax.rem(dp + 4, N_DP)
    down = lax.rem(dp + N_DP - 4, N_DP)
    before = lax.rem(section + N_SECTION - 1, N_SECTION)
    after = lax.rem(section + 1, N_SECTION)
    before_two = lax.rem(section + N_SECTION - 2, N_SECTION)
    after_two = lax.rem(section + 2, N_SECTION)
    width = weights.shape[2]

    loads = [
        pltpu.make_async_copy(params_hbm, shard, sem_local.at[0]),
        pltpu.make_async_copy(sent_hbm, sent, sem_local.at[1]),
        pltpu.make_async_copy(back_hbm, back, sem_local.at[2]),
    ]
    for load in loads:
        load.start()

    row_of = lax.broadcasted_iota(jnp.int32, (8, 128), 0)
    ids_own[...] = jnp.where(row_of == 0, ids_ref[0, 0], ids_ref[0, 1])

    barrier = pltpu.get_barrier_semaphore()
    beyond = jnp.where(odd_section == 0, before, after)
    peers = [(section, sibling), (section, up), (section, down), (before_two, dp), (after_two, dp), (beyond, dp)]
    for quarter in range(4):
        peers.append((partner, 4 * z + quarter))
    for peer in peers:
        pl.semaphore_signal(barrier, inc=1, device_id=peer, device_id_type=MESH)
    pl.semaphore_wait(barrier, len(peers))

    id_copies = [
        pltpu.make_async_remote_copy(
            src_ref=ids_own,
            dst_ref=ids_next,
            send_sem=sem_ids_send.at[0],
            recv_sem=sem_ids_recv.at[0],
            device_id=(before, dp),
            device_id_type=MESH,
        ),
        pltpu.make_async_remote_copy(
            src_ref=ids_own,
            dst_ref=ids_prev,
            send_sem=sem_ids_send.at[1],
            recv_sem=sem_ids_recv.at[1],
            device_id=(after, dp),
            device_id_type=MESH,
        ),
    ]
    for copy in id_copies:
        copy.start()

    loads[0].wait()

    def first_copy(piece, half):
        row = SHARD * dp + PIECE * piece
        block = lax.div(row, CHUNK)
        return pltpu.make_async_remote_copy(
            src_ref=shard.at[pl.ds(PIECE * piece, PIECE)],
            dst_ref=weights.at[place_of(block), pl.ds(pl.multiple_of(lax.rem(row, CHUNK), PIECE), PIECE)],
            send_sem=first_send.at[2 * piece + half],
            recv_sem=gather_recv.at[place_of(block)],
            device_id=(partner, 4 * z + 2 * half + core_of(block)),
            device_id_type=MESH,
        )

    def relay_piece(piece, local):
        row = SHARD * dp + PIECE * piece
        block = lax.div(row, CHUNK)
        source = shard.at[pl.ds(PIECE * piece, PIECE)]
        target = relay.at[place_of(block), pl.ds(pl.multiple_of(lax.rem(row, CHUNK), PIECE), PIECE)]
        arrived = relay_recv.at[place_of(block)]
        if local:
            return pltpu.make_async_copy(source, target, arrived)
        return pltpu.make_async_remote_copy(
            src_ref=source,
            dst_ref=target,
            send_sem=first_send.at[2 * piece],
            recv_sem=arrived,
            device_id=(section, sibling),
            device_id_type=MESH,
        )

    def piece_way(piece):
        block = lax.div(SHARD * dp + PIECE * piece, CHUNK)
        across = by_y(z, block - PER_Z * z)
        here = core_of(block) == core
        return across, jnp.logical_and(across, here), jnp.logical_and(across, jnp.logical_not(here))

    for piece in range(PIECES):
        across, here, there = piece_way(piece)

        @pl.when(jnp.logical_not(across))
        def _(piece=piece):
            for half in range(2):
                first_copy(piece, half).start()

        @pl.when(here)
        def _(piece=piece):
            relay_piece(piece, True).start()

        @pl.when(there)
        def _(piece=piece):
            relay_piece(piece, False).start()

    def gather_copy(place, going_up):
        return pltpu.make_async_remote_copy(
            src_ref=weights.at[place],
            dst_ref=weights.at[place],
            send_sem=(gather_up if going_up else gather_down).at[place],
            recv_sem=gather_recv.at[place],
            device_id=(section, up if going_up else down),
            device_id_type=MESH,
        )

    def relay_copy(place, going_up):
        return pltpu.make_async_remote_copy(
            src_ref=relay.at[place],
            dst_ref=relay.at[place],
            send_sem=(relay_up if going_up else relay_down).at[place],
            recv_sem=relay_recv.at[place],
            device_id=(section, up if going_up else down),
            device_id_type=MESH,
        )

    def relay_over(place, half):
        return pltpu.make_async_remote_copy(
            src_ref=relay.at[place],
            dst_ref=weights.at[place],
            send_sem=relay_out.at[LOCAL * half + place],
            recv_sem=gather_recv.at[place],
            device_id=(partner, 4 * z + 2 * half + core),
            device_id_type=MESH,
        )

    def gather_step(n):
        m = n - PER_Z
        middle = jnp.logical_and(n >= PER_Z, n < 35)
        away = jnp.where(n < PER_Z, 0, jnp.where(middle, 1 + tens(m), 4))
        turn = jnp.where(n < PER_Z, n, jnp.where(middle, half(m - 10 * tens(m)), n - 35))
        rising = jnp.logical_and(middle, low_bit(m) == 0)
        home = round_z(jnp.where(rising, z - away, z + away))
        which = in_order(home, turn, False)
        block = PER_Z * home + which
        odd = more_down(home, which)
        mine = core_of(block) == core
        across = by_y(home, which)
        mine_relay = jnp.logical_and(jnp.logical_and(mine, across), jnp.where(which < 3, 0, 1) == my_y)
        mine_ring = jnp.logical_and(mine, jnp.logical_not(across))
        start = n < PER_Z
        falling = jnp.logical_and(middle, jnp.logical_not(rising))
        send_up = jnp.logical_or(start, jnp.logical_and(rising, away < 4 - odd))
        send_down = jnp.logical_or(start, jnp.logical_and(falling, away < 3 + odd))
        return place_of(block), mine_ring, mine_relay, send_up, send_down

    def gather(n, carry):
        place, mine_ring, mine_relay, send_up, send_down = gather_step(n)

        @pl.when(mine_ring)
        def _():
            gather_copy(place, True).wait_recv()

            @pl.when(send_up)
            def _():
                gather_copy(place, True).start()

            @pl.when(send_down)
            def _():
                gather_copy(place, False).start()

        @pl.when(mine_relay)
        def _():
            relay_copy(place, True).wait_recv()

            @pl.when(send_up)
            def _():
                relay_copy(place, True).start()

            @pl.when(send_down)
            def _():
                relay_copy(place, False).start()

            for half_y in range(2):
                relay_over(place, half_y).start()

        return carry

    lax.fori_loop(0, 5, gather, 0)

    stays, leaves = odd_section, 1 - odd_section
    target_section = jnp.where(odd_section == 0, before_two, after_two)
    id_copies[0].wait_recv()
    to_one = pltpu.make_async_copy(ids_next, ids_one, sem_ids.at[0])
    to_one.start()
    to_one.wait()
    id_copies[1].wait_recv()
    to_two = pltpu.make_async_copy(ids_prev, ids_two, sem_ids.at[1])
    to_two.start()
    to_two.wait()
    loads[1].wait()
    loads[2].wait()
    own_copies = []
    own_locals = []
    pick_copies = []
    for m in range(MB):
        wanted_one, wanted_two = ids_one[m, 0], ids_two[m, 0]

        def pick_rows(n, carry, m=m, wanted_one=wanted_one, wanted_two=wanted_two):
            rows = pl.ds(pl.multiple_of(n * 16, 16), 16)
            value = sent[wanted_one, rows, :].astype(F32)
            scaling = lax.rsqrt(jnp.mean(value * value, axis=-1, keepdims=True) + 1e-05)
            picked[0, m, rows, :] = (value * scaling).astype(BF16)
            picked[1, m, rows, :] = back[wanted_two, rows, :]
            return carry

        lax.fori_loop(0, SEQ // 16, pick_rows, 0)
        pick_copies.append(
            pltpu.make_async_remote_copy(
                src_ref=picked.at[leaves, m],
                dst_ref=acts.at[leaves, 2 * core + m],
                send_sem=pick_send.at[m],
                recv_sem=pick_recv.at[m],
                device_id=(target_section, dp),
                device_id_type=MESH,
            )
        )
        own_copies.append(
            pltpu.make_async_remote_copy(
                src_ref=picked.at[stays, m],
                dst_ref=acts.at[stays, 2 * core + m],
                send_sem=own_send.at[m],
                recv_sem=own_recv.at[m],
                device_id=(section, sibling),
                device_id_type=MESH,
            )
        )
        own_locals.append(
            pltpu.make_async_copy(picked.at[stays, m], acts.at[stays, 2 * core + m], own_local.at[m])
        )
        pick_copies[m].start()
        own_copies[m].start()
        own_locals[m].start()

    lax.fori_loop(5, 40, gather, 0)

    pass_copies = []
    for m in range(MB):
        pick_copies[m].wait_recv()
        pass_copies.append(
            pltpu.make_async_remote_copy(
                src_ref=acts.at[leaves, 2 * core + m],
                dst_ref=acts.at[leaves, 2 * core + m],
                send_sem=pass_send.at[m],
                recv_sem=pass_recv.at[m],
                device_id=(section, sibling),
                device_id_type=MESH,
            )
        )
        pass_copies[m].start()

    def arrive(block, carry):
        across = by_y(lax.div(block, PER_Z), lax.rem(block, PER_Z))

        @pl.when(jnp.logical_and(across, core_of(block) == core))
        def _():
            gather_copy(place_of(block), True).wait_recv()

        return carry

    for m in range(MB):
        own_locals[m].wait()
        own_copies[m].wait_recv()
        pass_copies[m].wait_recv()

    def project(batch, carry):
        rows = weights[:QKV_BLOCKS].reshape(O_AT, width)
        proj[batch] = nt(rows, acts[0, batch])
        return carry

    def cotangent(batch, carry):
        rows = weights[QKV_BLOCKS:].reshape(Q_ROWS, width)
        dctx[batch] = nt(rows, acts[1, batch]).astype(BF16)
        return carry

    def use(turn, carry):
        output_side = low_bit(turn + jnp.where(z >= 4, 1, 0)) == 1

        @pl.when(output_side)
        def _():
            lax.fori_loop(24, 40, arrive, 0)
            lax.fori_loop(0, 2 * MB, cotangent, 0)

        @pl.when(jnp.logical_not(output_side))
        def _():
            lax.fori_loop(0, 24, arrive, 0)
            lax.fori_loop(0, 2 * MB, project, 0)

        return carry

    lax.fori_loop(0, 2, use, 0)

    cosine, sine = cos_ref[...], sin_ref[...]
    middle_row = HEAD_SIZE // 2

    def rotate(value):
        a, b = value[:middle_row], value[middle_row:]
        return jnp.concatenate([a * cosine - b * sine, b * cosine + a * sine], axis=0)

    def rotate_back(value):
        a, b = value[:middle_row], value[middle_row:]
        return jnp.concatenate([a * cosine + b * sine, b * cosine - a * sine], axis=0)

    def attention(n, carry):
        batch, group = lax.div(n, 2), lax.rem(n, 2)
        key_rows = pl.ds(pl.multiple_of(K_AT + HEAD_SIZE * group, HEAD_SIZE), HEAD_SIZE)
        value_rows = pl.ds(pl.multiple_of(V_AT + HEAD_SIZE * group, HEAD_SIZE), HEAD_SIZE)
        key_t = rotate(proj[batch, key_rows, :])
        value_t = proj[batch, value_rows, :]
        key = key_t.T.astype(BF16)
        value = value_t.T.astype(BF16)
        key_t = key_t.astype(BF16)
        value_t = value_t.astype(BF16)
        ones = jnp.ones((16, SEQ), BF16)
        value_ones = jnp.concatenate([value_t, ones], axis=0)
        kept = lax.broadcasted_iota(jnp.int32, (SEQ, SEQ), 0) <= lax.broadcasted_iota(jnp.int32, (SEQ, SEQ), 1)
        kept = jnp.concatenate([kept.astype(jnp.int32)] * STACK, axis=1) > 0
        dkey = jnp.zeros((HEAD_SIZE, SEQ), F32)
        dvalue = jnp.zeros((HEAD_SIZE, SEQ), F32)
        for stack in range(4 // STACK):
            firsts = [256 * group + HEAD_SIZE * (STACK * stack + head) for head in range(STACK)]
            rows = [pl.ds(pl.multiple_of(first, HEAD_SIZE), HEAD_SIZE) for first in firsts]
            query_t = [(rotate(proj[batch, row, :]) * HEAD_SIZE**-0.5) for row in rows]
            query_t = jnp.concatenate(query_t, axis=1).astype(BF16)
            scores = jnp.where(kept, nn(key, query_t), -1e30)
            raised = jnp.exp(scores - jnp.max(scores, axis=0, keepdims=True))
            raised_b = raised.astype(BF16)
            context = nn(value_ones, raised_b)
            inverse = 1.0 / context[HEAD_SIZE : HEAD_SIZE + 1]
            context = context[:HEAD_SIZE] * inverse
            cot = jnp.concatenate([dctx[batch, row, :].astype(F32) for row in rows], axis=1)
            delta = jnp.sum(cot * context, axis=0, keepdims=True) * inverse
            cot = (cot * inverse).astype(BF16)
            dscores = (raised * (nn(value, cot) - delta)).astype(BF16)
            dvalue = dvalue + nt(cot, raised_b)
            dquery = nn(key_t, dscores) * HEAD_SIZE**-0.5
            dkey = dkey + nt(query_t, dscores)
            for head in range(STACK):
                lanes = slice(SEQ * head, SEQ * (head + 1))
                context_rows = pl.ds(pl.multiple_of(O_AT + firsts[head], HEAD_SIZE), HEAD_SIZE)
                lhs[batch, context_rows, :] = context[:, lanes].astype(BF16)
                lhs[batch, rows[head], :] = rotate_back(dquery[:, lanes]).astype(BF16)
        lhs[batch, key_rows, :] = rotate_back(dkey).astype(BF16)
        lhs[batch, value_rows, :] = dvalue.astype(BF16)
        return carry

    lax.fori_loop(0, 8, attention, 0, unroll=2)

    def part_rows(part):
        return pl.ds(PART * part, PART)

    def sum_copy(place, part, going_up, source):
        landing, arrived = (from_low, low_recv) if going_up else (from_high, high_recv)
        return pltpu.make_async_remote_copy(
            src_ref=source.at[place, part_rows(part)],
            dst_ref=landing.at[place, part_rows(part)],
            send_sem=sum_send.at[PARTS * place + part],
            recv_sem=arrived.at[PARTS * place + part],
            device_id=(section, up if going_up else down),
            device_id_type=MESH,
        )

    def give_copy(place, part, which):
        return pltpu.make_async_remote_copy(
            src_ref=stage.at[place, part_rows(part)],
            dst_ref=given.at[my_y, place, part_rows(part)],
            send_sem=give_send.at[PARTS * place + part],
            recv_sem=give_recv.at[PARTS * (LOCAL * my_y + place) + part],
            device_id=(partner, 4 * z + 2 * jnp.where(which < 3, 0, 1) + core),
            device_id_type=MESH,
        )

    def given_wait(place, part, source):
        pltpu.make_async_remote_copy(
            src_ref=given.at[source, place, part_rows(part)],
            dst_ref=given.at[source, place, part_rows(part)],
            send_sem=give_send.at[PARTS * place + part],
            recv_sem=give_recv.at[PARTS * (LOCAL * source + place) + part],
            device_id=(partner, dp),
            device_id_type=MESH,
        ).wait_recv()

    def keeper_of(which, quarter):
        inside = CHUNK * which + PIECE * quarter
        keeper = lax.div(inside, SHARD)
        return keeper, lax.div(inside - SHARD * keeper, PIECE)

    def final_copy(which, quarter):
        keeper, piece = keeper_of(which, quarter)
        return pltpu.make_async_remote_copy(
            src_ref=stage.at[place_of(PER_Z * z + which), pl.ds(PIECE * quarter, PIECE)],
            dst_ref=final.at[my_y, pl.ds(pl.multiple_of(PIECE * piece, PIECE), PIECE)],
            send_sem=final_send.at[4 * which + quarter],
            recv_sem=final_recv.at[PIECES * my_y + piece],
            device_id=(partner, 4 * z + keeper),
            device_id_type=MESH,
        )

    def relay_final(which, quarter, local):
        _, piece = keeper_of(which, quarter)
        source = given.at[0, place_of(PER_Z * z + which), pl.ds(PIECE * quarter, PIECE)]
        target = final.at[0, pl.ds(pl.multiple_of(PIECE * piece, PIECE), PIECE)]
        if local:
            return pltpu.make_async_copy(source, target, final_recv.at[piece])
        return pltpu.make_async_remote_copy(
            src_ref=source,
            dst_ref=target,
            send_sem=final_send.at[4 * which + quarter],
            recv_sem=final_recv.at[piece],
            device_id=(section, sibling),
            device_id_type=MESH,
        )

    def sum_step(n):
        m = n - PER_Z
        middle = jnp.logical_and(n >= PER_Z, n < 35)
        last = n >= 35
        away = jnp.where(n < PER_Z, 4, jnp.where(middle, 3 - tens(m), 0))
        turn = jnp.where(n < PER_Z, n, jnp.where(middle, half(m - 10 * tens(m)), n - 35))
        falling = jnp.logical_and(middle, low_bit(m) == 1)
        home = round_z(jnp.where(falling, z - away, z + away))
        which = in_order(home, turn, True)
        block = PER_Z * home + which
        odd = more_down(home, which)
        mine = core_of(block) == core
        across = by_y(home, which)
        mine_give = jnp.logical_and(mine, across)
        mine_relay = jnp.logical_and(mine_give, jnp.where(which < 3, 0, 1) == my_y)
        mine_ring = jnp.logical_and(mine, jnp.logical_not(across))
        rises = jnp.where(middle, jnp.logical_not(falling), odd == 0)
        has_low = jnp.logical_or(last, jnp.logical_and(rises, away < 4 - odd))
        has_high = jnp.logical_or(last, jnp.logical_and(jnp.logical_not(rises), away < 3 + odd))
        go_up = jnp.logical_and(rises, jnp.logical_not(last))
        go_down = jnp.logical_and(jnp.logical_not(rises), jnp.logical_not(last))
        return place_of(block), which, mine_ring, mine_give, mine_relay, has_low, has_high, go_up, go_down, last

    def block_gradient(place):
        rows = pl.ds(pl.multiple_of(place * CHUNK, CHUNK), CHUNK)
        side = jnp.where(place >= QKV_BLOCKS, 1, 0)
        for tile in range(4):
            columns = slice(tile * width // 4, (tile + 1) * width // 4)
            value = nn(lhs[0, rows, :], acts[side, 0, :, columns])
            for batch in range(1, 2 * MB):
                value = value + nn(lhs[batch, rows, :], acts[side, batch, :, columns])
            total[:, columns] = value

    def give(n):
        place, which, _, mine_give, _, _, _, _, _, _ = sum_step(n)

        @pl.when(mine_give)
        def _():
            block_gradient(place)
            stage[place] = total[...].astype(BF16)
            for part in range(PARTS):
                give_copy(place, part, which).start()

    def reduce(n):
        place, which, mine_ring, _, mine_relay, has_low, has_high, go_up, go_down, last = sum_step(n)

        def pass_on(part, buffer, keep):
            rows = part_rows(part)
            for going_up, has, landing in ((True, has_low, from_low), (False, has_high, from_high)):

                @pl.when(has)
                def _(going_up=going_up, landing=landing):
                    sum_copy(place, part, going_up, buffer).wait_recv()
                    total[rows, :] += landing[place, rows, :].astype(F32)

            buffer[place, rows, :] = total[rows, :].astype(BF16)
            for going_up, goes in ((True, go_up), (False, go_down)):

                @pl.when(goes)
                def _(going_up=going_up):
                    sum_copy(place, part, going_up, buffer).start()

            @pl.when(last)
            def _():
                for quarter in range(PART // PIECE * part, PART // PIECE * (part + 1)):
                    keep(quarter)

        def keep_ring(quarter):
            final_copy(which, quarter).start()

        def keep_relay(quarter):
            keeper, _ = keeper_of(which, quarter)
            here = low_bit(keeper) == core

            @pl.when(here)
            def _():
                relay_final(which, quarter, True).start()

            @pl.when(jnp.logical_not(here))
            def _():
                relay_final(which, quarter, False).start()

        @pl.when(mine_ring)
        def _():
            block_gradient(place)
            for part in range(PARTS):
                pass_on(part, stage, keep_ring)

        @pl.when(mine_relay)
        def _():
            for part in range(PARTS):
                rows = part_rows(part)
                for source in range(2):
                    given_wait(place, part, source)
                total[rows, :] = given[0, place, rows, :].astype(F32) + given[1, place, rows, :].astype(F32)
                pass_on(part, given.at[0], keep_relay)

    def gather_sent(n):
        place, mine_ring, mine_relay, send_up, send_down = gather_step(n)
        for going_up, goes in ((True, send_up), (False, send_down)):

            @pl.when(jnp.logical_and(mine_ring, goes))
            def _(going_up=going_up):
                gather_copy(place, going_up).wait_send()

            @pl.when(jnp.logical_and(mine_relay, goes))
            def _(going_up=going_up):
                relay_copy(place, going_up).wait_send()

        @pl.when(mine_relay)
        def _():
            for half_y in range(2):
                relay_over(place, half_y).wait_send()

    def drain(n, carry):
        place, which, mine_ring, mine_give, mine_relay, _, _, _, _, last = sum_step(n)

        @pl.when(mine_give)
        def _():
            for part in range(PARTS):
                give_copy(place, part, which).wait_send()

        @pl.when(jnp.logical_and(jnp.logical_or(mine_ring, mine_relay), jnp.logical_not(last)))
        def _():
            for part in range(PARTS):
                sum_copy(place, part, True, stage).wait_send()

        @pl.when(last)
        def _():
            for quarter in range(CHUNK // PIECE):
                keeper, _ = keeper_of(which, quarter)
                away_core = low_bit(keeper) != core

                @pl.when(jnp.logical_or(mine_ring, jnp.logical_and(mine_relay, away_core)))
                def _(quarter=quarter):
                    final_copy(which, quarter).wait_send()

        return carry

    def lead(n, carry):
        give(n)
        gather_sent(n)
        return carry

    def both(n, carry):
        @pl.when(n < 40)
        def _():
            give(n)
            gather_sent(n)

        reduce(n - LEAD)

        @pl.when(n >= LEAD + LAG)
        def _():
            drain(n - LEAD - LAG, 0)

        return carry

    lax.fori_loop(0, LEAD, lead, 0)
    lax.fori_loop(LEAD, 40 + LEAD, both, 0)

    for copy in id_copies + pick_copies + own_copies + pass_copies:
        copy.wait_send()
    for piece in range(PIECES):
        across, _, there = piece_way(piece)

        @pl.when(jnp.logical_not(across))
        def _(piece=piece):
            for half_y in range(2):
                first_copy(piece, half_y).wait_send()

        @pl.when(there)
        def _(piece=piece):
            relay_piece(piece, False).wait_send()

    lax.fori_loop(40 - LAG, 40, drain, 0)

    def final_wait(piece, source):
        rows = pl.ds(PIECE * piece, PIECE)
        pltpu.make_async_remote_copy(
            src_ref=final.at[source, rows],
            dst_ref=final.at[source, rows],
            send_sem=final_send.at[0],
            recv_sem=final_recv.at[PIECES * source + piece],
            device_id=(section, sibling),
            device_id_type=MESH,
        ).wait_recv()

    for piece in range(PIECES):
        rows = pl.ds(PIECE * piece, PIECE)
        across, _, _ = piece_way(piece)
        final_wait(piece, 0)
        grad_ref[rows, :] = final[0, rows, :].astype(F32)

        @pl.when(jnp.logical_not(across))
        def _(piece=piece, rows=rows):
            final_wait(piece, 1)
            grad_ref[rows, :] += final[1, rows, :].astype(F32)


def summed_gradient(params, sent, back, ids):
    width = params.shape[-1]
    frequency = rope_base ** (-np.arange(HEAD_SIZE // 2, dtype=np.float64) * 2.0 / HEAD_SIZE)
    angles = frequency[:, None] * np.arange(SEQ, dtype=np.float64)[None, :]
    cosine = jnp.asarray(np.cos(angles), F32)
    sine = jnp.asarray(np.sin(angles), F32)
    dma = pltpu.SemaphoreType.DMA
    in_vmem = pl.BlockSpec(memory_space=pltpu.VMEM)
    in_smem = pl.BlockSpec(memory_space=pltpu.SMEM)
    anywhere = pl.BlockSpec(memory_space=pl.ANY)
    return pl.pallas_call(
        kernel,
        out_shape=jax.ShapeDtypeStruct((SHARD, width), F32),
        in_specs=[anywhere, anywhere, anywhere, in_smem, in_vmem, in_vmem],
        out_specs=in_vmem,
        scratch_shapes=[
            pltpu.VMEM((SHARD, width), BF16),
            pltpu.VMEM((LOG, SEQ, width), BF16),
            pltpu.VMEM((LOG, SEQ, width), BF16),
            pltpu.VMEM((8, 128), jnp.int32),
            pltpu.VMEM((8, 128), jnp.int32),
            pltpu.VMEM((8, 128), jnp.int32),
            pltpu.SMEM((8, 128), jnp.int32),
            pltpu.SMEM((8, 128), jnp.int32),
            pltpu.VMEM((LOCAL, CHUNK, width), BF16),
            pltpu.VMEM((LOCAL, CHUNK, width), BF16),
            pltpu.VMEM((2, 2 * MB, SEQ, width), BF16),
            pltpu.VMEM((2, MB, SEQ, width), BF16),
            pltpu.VMEM((2 * MB, O_AT, SEQ), F32),
            pltpu.VMEM((2 * MB, Q_ROWS, SEQ), BF16),
            pltpu.VMEM((2 * MB, LOCAL * CHUNK, SEQ), BF16),
            pltpu.VMEM((CHUNK, width), F32),
            pltpu.VMEM((LOCAL, CHUNK, width), BF16),
            pltpu.VMEM((2, LOCAL, CHUNK, width), BF16),
            pltpu.VMEM((LOCAL, CHUNK, width), BF16),
            pltpu.VMEM((LOCAL, CHUNK, width), BF16),
            pltpu.VMEM((2, SHARD, width), BF16),
            dma((3,)),
            dma((2,)),
            dma((2,)),
            dma((2,)),
            dma((2 * PIECES,)),
            dma((LOCAL,)),
            dma((LOCAL,)),
            dma((LOCAL,)),
            dma((LOCAL,)),
            dma((LOCAL,)),
            dma((2 * LOCAL,)),
            dma((LOCAL,)),
            dma((MB,)),
            dma((MB,)),
            dma((MB,)),
            dma((MB,)),
            dma((MB,)),
            dma((MB,)),
            dma((MB,)),
            dma((PARTS * LOCAL,)),
            dma((PARTS * LOCAL,)),
            dma((PARTS * LOCAL,)),
            dma((PARTS * LOCAL,)),
            dma((2 * PARTS * LOCAL,)),
            dma((4 * PER_Z,)),
            dma((2 * PIECES,)),
        ],
        compiler_params=pltpu.CompilerParams(
            collective_id=0, has_side_effects=True, vmem_limit_bytes=63 * 1024 * 1024
        ),
    )(params, sent, back, ids.reshape(1, MB), cosine, sine)


def apply_adam(weights, first_moment, second_moment, gradient):
    first_new = 0.9 * first_moment + 0.1 * gradient
    second_new = 0.999 * second_moment + 0.001 * gradient * gradient
    fix_first = 1.0 - 0.9**STEP
    fix_second = 1.0 - 0.999**STEP
    update = first_new / fix_first / (jnp.sqrt(second_new / fix_second) + 1e-08)
    current = weights.astype(F32)
    renewed = (current - learn_rate * (update + decay_rate * current)).astype(BF16)
    return (renewed, first_new, second_new)


def shards(params, moment_one, moment_two, sent_rows, back_rows, slot_ids):
    summed = summed_gradient(params[0], sent_rows[0, 0], back_rows[0, 0], slot_ids[0, 0])
    renewed, first_new, second_new = apply_adam(params[0], moment_one[0], moment_two[0], summed / N_DP)
    return (renewed[None], first_new[None], second_new[None])


def solution(mesh):
    in_specs = (
        P("section", "dp", None),
        P("section", "dp", None),
        P("section", "dp", None),
        P("section", "dp", None, None, None),
        P("section", "dp", None, None, None),
        P("section", "dp", None),
    )
    out_specs = (P("section", "dp", None), P("section", "dp", None), P("section", "dp", None))
    return jax.shard_map(shards, mesh=mesh, in_specs=in_specs, out_specs=out_specs, check_vma=False)
```
